256 devices in a mesh: row: 8 (over z_lo, y), col: 32 (over x, z_hi, core).
Axes of the slice: x: 4, y: 4, z: 8 (z_hi: 4, z_lo: 2; z = z_hi * 2 + z_lo), core: 2. Of those that a mesh axis runs over, the one named last changes fastest.
Arguments:
- pair_map: bfloat16 [512, 512, 128], P('row', 'col'), may hold values from -6 to 6
- res_mask: int32 [512], replicated, may hold values from 0 to 1, as said below
- tri_proj: bfloat16 [128, 512], replicated, may hold values from -0.5 to 0.5
- tri_gate: bfloat16 [128, 128], replicated, may hold values from -0.5 to 0.5
- tri_out: bfloat16 [128, 128], replicated, may hold values from -0.5 to 0.5
- att_qkvg: bfloat16 [128, 512], replicated, may hold values from -8 to 8
- att_bias: bfloat16 [128, 4], replicated, may hold values from -1 to 1
- att_out: bfloat16 [128, 128], replicated, may hold values from -0.5 to 0.5
Outputs:
- result: bfloat16 [512, 512, 128], P('row', 'col')
The draws below stay inside these ranges and needn't reach their ends.
Inputs may be any that keep to these rules, and one draw needn't show every extreme that they name: `res_mask`: the first entry is 1 and the last entry is 0.
All inputs are finite; a program needn't handle non-finite values.
Results may differ from the reference program's by a relative error of at most 0.015.
The reference program's roundings to bfloat16 on the way (of `normed`, `tri_norm`, `normed_two`, `tri_bias`, `weights` and `gated`) count: a program that leaves them out, or rounds other values in their place, can miss the bound.
Values may be sent and summed in bfloat16 or wider, within the bound.
A program may use at most 256 MiB of HBM per device.

```python
import math
import jax
import jax.numpy as jnp
from jax import lax

C = 128
CH = 128
HEADS = 4
HD = 32
HH = 128
N = 512


def draw_res_mask(key, part):
    key = jax.random.fold_in(key, 11)
    levels = jax.random.randint(key, (N,), 0, 4)
    positions = jnp.arange(N)
    live = jnp.where(levels > 0, 1, 0)
    live = jnp.where(positions == 0, 1, live)
    live = jnp.where(positions == N - 1, 0, live)
    return live.astype(jnp.int32)


def draw_att_qkvg(key, part):
    key = jax.random.fold_in(key, 23)
    key_base = jax.random.fold_in(key, 0)
    base_draw = jnp.clip(jax.random.normal(key_base, (C, 4 * HH), jnp.float32), -4.0, 4.0)
    columns = jnp.arange(4 * HH)
    column_scale = jnp.where(columns < 2 * HH, (3.0 / C) ** 0.5, (1.0 / C) ** 0.5)
    weights = base_draw * column_scale[None, :]
    return weights.astype(jnp.bfloat16)


def shard_levels(stream_key, dims, pieces, smallest, top_value):
    factor_of, own = 1.0, jax.random.fold_in(stream_key, 6)
    for axis_at, blocks in pieces:
        draws = jnp.exp(jax.random.uniform(jax.random.fold_in(own, axis_at), (blocks,), jnp.float32, smallest / len(pieces), top_value / len(pieces)))
        factor_of = factor_of * jnp.repeat(draws, dims[axis_at] // blocks).reshape([-1 if axis == axis_at else 1 for axis in range(len(dims))])
    return factor_of


def bell_draw(stream_key, dims, width, bound, cuts=(), dtype=jnp.bfloat16):
    level = shard_levels(stream_key, dims, cuts, -0.22, 0.18) if cuts else 1.0
    values = jax.random.normal(stream_key, dims, jnp.float32) * width * level
    return jnp.minimum(jnp.maximum(values, -bound), bound).astype(dtype)


def setup_inputs(seed: int = 0) -> dict:
    key_list = jax.random.split(jax.random.key(seed), 9)
    pair_map = bell_draw(key_list[0], (N, N, C), 1.0, 6.0, ((0, 8), (1, 32)))
    res_mask = draw_res_mask(jax.random.fold_in(key_list[8], 71), 0)
    tri_proj = bell_draw(key_list[2], (C, 4 * CH), C ** -0.5, 0.5)
    tri_gate = bell_draw(key_list[3], (C, C), C ** -0.5, 0.5)
    tri_out = bell_draw(key_list[4], (CH, C), CH ** -0.5, 0.5)
    att_qkvg = draw_att_qkvg(jax.random.fold_in(key_list[8], 71), 0)
    att_bias = bell_draw(key_list[6], (C, HEADS), 0.18, 1.0)
    att_out = bell_draw(key_list[7], (HH, C), HH ** -0.5, 0.5)
    return {"pair_map": pair_map, "res_mask": res_mask, "tri_proj": tri_proj, "tri_gate": tri_gate, "tri_out": tri_out, "att_qkvg": att_qkvg, "att_bias": att_bias, "att_out": att_out}


EPS = 1e-05

def layer_norm(values):
    centre = values - lax.optimization_barrier(jnp.mean(values, axis=-1, keepdims=True))
    spread = lax.optimization_barrier(jnp.mean(centre * centre, axis=-1, keepdims=True))
    return centre * lax.rsqrt(spread + EPS)

def reference(pair_map, res_mask, tri_proj, tri_gate, tri_out, att_qkvg, att_bias, att_out):
    mask_float = res_mask.astype(jnp.float32)
    pair_mask = mask_float[:, None] * mask_float[None, :]
    normed = layer_norm(pair_map.astype(jnp.float32)).astype(jnp.bfloat16)
    projected = jnp.dot(normed, tri_proj, preferred_element_type=jnp.float32)
    left_side = (jax.nn.sigmoid(projected[..., :CH]) * projected[..., CH:2 * CH] * pair_mask[..., None]).astype(jnp.bfloat16)
    right_side = (jax.nn.sigmoid(projected[..., 2 * CH:3 * CH]) * projected[..., 3 * CH:] * pair_mask[..., None]).astype(jnp.bfloat16)
    tri_sum = jnp.einsum('ikc,jkc->ijc', left_side.astype(jnp.float32), right_side.astype(jnp.float32))
    tri_norm = layer_norm(tri_sum).astype(jnp.bfloat16)
    gating = jax.nn.sigmoid(jnp.dot(normed, tri_gate, preferred_element_type=jnp.float32))
    updated = pair_map.astype(jnp.float32) + gating * jnp.dot(tri_norm, tri_out, preferred_element_type=jnp.float32)
    normed_two = layer_norm(updated).astype(jnp.bfloat16)
    query = jnp.dot(normed_two, att_qkvg[:, :HH], preferred_element_type=jnp.float32).astype(jnp.bfloat16)
    keys_values = jnp.dot(normed_two, att_qkvg[:, HH:3 * HH], preferred_element_type=jnp.float32).astype(jnp.bfloat16)
    att_gating = jax.nn.sigmoid(jnp.dot(normed_two, att_qkvg[:, 3 * HH:], preferred_element_type=jnp.float32))
    tri_bias = jnp.dot(normed_two, att_bias, preferred_element_type=jnp.float32).astype(jnp.bfloat16)
    bias_heads = jnp.transpose(tri_bias.astype(jnp.float32), (2, 0, 1))
    key_live = mask_float > 0

    def attend_row(row_items):
        row_query, row_pairs = row_items
        query_heads = row_query.astype(jnp.float32).reshape(N, HEADS, HD)
        key_heads = row_pairs[:, :HH].astype(jnp.float32).reshape(N, HEADS, HD)
        value_heads = row_pairs[:, HH:].astype(jnp.float32).reshape(N, HEADS, HD)
        scores = jnp.einsum('jhd,khd->hjk', query_heads, key_heads) / math.sqrt(HD) + bias_heads
        scores = jnp.where(key_live[None, None, :], scores, -1000000000.0)
        scores = scores - lax.optimization_barrier(jnp.max(scores, axis=-1, keepdims=True))
        exps = jnp.exp(scores)
        weights = (exps / lax.optimization_barrier(jnp.sum(exps, axis=-1, keepdims=True))).astype(jnp.bfloat16)
        mixed = jnp.einsum('hjk,khd->jhd', weights.astype(jnp.float32), value_heads)
        return mixed.reshape(N, HH)
    attended = lax.map(attend_row, (query, keys_values))
    gated = (att_gating * attended).astype(jnp.bfloat16)
    return (updated + jnp.dot(gated, att_out, preferred_element_type=jnp.float32)).astype(jnp.bfloat16)
```

```python
import math

import jax
import jax.numpy as jnp
from jax import lax
from jax.experimental import pallas as pl
from jax.experimental.pallas import tpu as pltpu
from jax.sharding import PartitionSpec as P

EPS = 1e-05
MESH = pl.DeviceIdType.MESH
F32 = jnp.float32
BF16 = jnp.bfloat16
NT = (((1,), (1,)), ((), ()))


def loop(low, high, body):
    def step(index, carry):
        body(index)
        return carry

    lax.fori_loop(low, high, step, 0)


def norm_over(values, axis):
    centre = values - jnp.mean(values, axis=axis, keepdims=True)
    spread = jnp.mean(centre * centre, axis=axis, keepdims=True)
    return centre * lax.rsqrt(spread + EPS)


def dot(a, b):
    return jnp.dot(a, b, preferred_element_type=F32)


def dot_nt(a, b):
    return lax.dot_general(a, b, NT, preferred_element_type=F32)


def flip(values):
    return values.astype(F32).T.astype(BF16)


def wait_bytes(ref, sem):
    pltpu.make_async_copy(ref, ref, sem).wait()


def kernel(
    pair_ref, mask_smem, mask_ref, proj_ref, gate_ref, tout_ref, qkvg_ref, abias_ref, aout_ref,
    out_ref,
    xf, xn, nk, wpt, ms, sb, pt, gt, gate_t, tout_t, qkvg_t,
    a_buf, rt, s_buf, t_buf, updt, n2s, ns, bscr, bm, up,
    x_buf, bias, kb, vt, qt, gq, gs, h_buf,
    send1, recv1, fsend, frecv, send2, recv2, send3, recv3, bs1, br1, bs2, br2, send4, recv4,
):
    r = lax.axis_index("row")
    c = lax.axis_index("col")
    q = lax.div(c, 2)
    p = lax.rem(c, 2)
    chip = r * 16 + q
    half = lax.div(r, 4)
    rl = lax.rem(r, 4)
    sibling = (r, c + 1 - 2 * p)

    barrier = pltpu.get_barrier_semaphore()

    def greet_same(off):
        d = lax.rem(chip + off, 128)
        pl.semaphore_signal(
            barrier, inc=1, device_id=(lax.div(d, 16), 2 * lax.rem(d, 16) + p), device_id_type=MESH
        )

    def greet_cross(off):
        pl.semaphore_signal(barrier, inc=1, device_id=(r, 2 * off + 1 - p), device_id_type=MESH)

    loop(1, 128, greet_same)
    loop(0, 16, greet_cross)

    lane = lax.broadcasted_iota(jnp.int32, (1, 128), 1)
    low = lane < 64

    def half_lanes(a, b):
        return jnp.where(low, a, b)

    def swap(values):
        return pltpu.roll(values, 64, 1)

    flat = pair_ref[...].astype(F32).reshape(1024, 128)
    xf[...] = flat
    xn[...] = norm_over(flat, 1).astype(BF16).astype(F32)
    wpt[...] = flip(proj_ref[...])
    for k in range(16):
        part = xn[pl.ds(k, 64, stride=16), :].astype(BF16)
        nk[k] = jnp.concatenate([part, part], axis=0)

    two = mask_ref[pl.ds(lax.div(r, 2), 1), :].astype(F32)
    odd = lax.rem(r, 2) == 1
    turned = swap(jnp.broadcast_to(two, (8, 128)))[0:1]
    row_live = half_lanes(jnp.where(odd, turned, two), jnp.where(odd, two, turned))
    col_live = [mask_smem[c * 16 + k].astype(F32) for k in range(16)]

    pl.semaphore_wait(barrier, 143)

    def project(step):
        block = lax.rem(lax.div(r, 2) + step, 4)
        first = pl.multiple_of(block * 32, 32)
        weights = jnp.concatenate([wpt[pl.ds(128 * b + first, 32), :] for b in range(4)], axis=0)
        for k in range(16):
            z = dot_nt(weights, nk[k])
            g = half_lanes(z[0:32], z[64:96])
            v = half_lanes(z[32:64], z[96:128])
            ms[pl.ds(k, 32, stride=16), :] = jax.nn.sigmoid(g) * v * (row_live * col_live[k])
        sb[pl.ds(first, 32)] = ms[...].astype(BF16).reshape(32, 16, 128)

        def send(off):
            ch = first + lax.rem(chip + off, 32)
            pltpu.make_async_remote_copy(
                src_ref=sb.at[ch],
                dst_ref=a_buf.at[p, r, q],
                send_sem=send1,
                recv_sem=recv1.at[r],
                device_id=(lax.div(ch, 16), 2 * lax.rem(ch, 16) + p),
                device_id_type=MESH,
            ).start()

        @pl.when(step == 0)
        def _():
            pltpu.make_async_copy(sb.at[chip], a_buf.at[p, r, q], recv1.at[r]).start()

        loop(jnp.where(step == 0, 1, 0), 32, send)

    loop(0, 4, project)

    gate_t[...] = flip(gate_ref[...])
    tout_t[...] = flip(tout_ref[...])
    qkvg_t[...] = flip(qkvg_ref[...])

    def prepare(s):
        pos = jnp.concatenate(
            [xf[pl.ds(s, 64, stride=16), :], xf[pl.ds(s + 8, 64, stride=16), :]], axis=0
        )
        pt[s] = pos.T
        norm_pos = jnp.concatenate([nk[s, 0:64], nk[s + 8, 0:64]], axis=0)
        gt[s] = jax.nn.sigmoid(dot_nt(gate_t[...], norm_pos))

    loop(0, 8, prepare)

    def forward_copy(row):
        return pltpu.make_async_remote_copy(
            src_ref=a_buf.at[p, row],
            dst_ref=a_buf.at[p, row],
            send_sem=fsend.at[row],
            recv_sem=frecv.at[row],
            device_id=sibling,
            device_id_type=MESH,
        )

    def forward(step):
        row = lax.rem(r + step, 8)
        wait_bytes(a_buf.at[p, row], recv1.at[row])
        forward_copy(row).start()

    loop(0, 8, forward)

    def turn(row):
        wait_bytes(a_buf.at[1 - p, row], frecv.at[row])
        both = a_buf[:, row].reshape(512, 128)
        both_t = flip(both)
        for cc in range(2):
            rt[pl.ds(pl.multiple_of(row * 32 + cc * 16, 16), 16), :] = jnp.where(
                p == 0, both_t[64 + 32 * cc : 80 + 32 * cc], both_t[80 + 32 * cc : 96 + 32 * cc]
            )

    loop(0, 8, turn)

    def triangle(step):
        row = lax.rem(r + step, 8)
        prod = dot(rt[...], a_buf[:, row].reshape(512, 128)).reshape(16, 2, 8, 128)
        hi = swap(prod[:, 1].reshape(128, 128)).reshape(16, 8, 128)
        s_buf[row] = jnp.where(low[None], prod[:, 0], hi)

        def send(off):
            to = lax.rem(q + off, 16)
            pltpu.make_async_remote_copy(
                src_ref=s_buf.at[row, to],
                dst_ref=t_buf.at[pl.ds(pl.multiple_of(chip * 8, 8), 8), :],
                send_sem=send2,
                recv_sem=recv2,
                device_id=(row, 2 * to + p),
                device_id_type=MESH,
            ).start()

        @pl.when(step == 0)
        def _():
            pltpu.make_async_copy(
                s_buf.at[row, q], t_buf.at[pl.ds(pl.multiple_of(chip * 8, 8), 8), :], recv2
            ).start()

        loop(jnp.where(step == 0, 1, 0), 16, send)

    loop(0, 8, triangle)

    wait_bytes(t_buf, recv2)

    def home(s):
        tri = t_buf[pl.ds(s, 128, stride=8), :]
        tri_norm = norm_over(tri, 0).astype(BF16)
        updated = pt[s] + gt[s] * dot(tout_t[...], tri_norm)
        updt[s] = updated
        norm_two = norm_over(updated, 0)
        here = jnp.where(
            low, mask_smem[c * 16 + s].astype(F32), mask_smem[c * 16 + s + 8].astype(F32)
        )
        heads = dot(abias_ref[...], norm_two.astype(BF16))[0:8]
        bscr[pl.ds(s, 8, stride=8), :] = jnp.where(here > 0, heads, -1000000000.0)
        turned = norm_two.T
        n2s[pl.ds(s, 64, stride=16), :] = turned[0:64]
        n2s[pl.ds(s + 8, 64, stride=16), :] = turned[64:128]

    loop(0, 8, home)

    for pair in range(2):
        h0 = bscr[16 * pair : 16 * pair + 8, :]
        h1 = bscr[16 * pair + 8 : 16 * pair + 16, :]
        tile = jnp.concatenate([half_lanes(h0, swap(h1)), half_lanes(swap(h0), h1)], axis=0)
        bm[:, 128 * pair : 128 * pair + 128] = tile.astype(BF16)

    def bias_copy(to):
        return pltpu.make_async_remote_copy(
            src_ref=bm,
            dst_ref=bias.at[rl, c],
            send_sem=bs1,
            recv_sem=br1,
            device_id=(r, 2 * to + half),
            device_id_type=MESH,
        )

    def bias_send(off):
        bias_copy(lax.rem(q + off, 16)).start()

    @pl.when(p == half)
    def _():
        pltpu.make_async_copy(bm, bias.at[rl, c], br1).start()

    @pl.when(p != half)
    def _():
        bias_copy(q).start()

    loop(1, 16, bias_send)

    ns[...] = n2s[...].astype(BF16).reshape(64, 16, 128)
    pltpu.make_async_copy(ns.at[pl.ds(4 * q, 4)], x_buf.at[:, c], recv3).start()

    def rows_send(off):
        to = lax.rem(c + off, 32)
        pltpu.make_async_remote_copy(
            src_ref=ns.at[pl.ds(4 * lax.div(to, 2), 4)],
            dst_ref=x_buf.at[:, c],
            send_sem=send3,
            recv_sem=recv3,
            device_id=(r, to),
            device_id_type=MESH,
        ).start()

    loop(1, 32, rows_send)

    def bias_row_copy(off):
        return pltpu.make_async_remote_copy(
            src_ref=bias.at[rl],
            dst_ref=bias.at[rl],
            send_sem=bs2.at[off - 1],
            recv_sem=br2.at[rl],
            device_id=(lax.rem(r + off, 8), c),
            device_id_type=MESH,
        )

    @pl.when(p == half)
    def _():
        wait_bytes(bias.at[rl], br1)
        loop(1, 8, lambda off: bias_row_copy(off).start())

    def restore(s):
        turned = updt[s].T
        up[pl.ds(s, 64, stride=16), :] = turned[0:64]
        up[pl.ds(s + 8, 64, stride=16), :] = turned[64:128]

    loop(0, 8, restore)

    wait_bytes(x_buf, recv3)

    def qkvg(i):
        rows = x_buf[i].reshape(512, 128)
        mine = x_buf[i, pl.ds(16 * p, 16)].reshape(256, 128)
        kb[i] = dot(rows, qkvg_ref[:, 128:256]).astype(BF16)
        vt[i] = dot_nt(qkvg_t[256:384, :], rows).astype(BF16)
        qt[i] = dot_nt(qkvg_t[0:128, :], mine).astype(BF16).astype(F32)
        gq[i] = jax.nn.sigmoid(dot_nt(qkvg_t[384:512, :], mine))

    loop(0, 4, qkvg)

    head_of_row = lax.broadcasted_iota(jnp.int32, (128, 128), 0) // 32
    head_of_lane = lax.broadcasted_iota(jnp.int32, (128, 128), 1) // 64
    scale = 1.0 / math.sqrt(32.0)

    def attend(t):
        for e in range(2):
            block = 2 * t + e

            @pl.when(jnp.logical_or(p != half, rl != block))
            def _():
                wait_bytes(bias.at[block], br2.at[block])

        def row(i):
            x = qt[i, :, pl.ds(pl.multiple_of(128 * t, 128), 128)]
            xs = swap(x)
            outs = []
            for e in range(2):
                d = half_lanes(x, xs) if e == 0 else half_lanes(xs, x)
                queries = jnp.concatenate(
                    [jnp.where(head_of_row == head_of_lane + 2 * pair, d, 0.0) for pair in range(2)],
                    axis=1,
                ).astype(BF16)
                scores = dot(kb[i], queries) * scale
                scores = scores + bias[2 * t + e].reshape(512, 256).astype(F32)
                exps = jnp.exp(scores - jnp.max(scores, axis=0, keepdims=True))
                weights = exps * (1.0 / jnp.sum(exps, axis=0, keepdims=True))
                outs.append(dot(vt[i], weights.astype(BF16)))
            parts = []
            for h in range(4):
                at = (h // 2) * 128
                first = outs[0][32 * h : 32 * h + 32, at : at + 128]
                second = outs[1][32 * h : 32 * h + 32, at : at + 128]
                if h % 2 == 0:
                    parts.append(half_lanes(first, swap(second)))
                else:
                    parts.append(half_lanes(swap(first), second))
            attended = jnp.concatenate(parts, axis=0)
            gated = gq[i, :, pl.ds(pl.multiple_of(128 * t, 128), 128)] * attended
            gs[i, pl.ds(8 * t, 8)] = gated.T.astype(BF16).reshape(8, 16, 128)

        loop(0, 4, row)

        def send(off):
            cl = 8 * t + off
            to = 16 * p + cl

            @pl.when(to == c)
            def _():
                pltpu.make_async_copy(gs.at[:, cl], h_buf.at[pl.ds(4 * q, 4)], recv4).start()

            @pl.when(to != c)
            def _():
                pltpu.make_async_remote_copy(
                    src_ref=gs.at[:, cl],
                    dst_ref=h_buf.at[pl.ds(4 * q, 4)],
                    send_sem=send4,
                    recv_sem=recv4,
                    device_id=(r, to),
                    device_id_type=MESH,
                ).start()

        loop(0, 8, send)

    loop(0, 2, attend)

    wait_bytes(sb.at[pl.ds(0, 127)], send1)
    loop(0, 8, lambda row: forward_copy(row).wait_send())
    wait_bytes(t_buf.at[pl.ds(0, 127 * 8), :], send2)
    wait_bytes(x_buf.at[:, pl.ds(0, 31)], send3)
    wait_bytes(bias.at[0, pl.ds(0, 15)], bs1)

    @pl.when(p != half)
    def _():
        wait_bytes(bias.at[0, 0], bs1)

    @pl.when(p == half)
    def _():
        loop(1, 8, lambda off: bias_row_copy(off).wait_send())

    wait_bytes(gs.at[:, pl.ds(0, 15)], send4)

    @pl.when(lax.div(c, 16) != p)
    def _():
        wait_bytes(gs.at[:, 0], send4)

    wait_bytes(h_buf, recv4)
    product = dot(h_buf[...].reshape(1024, 128), aout_ref[...])
    out_ref[...] = (up[...] + product).astype(BF16).reshape(64, 16, 128)


def local(pair_map, res_mask, tri_proj, tri_gate, tri_out, att_qkvg, att_bias, att_out):
    bias_rows = jnp.pad(att_bias.T, ((0, 12), (0, 0)))
    vmem = pl.BlockSpec(memory_space=pltpu.VMEM)
    smem = pl.BlockSpec(memory_space=pltpu.SMEM)
    dma = pltpu.SemaphoreType.DMA
    return pl.pallas_call(
        kernel,
        out_shape=jax.ShapeDtypeStruct((64, 16, 128), BF16),
        in_specs=[vmem, smem, vmem, vmem, vmem, vmem, vmem, vmem, vmem],
        out_specs=vmem,
        scratch_shapes=[
            pltpu.VMEM((1024, 128), F32),
            pltpu.VMEM((1024, 128), F32),
            pltpu.VMEM((16, 128, 128), BF16),
            pltpu.VMEM((512, 128), BF16),
            pltpu.VMEM((512, 128), F32),
            pltpu.VMEM((128, 16, 128), BF16),
            pltpu.VMEM((8, 128, 128), F32),
            pltpu.VMEM((8, 128, 128), F32),
            pltpu.VMEM((128, 128), BF16),
            pltpu.VMEM((128, 128), BF16),
            pltpu.VMEM((512, 128), BF16),
            pltpu.VMEM((2, 8, 16, 16, 128), BF16),
            pltpu.VMEM((256, 512), BF16),
            pltpu.VMEM((8, 16, 8, 128), F32),
            pltpu.VMEM((1024, 128), F32),
            pltpu.VMEM((8, 128, 128), F32),
            pltpu.VMEM((1024, 128), F32),
            pltpu.VMEM((64, 16, 128), BF16),
            pltpu.VMEM((64, 128), F32),
            pltpu.VMEM((16, 256), BF16),
            pltpu.VMEM((1024, 128), F32),
            pltpu.VMEM((4, 32, 16, 128), BF16),
            pltpu.VMEM((4, 32, 16, 256), BF16),
            pltpu.VMEM((4, 512, 128), BF16),
            pltpu.VMEM((4, 128, 512), BF16),
            pltpu.VMEM((4, 128, 256), F32),
            pltpu.VMEM((4, 128, 256), F32),
            pltpu.VMEM((4, 16, 16, 128), BF16),
            pltpu.VMEM((64, 16, 128), BF16),
            dma, dma((8,)),
            dma((8,)), dma((8,)),
            dma, dma,
            dma, dma,
            dma, dma,
            dma((7,)), dma((4,)),
            dma, dma,
        ],
        compiler_params=pltpu.CompilerParams(
            collective_id=0, has_side_effects=True, vmem_limit_bytes=40 * 1024 * 1024
        ),
    )(
        pair_map, res_mask, res_mask.reshape(4, 128), tri_proj, tri_gate, tri_out, att_qkvg,
        bias_rows, att_out,
    )


def solution(mesh):
    in_specs = (P("row", "col", None), P(), P(), P(), P(), P(), P(), P())
    out_specs = P("row", "col", None)
    return jax.shard_map(local, mesh=mesh, in_specs=in_specs, out_specs=out_specs, check_vma=False)
```

```python
import math

import jax
import jax.numpy as jnp
from jax import lax
from jax.experimental import pallas as pl
from jax.experimental.pallas import tpu as pltpu
from jax.sharding import PartitionSpec as P

EPS = 1e-05
MESH = pl.DeviceIdType.MESH
F32 = jnp.float32
BF16 = jnp.bfloat16
NT = (((1,), (1,)), ((), ()))
FAR4 = (2, 3, 1, 0)
FAR8 = (4, 5, 7, 3, 6, 2, 1, 0)


def loop(low, high, body, unroll=None):
    def step(index, carry):
        body(index)
        return carry

    lax.fori_loop(low, high, step, 0, unroll=unroll)


def norm_over(values, axis):
    centre = values - jnp.mean(values, axis=axis, keepdims=True)
    spread = jnp.mean(centre * centre, axis=axis, keepdims=True)
    return centre * lax.rsqrt(spread + EPS)


def dot(a, b):
    return jnp.dot(a, b, preferred_element_type=F32)


def dot_nt(a, b):
    return lax.dot_general(a, b, NT, preferred_element_type=F32)


def flip(values):
    return values.astype(F32).T.astype(BF16)


def wait_bytes(ref, sem):
    pltpu.make_async_copy(ref, ref, sem).wait()


def kernel(
    pair_hbm, mask_hbm, mask_rows_hbm, proj_hbm, gate_hbm, tout_hbm, qkvg_hbm, abias_hbm, aout_hbm,
    out_ref,
    pair_ref, mask_smem, mask_ref, proj_ref, gate_ref, tout_ref, qkvg_ref, abias_ref, aout_ref, loads,
    xf, xn, nk, wpt, ms, sb, pt, gt, gate_t, tout_t, qkvg_t,
    a_buf, rt, s_buf, t_buf, tf, updt, n2s, ns, bscr, bm, up,
    x_buf, bias, kb, vt, qt, gq, gs, h_buf,
    send1, recv1, fsend, frecv, send2, recv2, gsend, grecv, send3, recv3, xsend, xrecv,
    bsend, bz, ba, bb, bya, bxb, send4, recv4,
):
    r = lax.axis_index("row")
    c = lax.axis_index("col")
    q = c >> 1
    p = c & 1
    chip = r * 16 + q
    half = r >> 2
    y = r & 3
    x = c >> 3
    zh = q & 3
    sibling = (r, c ^ 1)

    fetches = [
        pltpu.make_async_copy(source, target, loads.at[at])
        for at, (source, target) in enumerate(
            [
                (pair_hbm, pair_ref), (mask_hbm, mask_smem), (mask_rows_hbm, mask_ref),
                (proj_hbm, proj_ref), (gate_hbm, gate_ref), (tout_hbm, tout_ref),
                (qkvg_hbm, qkvg_ref), (abias_hbm, abias_ref), (aout_hbm, aout_ref),
            ]
        )
    ]
    for fetch in fetches:
        fetch.start()

    barrier = pltpu.get_barrier_semaphore()

    def greet(row, col):
        pl.semaphore_signal(barrier, inc=1, device_id=(row, col), device_id_type=MESH)

    for dz in FAR8:
        for dy in FAR4:
            for dx in FAR4:
                if dz or dy or dx:
                    greet(r ^ ((dz & 1) << 2 | dy), c ^ (dx << 3 | (dz >> 1) << 1))
    for dq in range(16):
        greet(r, c ^ (2 * dq + 1))
    for dz in range(4):
        greet(r ^ 4, c ^ (2 * dz + 1))

    lane = lax.broadcasted_iota(jnp.int32, (1, 128), 1)
    low = lane < 64

    def half_lanes(a, b):
        return jnp.where(low, a, b)

    def swap(values):
        return pltpu.roll(values, 64, 1)

    for fetch in fetches:
        fetch.wait()

    flat = pair_ref[...].astype(F32).reshape(1024, 128)
    xf[...] = flat
    xn[...] = norm_over(flat, 1).astype(BF16).astype(F32)
    wpt[...] = flip(proj_ref[...])
    for k in range(16):
        part = xn[pl.ds(k, 64, stride=16), :].astype(BF16)
        nk[k] = jnp.concatenate([part, part], axis=0)

    two = mask_ref[pl.ds(r >> 1, 1), :].astype(F32)
    odd = (r & 1) == 1
    turned = swap(jnp.broadcast_to(two, (8, 128)))[0:1]
    row_live = half_lanes(jnp.where(odd, turned, two), jnp.where(odd, two, turned))
    col_live = [mask_smem[c * 16 + k].astype(F32) for k in range(16)]

    pl.semaphore_wait(barrier, 147)

    def project(step):
        to_y = y ^ 2 ^ step ^ (step >> 1)
        first = pl.multiple_of(to_y * 16, 16)
        weights = jnp.concatenate(
            [wpt[pl.ds(64 * b + first, 16), :] for b in range(8)], axis=0
        )
        for k in range(16):
            z = dot_nt(weights, nk[k])
            g = half_lanes(z[0:32], z[64:96])
            v = half_lanes(z[32:64], z[96:128])
            ms[pl.ds(k, 32, stride=16), :] = jax.nn.sigmoid(g) * v * (row_live * col_live[k])
        for zl in range(2):
            sb[zl, to_y] = ms[256 * zl : 256 * zl + 256, :].astype(BF16).reshape(16, 16, 128)

        def send(dx, dz):
            to_zl = half ^ (dz & 1)
            flips = dx << 2 | dz >> 1
            return pltpu.make_async_remote_copy(
                src_ref=sb.at[to_zl, to_y, q ^ flips],
                dst_ref=a_buf.at[p, r, q],
                send_sem=send1,
                recv_sem=recv1.at[r],
                device_id=(to_zl * 4 + to_y, c ^ (flips << 1)),
                device_id_type=MESH,
            )

        for dx in FAR4:
            for dz in FAR8:
                if dx or dz:
                    send(dx, dz).start()

        @pl.when(step < 3)
        def _():
            send(0, 0).start()

        @pl.when(step == 3)
        def _():
            pltpu.make_async_copy(sb.at[half, y, q], a_buf.at[p, r, q], recv1.at[r]).start()

    loop(0, 4, project)
    sent = [lambda: wait_bytes(sb.at[0], send1), lambda: wait_bytes(sb.at[0, pl.ds(0, 3)], send1)]
    sent.append(lambda: wait_bytes(sb.at[0, 0, pl.ds(0, 15)], send1))

    gate_t[...] = flip(gate_ref[...])
    tout_t[...] = flip(tout_ref[...])
    qkvg_t[...] = flip(qkvg_ref[...])

    def prepare(s):
        pos = jnp.concatenate(
            [xf[pl.ds(s, 64, stride=16), :], xf[pl.ds(s + 8, 64, stride=16), :]], axis=0
        )
        pt[s] = pos.T
        norm_pos = jnp.concatenate([nk[s, 0:64], nk[s + 8, 0:64]], axis=0)
        gt[s] = jax.nn.sigmoid(dot_nt(gate_t[...], norm_pos))

    loop(0, 8, prepare)

    def forward_copy(row):
        return pltpu.make_async_remote_copy(
            src_ref=a_buf.at[p, row],
            dst_ref=a_buf.at[p, row],
            send_sem=fsend.at[row],
            recv_sem=frecv.at[row],
            device_id=sibling,
            device_id_type=MESH,
        )

    def turn(core, row):
        part = flip(a_buf[core, row].reshape(256, 128))
        rt[core, pl.ds(pl.multiple_of(row * 64, 64), 64), :] = part[64:128]

    def arriving(step):
        pair = step >> 1
        return r ^ (2 ^ pair ^ (pair >> 1)) ^ ((step & 1) << 2)

    def forward(step):
        row = arriving(step)
        wait_bytes(a_buf.at[p, row], recv1.at[row])
        forward_copy(row).start()
        turn(p, row)

    loop(0, 8, forward)
    sent.append(lambda: loop(0, 8, lambda row: forward_copy(row).wait_send()))

    def turn_other(step):
        row = arriving(step)
        wait_bytes(a_buf.at[1 - p, row], frecv.at[row])
        turn(1 - p, row)

    loop(0, 8, turn_other)

    def triangle(step):
        to_y = y ^ 2 ^ step ^ (step >> 1)
        row = 4 * p + to_y
        prod = dot(rt[0], a_buf[0, row].reshape(256, 128))
        prod = (prod + dot(rt[1], a_buf[1, row].reshape(256, 128))).reshape(16, 2, 16, 128)
        hi = swap(prod[:, 1].reshape(256, 128)).reshape(16, 16, 128)
        s_buf[to_y] = jnp.where(low[None], prod[:, 0], hi).astype(BF16)

        def send(flips):
            return pltpu.make_async_remote_copy(
                src_ref=s_buf.at[to_y, q ^ flips],
                dst_ref=t_buf.at[chip],
                send_sem=send2,
                recv_sem=recv2.at[r],
                device_id=(row, c ^ (flips << 1)),
                device_id_type=MESH,
            )

        for dx in FAR4:
            for dz in FAR4:
                if dx or dz:
                    send(dx << 2 | dz).start()

        @pl.when(jnp.logical_or(step < 3, p != half))
        def _():
            send(0).start()

        @pl.when(jnp.logical_and(step == 3, p == half))
        def _():
            pltpu.make_async_copy(s_buf.at[to_y, q], t_buf.at[chip], recv2.at[r]).start()

    loop(0, 4, triangle)

    def triangle_sent():
        wait_bytes(s_buf.at[pl.ds(0, 3)], send2)
        wait_bytes(s_buf.at[0, pl.ds(0, 15)], send2)

        @pl.when(p != half)
        def _():
            wait_bytes(s_buf.at[0, 0], send2)

    sent.append(triangle_sent)

    def hand_copy(row):
        block = t_buf.at[pl.ds(pl.multiple_of(row * 16, 16), 16)]
        return pltpu.make_async_remote_copy(
            src_ref=block,
            dst_ref=block,
            send_sem=gsend.at[row],
            recv_sem=grecv.at[row],
            device_id=sibling,
            device_id_type=MESH,
        )

    def widen(row):
        block = t_buf[pl.ds(pl.multiple_of(row * 16, 16), 16)]
        tf[pl.ds(pl.multiple_of(row * 256, 256), 256), :] = block.astype(F32).reshape(256, 128)

    @pl.when(p == half)
    def _():
        def hand(step):
            row = arriving(step)
            wait_bytes(t_buf.at[pl.ds(pl.multiple_of(row * 16, 16), 16)], recv2.at[row])
            hand_copy(row).start()
            widen(row)

        loop(0, 8, hand)

    @pl.when(p != half)
    def _():
        def take(step):
            row = arriving(step)
            wait_bytes(t_buf.at[pl.ds(pl.multiple_of(row * 16, 16), 16)], grecv.at[row])
            widen(row)

        loop(0, 8, take)

    def handed():
        @pl.when(p == half)
        def _():
            loop(0, 8, lambda row: hand_copy(row).wait_send())

    sent.append(handed)

    def home(s):
        one = tf[pl.ds(s, 128, stride=16), :]
        two = tf[pl.ds(s + 8, 128, stride=16), :]
        mixed = swap(half_lanes(two, one))
        tri = half_lanes(jnp.where(p == 0, one, mixed), jnp.where(p == 0, mixed, two))
        tri_norm = norm_over(tri, 0).astype(BF16)
        updated = pt[s] + gt[s] * dot(tout_t[...], tri_norm)
        updt[s] = updated
        norm_two = norm_over(updated, 0)
        here = jnp.where(
            low, mask_smem[c * 16 + s].astype(F32), mask_smem[c * 16 + s + 8].astype(F32)
        )
        heads = dot(abias_ref[...], norm_two.astype(BF16))[0:4]
        bscr[pl.ds(s, 4, stride=8), :] = jnp.where(here > 0, heads, -1000000000.0)
        turned = norm_two.T
        n2s[pl.ds(s, 64, stride=16), :] = turned[0:64]
        n2s[pl.ds(s + 8, 64, stride=16), :] = turned[64:128]

    loop(0, 8, home, unroll=2)

    for pair in range(2):
        h0 = bscr[16 * pair : 16 * pair + 8, :]
        h1 = bscr[16 * pair + 8 : 16 * pair + 16, :]
        tile = jnp.concatenate([half_lanes(h0, swap(h1)), half_lanes(swap(h0), h1)], axis=0)
        bm[:, 128 * pair : 128 * pair + 128] = tile.astype(BF16)

    def bias_copy(src, dst, sem, recv, row, col):
        return pltpu.make_async_remote_copy(
            src_ref=src, dst_ref=dst, send_sem=bsend.at[sem], recv_sem=recv,
            device_id=(row, col), device_id_type=MESH,
        )

    def along_z(dz):
        to = (c ^ ((dz >> 1) << 1)) & 30 | half
        return bias_copy(bm, bias.at[p, y, x, zh], 0, bz, r ^ ((dz & 1) << 2), to)

    for dz in FAR8:
        if dz:
            along_z(dz).start()

    @pl.when(p == half)
    def _():
        pltpu.make_async_copy(bm, bias.at[p, y, x, zh], bz).start()

    @pl.when(p != half)
    def _():
        along_z(0).start()

    def bias_z_sent():
        wait_bytes(bias.at[0, 0, 0], bsend.at[0])
        wait_bytes(bias.at[0, 0, 0, pl.ds(0, 3)], bsend.at[0])

        @pl.when(p != half)
        def _():
            wait_bytes(bias.at[0, 0, 0, 0], bsend.at[0])

    sent.append(bias_z_sent)

    ns[...] = n2s[...].astype(BF16).reshape(64, 16, 128)

    for dx in FAR4:
        for dz in FAR4:
            flips = dx << 2 | dz
            if flips:
                pltpu.make_async_remote_copy(
                    src_ref=ns.at[pl.ds(4 * (q ^ flips), 4)],
                    dst_ref=x_buf.at[:, p, q],
                    send_sem=send3,
                    recv_sem=recv3,
                    device_id=(r, c ^ (flips << 1)),
                    device_id_type=MESH,
                ).start()
    pltpu.make_async_copy(ns.at[pl.ds(4 * q, 4)], x_buf.at[:, p, q], recv3).start()
    sent.append(lambda: wait_bytes(x_buf.at[:, 0, pl.ds(0, 15)], send3))

    wait_bytes(bias.at[:, 0, 0], bz)

    def second_x(dx):
        block = bias.at[0, y, x]
        return bias_copy(block, block, dx, ba, r, c ^ (dx << 3))

    def second_y(dy):
        block = bias.at[1, y, x]
        return bias_copy(block, block, 3 + dy, bb, r ^ dy, c)

    for d in FAR4[:3]:
        second_x(d).start()
        second_y(d).start()

    def third_y(dy):
        block = bias.at[0, y]
        return bias_copy(block, block, 6 + dy, bya, r ^ dy, c)

    def third_x(dx):
        block = bias.at[1, :, x]
        return bias_copy(block, block, 9 + dx, bxb, r, c ^ (dx << 3))

    wait_bytes(bias.at[0, 0, pl.ds(0, 3)], ba)
    for d in FAR4[:3]:
        third_y(d).start()
    wait_bytes(bias.at[1, pl.ds(0, 3), 0], bb)
    for d in FAR4[:3]:
        third_x(d).start()

    def bias_sent():
        for d in FAR4[:3]:
            second_x(d).wait_send()
            second_y(d).wait_send()
            third_y(d).wait_send()
            third_x(d).wait_send()

    sent.append(bias_sent)

    wait_bytes(x_buf.at[:, p], recv3)
    rows_swap = pltpu.make_async_remote_copy(
        src_ref=x_buf.at[:, p], dst_ref=x_buf.at[:, p], send_sem=xsend, recv_sem=xrecv,
        device_id=sibling, device_id_type=MESH,
    )
    rows_swap.start()
    sent.append(lambda: rows_swap.wait_send())

    def keys_values(core):
        def body(i):
            rows = x_buf[i, core].reshape(256, 128)
            kb[i, core] = dot(rows, qkvg_ref[:, 128:256]).astype(BF16)
            vt[i, core] = dot_nt(qkvg_t[256:384, :], rows).astype(BF16)

        loop(0, 4, body)

    keys_values(p)

    def restore(s):
        turned = updt[s].T
        up[pl.ds(s, 64, stride=16), :] = turned[0:64]
        up[pl.ds(s + 8, 64, stride=16), :] = turned[64:128]

    loop(0, 8, restore)

    wait_bytes(x_buf.at[:, p], xrecv)
    keys_values(1 - p)

    def queries_gate(i):
        mine = jnp.concatenate(
            [x_buf[i, core, 8 * p + chips] for chips in range(8) for core in range(2)], axis=0
        )
        qt[i] = dot_nt(qkvg_t[0:128, :], mine).astype(BF16).astype(F32)
        gq[i] = jax.nn.sigmoid(dot_nt(qkvg_t[384:512, :], mine))

    loop(0, 4, queries_gate)

    head_of_row = lax.broadcasted_iota(jnp.int32, (128, 128), 0) // 32
    head_of_lane = lax.broadcasted_iota(jnp.int32, (128, 128), 1) // 64
    scale = 1.0 / math.sqrt(32.0)

    wait_bytes(bias.at[0, pl.ds(0, 3)], bya)
    wait_bytes(bias.at[1, :, pl.ds(0, 3)], bxb)

    def attend(t):
        def row(i):
            x_t = qt[i, :, pl.ds(pl.multiple_of(128 * t, 128), 128)]
            x_s = swap(x_t)
            outs = []
            for e in range(2):
                d = half_lanes(x_t, x_s) if e == 0 else half_lanes(x_s, x_t)
                queries = jnp.concatenate(
                    [jnp.where(head_of_row == head_of_lane + 2 * pair, d, 0.0) for pair in range(2)],
                    axis=1,
                ).astype(BF16)
                scores = dot(kb[i].reshape(512, 128), queries) * scale
                scores = scores + bias[:, 2 * t + e].reshape(512, 256).astype(F32)
                exps = jnp.exp(scores - jnp.max(scores, axis=0, keepdims=True))
                weights = exps * (1.0 / jnp.sum(exps, axis=0, keepdims=True))
                weights = weights.astype(BF16)
                outs.append(dot(vt[i, 0], weights[0:256]) + dot(vt[i, 1], weights[256:512]))
            parts = []
            for h in range(4):
                at = (h // 2) * 128
                first = outs[0][32 * h : 32 * h + 32, at : at + 128]
                second = outs[1][32 * h : 32 * h + 32, at : at + 128]
                if h % 2 == 0:
                    parts.append(half_lanes(first, swap(second)))
                else:
                    parts.append(half_lanes(swap(first), second))
            attended = jnp.concatenate(parts, axis=0)
            gated = gq[i, :, pl.ds(pl.multiple_of(128 * t, 128), 128)] * attended
            gs[i, pl.ds(8 * t, 8)] = gated.T.astype(BF16).reshape(8, 16, 128)

        loop(0, 4, row)

        def send(off):
            cl = 8 * t + off
            to = 16 * p + cl

            @pl.when(to == c)
            def _():
                pltpu.make_async_copy(gs.at[:, cl], h_buf.at[pl.ds(4 * q, 4)], recv4).start()

            @pl.when(to != c)
            def _():
                pltpu.make_async_remote_copy(
                    src_ref=gs.at[:, cl],
                    dst_ref=h_buf.at[pl.ds(4 * q, 4)],
                    send_sem=send4,
                    recv_sem=recv4,
                    device_id=(r, to),
                    device_id_type=MESH,
                ).start()

        loop(0, 8, send)

    loop(0, 2, attend)

    def gated_sent():
        wait_bytes(gs.at[:, pl.ds(0, 15)], send4)

        @pl.when((c >> 4) != p)
        def _():
            wait_bytes(gs.at[:, 0], send4)

    sent.append(gated_sent)

    for wait in sent:
        wait()

    wait_bytes(h_buf, recv4)
    product = dot(h_buf[...].reshape(1024, 128), aout_ref[...])
    out_ref[...] = (up[...] + product).astype(BF16).reshape(64, 16, 128)


def local(pair_map, res_mask, tri_proj, tri_gate, tri_out, att_qkvg, att_bias, att_out):
    dma = pltpu.SemaphoreType.DMA
    return pl.pallas_call(
        kernel,
        out_shape=jax.ShapeDtypeStruct((64, 16, 128), BF16),
        in_specs=[pl.BlockSpec(memory_space=pltpu.HBM)] * 9,
        out_specs=pl.BlockSpec(memory_space=pltpu.VMEM),
        scratch_shapes=[
            pltpu.VMEM((64, 16, 128), BF16),
            pltpu.SMEM((512,), jnp.int32),
            pltpu.VMEM((4, 128), jnp.int32),
            pltpu.VMEM((128, 512), BF16),
            pltpu.VMEM((128, 128), BF16),
            pltpu.VMEM((128, 128), BF16),
            pltpu.VMEM((128, 512), BF16),
            pltpu.VMEM((4, 128), BF16),
            pltpu.VMEM((128, 128), BF16),
            dma((9,)),
            pltpu.VMEM((1024, 128), F32),
            pltpu.VMEM((1024, 128), F32),
            pltpu.VMEM((16, 128, 128), BF16),
            pltpu.VMEM((512, 128), BF16),
            pltpu.VMEM((512, 128), F32),
            pltpu.VMEM((2, 4, 16, 16, 128), BF16),
            pltpu.VMEM((8, 128, 128), F32),
            pltpu.VMEM((8, 128, 128), F32),
            pltpu.VMEM((128, 128), BF16),
            pltpu.VMEM((128, 128), BF16),
            pltpu.VMEM((512, 128), BF16),
            pltpu.VMEM((2, 8, 16, 16, 128), BF16),
            pltpu.VMEM((2, 512, 256), BF16),
            pltpu.VMEM((4, 16, 16, 128), BF16),
            pltpu.VMEM((128, 16, 128), BF16),
            pltpu.VMEM((2048, 128), F32),
            pltpu.VMEM((8, 128, 128), F32),
            pltpu.VMEM((1024, 128), F32),
            pltpu.VMEM((64, 16, 128), BF16),
            pltpu.VMEM((32, 128), F32),
            pltpu.VMEM((16, 256), BF16),
            pltpu.VMEM((1024, 128), F32),
            pltpu.VMEM((4, 2, 16, 16, 128), BF16),
            pltpu.VMEM((2, 4, 4, 4, 16, 256), BF16),
            pltpu.VMEM((4, 2, 256, 128), BF16),
            pltpu.VMEM((4, 2, 128, 256), BF16),
            pltpu.VMEM((4, 128, 256), F32),
            pltpu.VMEM((4, 128, 256), F32),
            pltpu.VMEM((4, 16, 16, 128), BF16),
            pltpu.VMEM((64, 16, 128), BF16),
            dma, dma((8,)),
            dma((8,)), dma((8,)),
            dma, dma((8,)),
            dma((8,)), dma((8,)),
            dma, dma,
            dma, dma,
            dma((13,)),
            dma, dma, dma, dma, dma,
            dma, dma,
        ],
        compiler_params=pltpu.CompilerParams(
            collective_id=0, has_side_effects=True, vmem_limit_bytes=60 * 1024 * 1024
        ),
    )(
        pair_map, res_mask, res_mask.reshape(4, 128), tri_proj, tri_gate, tri_out, att_qkvg,
        att_bias.T, att_out,
    )


def solution(mesh):
    in_specs = (P("row", "col", None), P(), P(), P(), P(), P(), P(), P())
    out_specs = P("row", "col", None)
    return jax.shard_map(local, mesh=mesh, in_specs=in_specs, out_specs=out_specs, check_vma=False)
```

```python
import math

import jax
import jax.numpy as jnp
from jax import lax
from jax.experimental import pallas as pl
from jax.experimental.pallas import tpu as pltpu
from jax.sharding import PartitionSpec as P

EPS = 1e-05
MESH = pl.DeviceIdType.MESH
F32 = jnp.float32
BF16 = jnp.bfloat16
NT = (((1,), (1,)), ((), ()))
FAR4 = (2, 3, 1, 0)
FAR8 = (4, 5, 7, 3, 6, 2, 1, 0)


def loop(low, high, body, unroll=None):
    def step(index, carry):
        body(index)
        return carry

    lax.fori_loop(low, high, step, 0, unroll=unroll)


def norm_over(values, axis):
    centre = values - jnp.mean(values, axis=axis, keepdims=True)
    spread = jnp.mean(centre * centre, axis=axis, keepdims=True)
    return centre * lax.rsqrt(spread + EPS)


def dot(a, b):
    return jnp.dot(a, b, preferred_element_type=F32)


def dot_nt(a, b):
    return lax.dot_general(a, b, NT, preferred_element_type=F32)


def flip(values):
    return values.astype(F32).T.astype(BF16)


def wait_bytes(ref, sem):
    pltpu.make_async_copy(ref, ref, sem).wait()


def kernel(
    pair_hbm, mask_hbm, mask_rows_hbm, proj_hbm, gate_hbm, tout_hbm, qkvg_hbm, abias_hbm, aout_hbm,
    out_ref,
    pair_ref, mask_smem, mask_ref, proj_ref, gate_ref, tout_ref, qkvg_ref, abias_ref, aout_ref, loads,
    xf, xn, nk, wpt, ms, sb, pt, gt, gate_t, tout_t, qkvg_t,
    a_buf, rt, s_buf, t_buf, tf, updt, n2t, n2s, ns, bscr, bm, up,
    x_buf, bias, kb, vt, qb, gq, bf, sc, wb, oscr, gs, h_buf,
    send1, recv1, fsend, frecv, send2, recv2, gsend, grecv, send3, recv3, xsend, xrecv,
    bsend, bz, bu, send4, recv4,
):
    r = lax.axis_index("row")
    c = lax.axis_index("col")
    q = c >> 1
    p = c & 1
    chip = r * 16 + q
    half = r >> 2
    y = r & 3
    x = c >> 3
    zh = q & 3
    sibling = (r, c ^ 1)

    fetches = [
        pltpu.make_async_copy(source, target, loads.at[at])
        for at, (source, target) in enumerate(
            [
                (pair_hbm, pair_ref), (mask_hbm, mask_smem), (mask_rows_hbm, mask_ref),
                (proj_hbm, proj_ref), (gate_hbm, gate_ref), (tout_hbm, tout_ref),
                (qkvg_hbm, qkvg_ref), (abias_hbm, abias_ref), (aout_hbm, aout_ref),
            ]
        )
    ]
    for fetch in fetches:
        fetch.start()

    barrier = pltpu.get_barrier_semaphore()

    def greet(row, col):
        pl.semaphore_signal(barrier, inc=1, device_id=(row, col), device_id_type=MESH)

    for dz in FAR8:
        for dy in FAR4:
            for dx in FAR4:
                if dz or dy or dx:
                    greet(r ^ ((dz & 1) << 2 | dy), c ^ (dx << 3 | (dz >> 1) << 1))
    for dq in range(16):
        greet(r, c ^ (2 * dq + 1))
    for dz in range(4):
        greet(r ^ 4, c ^ (2 * dz + 1))

    lane = lax.broadcasted_iota(jnp.int32, (1, 128), 1)
    low = lane < 64

    def half_lanes(a, b):
        return jnp.where(low, a, b)

    def swap(values):
        return pltpu.roll(values, 64, 1)

    for fetch in fetches:
        fetch.wait()

    flat = pair_ref[...].astype(F32).reshape(1024, 128)
    xf[...] = flat
    xn[...] = norm_over(flat, 1).astype(BF16).astype(F32)
    wpt[...] = flip(proj_ref[...])
    for k in range(16):
        part = xn[pl.ds(k, 64, stride=16), :].astype(BF16)
        nk[k] = jnp.concatenate([part, part], axis=0)

    two = mask_ref[pl.ds(r >> 1, 1), :].astype(F32)
    odd = (r & 1) == 1
    turned = swap(jnp.broadcast_to(two, (8, 128)))[0:1]
    row_live = half_lanes(jnp.where(odd, turned, two), jnp.where(odd, two, turned))
    col_live = [mask_smem[c * 16 + k].astype(F32) for k in range(16)]

    pl.semaphore_wait(barrier, 147)

    def project(step):
        to_y = y ^ 2 ^ step ^ (step >> 1)
        first = pl.multiple_of(to_y * 16, 16)
        weights = jnp.concatenate(
            [wpt[pl.ds(64 * b + first, 16), :] for b in range(8)], axis=0
        )
        for k in range(16):
            z = dot_nt(weights, nk[k])
            g = half_lanes(z[0:32], z[64:96])
            v = half_lanes(z[32:64], z[96:128])
            ms[pl.ds(k, 32, stride=16), :] = jax.nn.sigmoid(g) * v * (row_live * col_live[k])
        for zl in range(2):
            sb[zl, to_y] = ms[256 * zl : 256 * zl + 256, :].astype(BF16).reshape(16, 16, 128)

        def send(dx, dz):
            to_zl = half ^ (dz & 1)
            flips = dx << 2 | dz >> 1
            return pltpu.make_async_remote_copy(
                src_ref=sb.at[to_zl, to_y, q ^ flips],
                dst_ref=a_buf.at[p, r, q],
                send_sem=send1,
                recv_sem=recv1.at[r],
                device_id=(to_zl * 4 + to_y, c ^ (flips << 1)),
                device_id_type=MESH,
            )

        for dx in FAR4:
            for dz in FAR8:
                if dx or dz:
                    send(dx, dz).start()

        @pl.when(step < 3)
        def _():
            send(0, 0).start()

        @pl.when(step == 3)
        def _():
            pltpu.make_async_copy(sb.at[half, y, q], a_buf.at[p, r, q], recv1.at[r]).start()

    loop(0, 4, project)
    sent = [lambda: wait_bytes(sb.at[0], send1), lambda: wait_bytes(sb.at[0, pl.ds(0, 3)], send1)]
    sent.append(lambda: wait_bytes(sb.at[0, 0, pl.ds(0, 15)], send1))

    gate_t[...] = flip(gate_ref[...])
    tout_t[...] = flip(tout_ref[...])
    qkvg_t[...] = flip(qkvg_ref[...])

    def prepare(s):
        pos = jnp.concatenate(
            [xf[pl.ds(s, 64, stride=16), :], xf[pl.ds(s + 8, 64, stride=16), :]], axis=0
        )
        pt[s] = pos.T
        norm_pos = jnp.concatenate([nk[s, 0:64], nk[s + 8, 0:64]], axis=0)
        gt[s] = jax.nn.sigmoid(dot_nt(gate_t[...], norm_pos))

    loop(0, 8, prepare)

    def forward_copy(row):
        return pltpu.make_async_remote_copy(
            src_ref=a_buf.at[p, row],
            dst_ref=a_buf.at[p, row],
            send_sem=fsend.at[row],
            recv_sem=frecv.at[row],
            device_id=sibling,
            device_id_type=MESH,
        )

    def turn(core, row):
        part = flip(a_buf[core, row].reshape(256, 128))
        rt[core, pl.ds(pl.multiple_of(row * 64, 64), 64), :] = part[64:128]

    def arriving(step):
        pair = step >> 1
        return r ^ (2 ^ pair ^ (pair >> 1)) ^ ((step & 1) << 2)

    def forward(step):
        row = arriving(step)
        wait_bytes(a_buf.at[p, row], recv1.at[row])
        forward_copy(row).start()
        turn(p, row)

    loop(0, 8, forward)
    sent.append(lambda: loop(0, 8, lambda row: forward_copy(row).wait_send()))

    def turn_other(step):
        row = arriving(step)
        wait_bytes(a_buf.at[1 - p, row], frecv.at[row])
        turn(1 - p, row)

    loop(0, 8, turn_other)

    def triangle(step):
        to_y = y ^ 2 ^ step ^ (step >> 1)
        row = 4 * p + to_y
        prod = dot(rt[0], a_buf[0, row].reshape(256, 128))
        prod = (prod + dot(rt[1], a_buf[1, row].reshape(256, 128))).reshape(16, 2, 16, 128)
        hi = swap(prod[:, 1].reshape(256, 128)).reshape(16, 16, 128)
        s_buf[to_y] = jnp.where(low[None], prod[:, 0], hi).astype(BF16)

        def send(flips):
            return pltpu.make_async_remote_copy(
                src_ref=s_buf.at[to_y, q ^ flips],
                dst_ref=t_buf.at[chip],
                send_sem=send2,
                recv_sem=recv2.at[r],
                device_id=(row, c ^ (flips << 1)),
                device_id_type=MESH,
            )

        for dx in FAR4:
            for dz in FAR4:
                if dx or dz:
                    send(dx << 2 | dz).start()

        @pl.when(jnp.logical_or(step < 3, p != half))
        def _():
            send(0).start()

        @pl.when(jnp.logical_and(step == 3, p == half))
        def _():
            pltpu.make_async_copy(s_buf.at[to_y, q], t_buf.at[chip], recv2.at[r]).start()

    loop(0, 4, triangle)

    def triangle_sent():
        wait_bytes(s_buf.at[pl.ds(0, 3)], send2)
        wait_bytes(s_buf.at[0, pl.ds(0, 15)], send2)

        @pl.when(p != half)
        def _():
            wait_bytes(s_buf.at[0, 0], send2)

    sent.append(triangle_sent)

    def hand_copy(row):
        block = t_buf.at[pl.ds(pl.multiple_of(row * 16, 16), 16)]
        return pltpu.make_async_remote_copy(
            src_ref=block,
            dst_ref=block,
            send_sem=gsend.at[row],
            recv_sem=grecv.at[row],
            device_id=sibling,
            device_id_type=MESH,
        )

    def widen(row):
        block = t_buf[pl.ds(pl.multiple_of(row * 16, 16), 16)]
        tf[pl.ds(pl.multiple_of(row * 256, 256), 256), :] = block.astype(F32).reshape(256, 128)

    @pl.when(p == half)
    def _():
        def hand(step):
            row = arriving(step)
            wait_bytes(t_buf.at[pl.ds(pl.multiple_of(row * 16, 16), 16)], recv2.at[row])
            hand_copy(row).start()
            widen(row)

        loop(0, 8, hand)

    @pl.when(p != half)
    def _():
        def take(step):
            row = arriving(step)
            wait_bytes(t_buf.at[pl.ds(pl.multiple_of(row * 16, 16), 16)], grecv.at[row])
            widen(row)

        loop(0, 8, take)

    def handed():
        @pl.when(p == half)
        def _():
            loop(0, 8, lambda row: hand_copy(row).wait_send())

    sent.append(handed)

    def home(s):
        one = tf[pl.ds(s, 128, stride=16), :]
        two = tf[pl.ds(s + 8, 128, stride=16), :]
        mixed = swap(half_lanes(two, one))
        tri = half_lanes(jnp.where(p == 0, one, mixed), jnp.where(p == 0, mixed, two))
        tri_norm = norm_over(tri, 0).astype(BF16)
        updated = pt[s] + gt[s] * dot(tout_t[...], tri_norm)
        updt[s] = updated
        norm_two = norm_over(updated, 0)
        here = jnp.where(
            low, mask_smem[c * 16 + s].astype(F32), mask_smem[c * 16 + s + 8].astype(F32)
        )
        heads = dot(abias_ref[...], norm_two.astype(BF16))[0:4]
        bscr[pl.ds(s, 4, stride=8), :] = jnp.where(here > 0, heads, -1000000000.0)
        n2t[s] = norm_two

    loop(0, 8, home, unroll=2)

    for pair in range(2):
        h0 = bscr[16 * pair : 16 * pair + 8, :]
        h1 = bscr[16 * pair + 8 : 16 * pair + 16, :]
        tile = jnp.concatenate([half_lanes(h0, swap(h1)), half_lanes(swap(h0), h1)], axis=0)
        bm[:, 128 * pair : 128 * pair + 128] = tile.astype(BF16)

    def bias_copy(src, dst, sem, recv, row, col):
        return pltpu.make_async_remote_copy(
            src_ref=src, dst_ref=dst, send_sem=bsend.at[sem], recv_sem=recv,
            device_id=(row, col), device_id_type=MESH,
        )

    def along_z(dz):
        to = (c ^ ((dz >> 1) << 1)) & 30 | half
        return bias_copy(bm, bias.at[p, y, x, zh], 0, bz, r ^ ((dz & 1) << 2), to)

    for dz in FAR8:
        if dz:
            along_z(dz).start()

    @pl.when(p == half)
    def _():
        pltpu.make_async_copy(bm, bias.at[p, y, x, zh], bz).start()

    @pl.when(p != half)
    def _():
        along_z(0).start()

    def bias_z_sent():
        wait_bytes(bias.at[0, 0, 0], bsend.at[0])
        wait_bytes(bias.at[0, 0, 0, pl.ds(0, 3)], bsend.at[0])

        @pl.when(p != half)
        def _():
            wait_bytes(bias.at[0, 0, 0, 0], bsend.at[0])

    sent.append(bias_z_sent)

    def rows_of(source, target):
        def body(s):
            turned = source[s].T
            target[pl.ds(s, 64, stride=16), :] = turned[0:64]
            target[pl.ds(s + 8, 64, stride=16), :] = turned[64:128]

        loop(0, 8, body, unroll=2)

    rows_of(n2t, n2s)
    ns[...] = n2s[...].astype(BF16).reshape(64, 16, 128)

    for dx in FAR4:
        for dz in FAR4:
            flips = dx << 2 | dz
            if flips:
                pltpu.make_async_remote_copy(
                    src_ref=ns.at[pl.ds(4 * (q ^ flips), 4)],
                    dst_ref=x_buf.at[:, p, q],
                    send_sem=send3,
                    recv_sem=recv3,
                    device_id=(r, c ^ (flips << 1)),
                    device_id_type=MESH,
                ).start()
    pltpu.make_async_copy(ns.at[pl.ds(4 * q, 4)], x_buf.at[:, p, q], recv3).start()
    sent.append(lambda: wait_bytes(x_buf.at[:, 0, pl.ds(0, 15)], send3))

    rows_of(updt, up)

    def unit_copy(core, unit_y, unit_x, dy, dx):
        unit = bias.at[core, unit_y, unit_x]
        return bias_copy(unit, unit, 1, bu.at[core, unit_y, unit_x], r ^ dy, c ^ (dx << 3))

    def unit_wait(core, unit_y, unit_x):
        wait_bytes(bias.at[core, unit_y, unit_x], bu.at[core, unit_y, unit_x])

    wait_bytes(bias.at[:, 0, 0], bz)
    for d in FAR4[:3]:
        unit_copy(0, y, x, 0, d).start()
        unit_copy(1, y, x, d, 0).start()
    for d in FAR4[:3]:
        unit_copy(0, y, x, d, 0).start()
        unit_copy(1, y, x, 0, d).start()
    for near in (1, 3, 2):
        unit_wait(0, y, x ^ near)
        for d in FAR4[:3]:
            unit_copy(0, y, x ^ near, d, 0).start()
        unit_wait(1, y ^ near, x)
        for d in FAR4[:3]:
            unit_copy(1, y ^ near, x, 0, d).start()

    def bias_sent():
        wait_bytes(bias.at[0], bsend.at[1])
        wait_bytes(bias.at[1, pl.ds(0, 3)], bsend.at[1])
        wait_bytes(bias.at[1, 0, pl.ds(0, 2)], bsend.at[1])

    sent.append(bias_sent)

    wait_bytes(x_buf.at[:, p], recv3)
    rows_swap = pltpu.make_async_remote_copy(
        src_ref=x_buf.at[:, p], dst_ref=x_buf.at[:, p], send_sem=xsend, recv_sem=xrecv,
        device_id=sibling, device_id_type=MESH,
    )
    rows_swap.start()
    sent.append(lambda: rows_swap.wait_send())

    def keys_values(core):
        def body(i):
            rows = x_buf[i, core].reshape(256, 128)
            kb[i, core] = dot(rows, qkvg_ref[:, 128:256]).astype(BF16)
            vt[i, :, pl.ds(pl.multiple_of(256 * core, 256), 256)] = dot_nt(
                qkvg_t[256:384, :], rows
            ).astype(BF16)

        loop(0, 4, body)

    keys_values(p)
    wait_bytes(x_buf.at[:, p], xrecv)
    keys_values(1 - p)

    head_of_row = lax.broadcasted_iota(jnp.int32, (128, 128), 0) // 32
    head_of_lane = lax.broadcasted_iota(jnp.int32, (128, 128), 1) // 64

    def queries_gate(i):
        mine = jnp.concatenate(
            [x_buf[i, core, 8 * p + chips] for chips in range(8) for core in range(2)], axis=0
        )
        queries = dot_nt(qkvg_t[0:128, :], mine).astype(BF16).astype(F32)
        gq[i] = jax.nn.sigmoid(dot_nt(qkvg_t[384:512, :], mine))
        for unit_y in range(4):
            q_t = queries[:, 128 * (unit_y // 2) : 128 * (unit_y // 2) + 128]
            q_s = swap(q_t)
            both = half_lanes(q_t, q_s) if unit_y % 2 == 0 else half_lanes(q_s, q_t)
            for pair in range(2):
                qb[i, unit_y, :, 128 * pair : 128 * pair + 128] = jnp.where(
                    head_of_row == head_of_lane + 2 * pair, both, 0.0
                ).astype(BF16)

    loop(0, 4, queries_gate)

    log2e = 1.0 / math.log(2.0)
    scale = log2e / math.sqrt(32.0)

    def scores_of(i, unit_y, at, highest):
        core, first = at // 4, 64 * (at % 4)
        part = dot(kb[i, core, first : first + 64, :], qb[i, unit_y]) * scale
        part = part + bf[64 * at : 64 * at + 64, :]
        sc[i % 2, 64 * at : 64 * at + 64, :] = part
        top = jnp.max(part.reshape(8, 8, 256), axis=0)
        return top if highest is None else jnp.maximum(highest, top)

    def exps_of(i, at, highest, total):
        part = jnp.exp2(sc[i % 2, 64 * at : 64 * at + 64, :] - highest)
        wb[i % 2, 64 * at : 64 * at + 64, :] = part.astype(BF16)
        here = jnp.sum(part.reshape(8, 8, 256), axis=0)
        return here if total is None else total + here

    def block(step):
        unit_y = y ^ step ^ (step >> 1)

        @pl.when(step == 0)
        def _():
            for d in (1, 3, 2):
                unit_wait(1, y, x ^ d)

        @pl.when(step > 0)
        def _():
            unit_wait(0, unit_y, x)
            for d in (1, 3, 2):
                unit_wait(0, unit_y, x ^ d)
                unit_wait(1, unit_y, x ^ d)

        for core in range(2):
            bf[256 * core : 256 * core + 256, :] = (
                bias[core, unit_y].reshape(256, 256).astype(F32) * log2e
            )
        highest = None
        for at in range(8):
            highest = scores_of(0, unit_y, at, highest)
        for i in range(4):
            top = jnp.max(highest, axis=0, keepdims=True)
            highest = total = None
            for at in range(8):
                if i < 3:
                    highest = scores_of(i + 1, unit_y, at, highest)
                total = exps_of(i, at, top, total)
            inverse = 1.0 / jnp.sum(total, axis=0, keepdims=True)
            out = dot(vt[i], wb[i % 2]) * inverse
            for h in range(4):
                at = (h // 2) * 128
                oscr[i, unit_y, 32 * h : 32 * h + 32, :] = out[32 * h : 32 * h + 32, at : at + 128]

    odd_head = (head_of_row & 1) == 1

    def attend(turn_of):
        loop(2 * turn_of, 2 * turn_of + 2, block)
        t = (y >> 1) ^ turn_of

        def finish(i):
            first = oscr[i, 2 * t]
            second = oscr[i, 2 * t + 1]
            attended = half_lanes(
                jnp.where(odd_head, swap(first), first), jnp.where(odd_head, second, swap(second))
            )
            gated = gq[i, :, pl.ds(pl.multiple_of(128 * t, 128), 128)] * attended
            gs[i, pl.ds(8 * t, 8)] = gated.T.astype(BF16).reshape(8, 16, 128)

        loop(0, 4, finish, unroll=2)

        def send(off):
            cl = 8 * t + off
            to = 16 * p + cl

            @pl.when(to == c)
            def _():
                pltpu.make_async_copy(gs.at[:, cl], h_buf.at[pl.ds(4 * q, 4)], recv4).start()

            @pl.when(to != c)
            def _():
                pltpu.make_async_remote_copy(
                    src_ref=gs.at[:, cl],
                    dst_ref=h_buf.at[pl.ds(4 * q, 4)],
                    send_sem=send4,
                    recv_sem=recv4,
                    device_id=(r, to),
                    device_id_type=MESH,
                ).start()

        loop(0, 8, send)

    loop(0, 2, attend)

    def gated_sent():
        wait_bytes(gs.at[:, pl.ds(0, 15)], send4)

        @pl.when((c >> 4) != p)
        def _():
            wait_bytes(gs.at[:, 0], send4)

    sent.append(gated_sent)

    for wait in sent:
        wait()

    wait_bytes(h_buf, recv4)
    product = dot(h_buf[...].reshape(1024, 128), aout_ref[...])
    out_ref[...] = (up[...] + product).astype(BF16).reshape(64, 16, 128)


def local(pair_map, res_mask, tri_proj, tri_gate, tri_out, att_qkvg, att_bias, att_out):
    dma = pltpu.SemaphoreType.DMA
    return pl.pallas_call(
        kernel,
        out_shape=jax.ShapeDtypeStruct((64, 16, 128), BF16),
        in_specs=[pl.BlockSpec(memory_space=pltpu.HBM)] * 9,
        out_specs=pl.BlockSpec(memory_space=pltpu.VMEM),
        scratch_shapes=[
            pltpu.VMEM((64, 16, 128), BF16),
            pltpu.SMEM((512,), jnp.int32),
            pltpu.VMEM((4, 128), jnp.int32),
            pltpu.VMEM((128, 512), BF16),
            pltpu.VMEM((128, 128), BF16),
            pltpu.VMEM((128, 128), BF16),
            pltpu.VMEM((128, 512), BF16),
            pltpu.VMEM((4, 128), BF16),
            pltpu.VMEM((128, 128), BF16),
            dma((9,)),
            pltpu.VMEM((1024, 128), F32),
            pltpu.VMEM((1024, 128), F32),
            pltpu.VMEM((16, 128, 128), BF16),
            pltpu.VMEM((512, 128), BF16),
            pltpu.VMEM((512, 128), F32),
            pltpu.VMEM((2, 4, 16, 16, 128), BF16),
            pltpu.VMEM((8, 128, 128), F32),
            pltpu.VMEM((8, 128, 128), F32),
            pltpu.VMEM((128, 128), BF16),
            pltpu.VMEM((128, 128), BF16),
            pltpu.VMEM((512, 128), BF16),
            pltpu.VMEM((2, 8, 16, 16, 128), BF16),
            pltpu.VMEM((2, 512, 256), BF16),
            pltpu.VMEM((4, 16, 16, 128), BF16),
            pltpu.VMEM((128, 16, 128), BF16),
            pltpu.VMEM((2048, 128), F32),
            pltpu.VMEM((8, 128, 128), F32),
            pltpu.VMEM((8, 128, 128), F32),
            pltpu.VMEM((1024, 128), F32),
            pltpu.VMEM((64, 16, 128), BF16),
            pltpu.VMEM((32, 128), F32),
            pltpu.VMEM((16, 256), BF16),
            pltpu.VMEM((1024, 128), F32),
            pltpu.VMEM((4, 2, 16, 16, 128), BF16),
            pltpu.VMEM((2, 4, 4, 4, 16, 256), BF16),
            pltpu.VMEM((4, 2, 256, 128), BF16),
            pltpu.VMEM((4, 128, 512), BF16),
            pltpu.VMEM((4, 4, 128, 256), BF16),
            pltpu.VMEM((4, 128, 256), F32),
            pltpu.VMEM((512, 256), F32),
            pltpu.VMEM((2, 512, 256), F32),
            pltpu.VMEM((2, 512, 256), BF16),
            pltpu.VMEM((4, 4, 128, 128), F32),
            pltpu.VMEM((4, 16, 16, 128), BF16),
            pltpu.VMEM((64, 16, 128), BF16),
            dma, dma((8,)),
            dma((8,)), dma((8,)),
            dma, dma((8,)),
            dma((8,)), dma((8,)),
            dma, dma,
            dma, dma,
            dma((2,)),
            dma, dma((2, 4, 4)),
            dma, dma,
        ],
        compiler_params=pltpu.CompilerParams(
            collective_id=0, has_side_effects=True, vmem_limit_bytes=60 * 1024 * 1024
        ),
    )(
        pair_map, res_mask, res_mask.reshape(4, 128), tri_proj, tri_gate, tri_out, att_qkvg,
        att_bias.T, att_out,
    )


def solution(mesh):
    in_specs = (P("row", "col", None), P(), P(), P(), P(), P(), P(), P())
    out_specs = P("row", "col", None)
    return jax.shard_map(local, mesh=mesh, in_specs=in_specs, out_specs=out_specs, check_vma=False)
```

```python
import math

import jax
import jax.numpy as jnp
from jax import lax
from jax.experimental import pallas as pl
from jax.experimental.pallas import tpu as pltpu
from jax.sharding import PartitionSpec as P

EPS = 1e-05
MESH = pl.DeviceIdType.MESH
F32 = jnp.float32
BF16 = jnp.bfloat16
NT = (((1,), (1,)), ((), ()))
FAR4 = (2, 3, 1, 0)
CHUNK = 128
FAR8 = (4, 5, 7, 3, 6, 2, 1, 0)


def loop(low, high, body, unroll=None):
    def step(index, carry):
        body(index)
        return carry

    lax.fori_loop(low, high, step, 0, unroll=unroll)


def norm_over(values, axis):
    centre = values - jnp.mean(values, axis=axis, keepdims=True)
    spread = jnp.mean(centre * centre, axis=axis, keepdims=True)
    return centre * lax.rsqrt(spread + EPS)


def dot(a, b):
    return jnp.dot(a, b, preferred_element_type=F32)


def dot_nt(a, b):
    return lax.dot_general(a, b, NT, preferred_element_type=F32)


def flip(values):
    return values.astype(F32).T.astype(BF16)


def wait_bytes(ref, sem):
    pltpu.make_async_copy(ref, ref, sem).wait()


def kernel(
    pair_hbm, mask_hbm, mask_rows_hbm, proj_hbm, gate_hbm, tout_hbm, qkvg_hbm, abias_hbm, aout_hbm,
    out_ref,
    pair_ref, mask_smem, mask_ref, proj_ref, gate_ref, tout_ref, qkvg_ref, abias_ref, aout_ref, loads,
    xf, xn, nk, wpt, ms, sb, pt, gt, gate_t, tout_t, qkvg_t,
    a_buf, rt, s_buf, t_buf, tf, updt, n2t, n2s, ns, bscr, bm, up,
    x_buf, bias, kb, vt, qb, gq, bf, sc, wb, gs, h_buf,
    send1, recv1, fsend, frecv, send2, recv2, gsend, grecv, send3, recv3, xsend, xrecv,
    bsend, bz, bu, send4, recv4,
):
    r = lax.axis_index("row")
    c = lax.axis_index("col")
    q = c >> 1
    p = c & 1
    chip = r * 16 + q
    half = r >> 2
    y = r & 3
    x = c >> 3
    zh = q & 3
    sibling = (r, c ^ 1)

    fetches = [
        pltpu.make_async_copy(source, target, loads.at[at])
        for at, (source, target) in enumerate(
            [
                (pair_hbm, pair_ref), (mask_hbm, mask_smem), (mask_rows_hbm, mask_ref),
                (proj_hbm, proj_ref), (gate_hbm, gate_ref), (tout_hbm, tout_ref),
                (qkvg_hbm, qkvg_ref), (abias_hbm, abias_ref), (aout_hbm, aout_ref),
            ]
        )
    ]
    for fetch in fetches:
        fetch.start()

    barrier = pltpu.get_barrier_semaphore()

    def greet(row, col):
        pl.semaphore_signal(barrier, inc=1, device_id=(row, col), device_id_type=MESH)

    for dz in FAR8:
        for dy in FAR4:
            for dx in FAR4:
                if dz or dy or dx:
                    greet(r ^ ((dz & 1) << 2 | dy), c ^ (dx << 3 | (dz >> 1) << 1))
    for dq in range(16):
        greet(r, c ^ (2 * dq + 1))
    for dz in range(4):
        greet(r ^ 4, c ^ (2 * dz + 1))

    lane = lax.broadcasted_iota(jnp.int32, (1, 128), 1)
    low = lane < 64

    def half_lanes(a, b):
        return jnp.where(low, a, b)

    def swap(values):
        return pltpu.roll(values, 64, 1)

    for fetch in fetches:
        fetch.wait()

    flat = pair_ref[...].astype(F32).reshape(1024, 128)
    xf[...] = flat
    xn[...] = norm_over(flat, 1).astype(BF16).astype(F32)
    wpt[...] = flip(proj_ref[...])
    for k in range(16):
        part = xn[pl.ds(k, 64, stride=16), :].astype(BF16)
        nk[k] = jnp.concatenate([part, part], axis=0)

    two = mask_ref[pl.ds(r >> 1, 1), :].astype(F32)
    odd = (r & 1) == 1
    turned = swap(jnp.broadcast_to(two, (8, 128)))[0:1]
    row_live = half_lanes(jnp.where(odd, turned, two), jnp.where(odd, two, turned))
    col_live = [mask_smem[c * 16 + k].astype(F32) for k in range(16)]

    pl.semaphore_wait(barrier, 147)

    def project(step):
        to_y = y ^ 2 ^ step ^ (step >> 1)
        first = pl.multiple_of(to_y * 16, 16)
        weights = jnp.concatenate(
            [wpt[pl.ds(64 * b + first, 16), :] for b in range(8)], axis=0
        )
        for k in range(16):
            z = dot_nt(weights, nk[k])
            g = half_lanes(z[0:32], z[64:96])
            v = half_lanes(z[32:64], z[96:128])
            ms[pl.ds(k, 32, stride=16), :] = jax.nn.sigmoid(g) * v * (row_live * col_live[k])
        for zl in range(2):
            sb[zl, to_y] = ms[256 * zl : 256 * zl + 256, :].astype(BF16).reshape(16, 16, 128)

        def send(dx, dz):
            to_zl = half ^ (dz & 1)
            flips = dx << 2 | dz >> 1
            return pltpu.make_async_remote_copy(
                src_ref=sb.at[to_zl, to_y, q ^ flips],
                dst_ref=a_buf.at[p, r, q],
                send_sem=send1,
                recv_sem=recv1.at[r],
                device_id=(to_zl * 4 + to_y, c ^ (flips << 1)),
                device_id_type=MESH,
            )

        for dx in FAR4:
            for dz in FAR8:
                if dx or dz:
                    send(dx, dz).start()

        @pl.when(step < 3)
        def _():
            send(0, 0).start()

        @pl.when(step == 3)
        def _():
            pltpu.make_async_copy(sb.at[half, y, q], a_buf.at[p, r, q], recv1.at[r]).start()

    loop(0, 4, project)
    sent = [lambda: wait_bytes(sb.at[0], send1), lambda: wait_bytes(sb.at[0, pl.ds(0, 3)], send1)]
    sent.append(lambda: wait_bytes(sb.at[0, 0, pl.ds(0, 15)], send1))

    gate_t[...] = flip(gate_ref[...])
    tout_t[...] = flip(tout_ref[...])
    qkvg_t[...] = flip(qkvg_ref[...])

    def prepare(s):
        pos = jnp.concatenate(
            [xf[pl.ds(s, 64, stride=16), :], xf[pl.ds(s + 8, 64, stride=16), :]], axis=0
        )
        pt[s] = pos.T
        norm_pos = jnp.concatenate([nk[s, 0:64], nk[s + 8, 0:64]], axis=0)
        gt[s] = jax.nn.sigmoid(dot_nt(gate_t[...], norm_pos))

    loop(0, 8, prepare)

    def forward_copy(row):
        return pltpu.make_async_remote_copy(
            src_ref=a_buf.at[p, row],
            dst_ref=a_buf.at[p, row],
            send_sem=fsend.at[row],
            recv_sem=frecv.at[row],
            device_id=sibling,
            device_id_type=MESH,
        )

    def turn(core, row):
        part = flip(a_buf[core, row].reshape(256, 128))
        rt[core, pl.ds(pl.multiple_of(row * 64, 64), 64), :] = part[64:128]

    def arriving(step):
        pair = step >> 1
        return r ^ (2 ^ pair ^ (pair >> 1)) ^ ((step & 1) << 2)

    def forward(step):
        row = arriving(step)
        wait_bytes(a_buf.at[p, row], recv1.at[row])
        forward_copy(row).start()
        turn(p, row)

    loop(0, 8, forward)
    sent.append(lambda: loop(0, 8, lambda row: forward_copy(row).wait_send()))

    def turn_other(step):
        row = arriving(step)
        wait_bytes(a_buf.at[1 - p, row], frecv.at[row])
        turn(1 - p, row)

    loop(0, 8, turn_other, unroll=4)

    def triangle(step):
        to_y = y ^ 2 ^ step ^ (step >> 1)
        row = 4 * p + to_y
        prod = dot(rt[0], a_buf[0, row].reshape(256, 128))
        prod = (prod + dot(rt[1], a_buf[1, row].reshape(256, 128))).reshape(16, 2, 16, 128)
        hi = swap(prod[:, 1].reshape(256, 128)).reshape(16, 16, 128)
        s_buf[to_y] = jnp.where(low[None], prod[:, 0], hi).astype(BF16)

        def send(flips):
            return pltpu.make_async_remote_copy(
                src_ref=s_buf.at[to_y, q ^ flips],
                dst_ref=t_buf.at[chip],
                send_sem=send2,
                recv_sem=recv2.at[r],
                device_id=(row, c ^ (flips << 1)),
                device_id_type=MESH,
            )

        for dx in FAR4:
            for dz in FAR4:
                if dx or dz:
                    send(dx << 2 | dz).start()

        @pl.when(jnp.logical_or(step < 3, p != half))
        def _():
            send(0).start()

        @pl.when(jnp.logical_and(step == 3, p == half))
        def _():
            pltpu.make_async_copy(s_buf.at[to_y, q], t_buf.at[chip], recv2.at[r]).start()

    loop(0, 4, triangle, unroll=4)

    def triangle_sent():
        wait_bytes(s_buf.at[pl.ds(0, 3)], send2)
        wait_bytes(s_buf.at[0, pl.ds(0, 15)], send2)

        @pl.when(p != half)
        def _():
            wait_bytes(s_buf.at[0, 0], send2)

    sent.append(triangle_sent)

    def hand_copy(row):
        block = t_buf.at[pl.ds(pl.multiple_of(row * 16, 16), 16)]
        return pltpu.make_async_remote_copy(
            src_ref=block,
            dst_ref=block,
            send_sem=gsend.at[row],
            recv_sem=grecv.at[row],
            device_id=sibling,
            device_id_type=MESH,
        )

    def widen(row):
        block = t_buf[pl.ds(pl.multiple_of(row * 16, 16), 16)]
        tf[pl.ds(pl.multiple_of(row * 256, 256), 256), :] = block.astype(F32).reshape(256, 128)

    @pl.when(p == half)
    def _():
        def hand(step):
            row = arriving(step)
            wait_bytes(t_buf.at[pl.ds(pl.multiple_of(row * 16, 16), 16)], recv2.at[row])
            hand_copy(row).start()
            widen(row)

        loop(0, 8, hand, unroll=4)

    @pl.when(p != half)
    def _():
        def take(step):
            row = arriving(step)
            wait_bytes(t_buf.at[pl.ds(pl.multiple_of(row * 16, 16), 16)], grecv.at[row])
            widen(row)

        loop(0, 8, take, unroll=4)

    def handed():
        @pl.when(p == half)
        def _():
            loop(0, 8, lambda row: hand_copy(row).wait_send())

    sent.append(handed)

    def home(s):
        one = tf[pl.ds(s, 128, stride=16), :]
        two = tf[pl.ds(s + 8, 128, stride=16), :]
        mixed = swap(half_lanes(two, one))
        tri = half_lanes(jnp.where(p == 0, one, mixed), jnp.where(p == 0, mixed, two))
        tri_norm = norm_over(tri, 0).astype(BF16)
        updated = pt[s] + gt[s] * dot(tout_t[...], tri_norm)
        updt[s] = updated
        norm_two = norm_over(updated, 0)
        here = jnp.where(
            low, mask_smem[c * 16 + s].astype(F32), mask_smem[c * 16 + s + 8].astype(F32)
        )
        heads = dot(abias_ref[...], norm_two.astype(BF16))[0:4]
        bscr[pl.ds(s, 4, stride=8), :] = jnp.where(here > 0, heads, -1000000000.0)
        n2t[s] = norm_two

    loop(0, 8, home, unroll=4)

    for pair in range(2):
        h0 = bscr[16 * pair : 16 * pair + 8, :]
        h1 = bscr[16 * pair + 8 : 16 * pair + 16, :]
        tile = jnp.concatenate([half_lanes(h0, swap(h1)), half_lanes(swap(h0), h1)], axis=0)
        bm[:, 128 * pair : 128 * pair + 128] = tile.astype(BF16)

    def bias_copy(src, dst, sem, recv, row, col):
        return pltpu.make_async_remote_copy(
            src_ref=src, dst_ref=dst, send_sem=bsend.at[sem], recv_sem=recv,
            device_id=(row, col), device_id_type=MESH,
        )

    def along_z(dz):
        to = (c ^ ((dz >> 1) << 1)) & 30 | half
        return bias_copy(bm, bias.at[p, y, x, zh], 0, bz, r ^ ((dz & 1) << 2), to)

    for dz in FAR8:
        if dz:
            along_z(dz).start()

    @pl.when(p == half)
    def _():
        pltpu.make_async_copy(bm, bias.at[p, y, x, zh], bz).start()

    @pl.when(p != half)
    def _():
        along_z(0).start()

    def bias_z_sent():
        wait_bytes(bias.at[0, 0, 0], bsend.at[0])
        wait_bytes(bias.at[0, 0, 0, pl.ds(0, 3)], bsend.at[0])

        @pl.when(p != half)
        def _():
            wait_bytes(bias.at[0, 0, 0, 0], bsend.at[0])

    sent.append(bias_z_sent)

    def rows_of(source, target):
        def body(s):
            turned = source[s].T
            target[pl.ds(s, 64, stride=16), :] = turned[0:64]
            target[pl.ds(s + 8, 64, stride=16), :] = turned[64:128]

        loop(0, 8, body, unroll=4)

    rows_of(n2t, n2s)
    ns[...] = n2s[...].astype(BF16).reshape(64, 16, 128)

    def rows_send(dx, dz):
        flips = dx << 2 | dz
        pltpu.make_async_remote_copy(
            src_ref=ns.at[pl.ds(4 * (q ^ flips), 4)],
            dst_ref=x_buf.at[:, p, q],
            send_sem=send3,
            recv_sem=recv3,
            device_id=(r, c ^ (flips << 1)),
            device_id_type=MESH,
        ).start()

    for dx in FAR4:
        rows_send(dx, 2)
    pltpu.make_async_copy(ns.at[pl.ds(4 * q, 4)], x_buf.at[:, p, q], recv3).start()
    sent.append(lambda: wait_bytes(x_buf.at[:, 0, pl.ds(0, 15)], send3))

    rows_of(updt, up)

    def unit_copy(core, unit_y, unit_x, dy, dx):
        unit = bias.at[core, unit_y, unit_x]
        return bias_copy(unit, unit, 1, bu.at[core, unit_y, unit_x], r ^ dy, c ^ (dx << 3))

    def unit_wait(core, unit_y, unit_x):
        wait_bytes(bias.at[core, unit_y, unit_x], bu.at[core, unit_y, unit_x])

    wait_bytes(bias.at[:, 0, 0], bz)
    for d in (1, 3, 2):
        unit_copy(0, y, x, 0, d).start()
        unit_copy(1, y, x, 0, d).start()
    for dz in (3, 1, 0):
        for dx in FAR4:
            if dz or dx:
                rows_send(dx, dz)
    for d in (1, 3, 2):
        unit_copy(0, y, x, d, 0).start()
        unit_copy(1, y, x, d, 0).start()
    for near in (1, 3, 2):
        unit_wait(0, y, x ^ near)
    for dy in (1, 3, 2):
        for near in (1, 3, 2):
            unit_copy(0, y, x ^ near, dy, 0).start()
        unit_wait(1, y ^ dy, x)
        for dx in (1, 3, 2):
            unit_copy(1, y ^ dy, x, 0, dx).start()

    def bias_sent():
        wait_bytes(bias.at[0], bsend.at[1])
        wait_bytes(bias.at[1, pl.ds(0, 3)], bsend.at[1])
        wait_bytes(bias.at[1, 0, pl.ds(0, 2)], bsend.at[1])

    sent.append(bias_sent)

    wait_bytes(x_buf.at[:, p], recv3)
    rows_swap = pltpu.make_async_remote_copy(
        src_ref=x_buf.at[:, p], dst_ref=x_buf.at[:, p], send_sem=xsend, recv_sem=xrecv,
        device_id=sibling, device_id_type=MESH,
    )
    rows_swap.start()
    sent.append(lambda: rows_swap.wait_send())

    def keys_values(core):
        def body(i):
            rows = x_buf[i, core].reshape(256, 128)
            kb[i, core] = dot(rows, qkvg_ref[:, 128:256]).astype(BF16)
            vt[i, :, pl.ds(pl.multiple_of(256 * core, 256), 256)] = dot_nt(
                qkvg_t[256:384, :], rows
            ).astype(BF16)

        loop(0, 4, body, unroll=4)

    keys_values(p)
    wait_bytes(x_buf.at[:, p], xrecv)
    keys_values(1 - p)

    head_of_row = lax.broadcasted_iota(jnp.int32, (128, 128), 0) // 32
    head_of_lane = lax.broadcasted_iota(jnp.int32, (128, 128), 1) // 64

    def queries_gate(pair_i):
        gates = []
        for i in (2 * pair_i, 2 * pair_i + 1):
            mine = jnp.concatenate(
                [x_buf[i, core, 8 * p + chips] for chips in range(8) for core in range(2)], axis=0
            )
            queries = dot_nt(qkvg_t[0:128, :], mine).astype(BF16).astype(F32)
            gates.append(jax.nn.sigmoid(dot_nt(qkvg_t[384:512, :], mine)))
            for unit_y in range(4):
                q_t = queries[:, 128 * (unit_y // 2) : 128 * (unit_y // 2) + 128]
                q_s = swap(q_t)
                both = half_lanes(q_t, q_s) if unit_y % 2 == 0 else half_lanes(q_s, q_t)
                for pair in range(2):
                    qb[i, unit_y, :, 128 * pair : 128 * pair + 128] = jnp.where(
                        head_of_row == head_of_lane + 2 * pair, both, 0.0
                    ).astype(BF16)
        for unit_y in range(4):
            at = 128 * (unit_y // 2)
            one, two = (gate[:, at : at + 128] for gate in gates)
            gq[pair_i, unit_y] = (
                half_lanes(one, swap(two)) if unit_y % 2 == 0 else half_lanes(swap(one), two)
            )

    for pair_i in range(2):
        queries_gate(pair_i)

    log2e = 1.0 / math.log(2.0)
    scale = log2e / math.sqrt(32.0)

    def scores_of(i, unit_y, at, highest):
        core, first = CHUNK * at // 256, CHUNK * at % 256
        part = dot(kb[i, core, first : first + CHUNK, :], qb[i, unit_y]) * scale
        part = part + bf[CHUNK * at : CHUNK * at + CHUNK, :]
        sc[i % 2, CHUNK * at : CHUNK * at + CHUNK, :] = part
        top = jnp.max(part.reshape(CHUNK // 8, 8, 256), axis=0)
        return top if highest is None else jnp.maximum(highest, top)

    def exps_of(i, at, highest, total):
        part = jnp.exp2(sc[i % 2, CHUNK * at : CHUNK * at + CHUNK, :] - highest)
        wb[i % 2, CHUNK * at : CHUNK * at + CHUNK, :] = part.astype(BF16)
        here = jnp.sum(part.reshape(CHUNK // 8, 8, 256), axis=0)
        return here if total is None else total + here

    odd_head = (head_of_row & 1) == 1

    def finish(pair_i, unit_y, first, second):
        attended = half_lanes(
            jnp.where(odd_head, swap(first), first), jnp.where(odd_head, second, swap(second))
        )
        gated = (gq[pair_i, unit_y] * attended).T.astype(BF16)
        for own in range(2):
            gs[2 * pair_i + own, pl.ds(4 * unit_y, 4)] = gated[64 * own : 64 * own + 64].reshape(
                4, 16, 128
            )

    def block(step):
        unit_y = y ^ step ^ (step >> 1)

        @pl.when(step == 0)
        def _():
            for d in (1, 3, 2):
                unit_wait(1, y, x ^ d)

        @pl.when(step > 0)
        def _():
            unit_wait(0, unit_y, x)
            for d in (1, 3, 2):
                unit_wait(0, unit_y, x ^ d)
                unit_wait(1, unit_y, x ^ d)

        for core in range(2):
            bf[256 * core : 256 * core + 256, :] = (
                bias[core, unit_y].reshape(256, 256).astype(F32) * log2e
            )
        highest = None
        for at in range(512 // CHUNK):
            highest = scores_of(0, unit_y, at, highest)
        outs = []
        for i in range(4):
            top = jnp.max(highest, axis=0, keepdims=True)
            highest = total = None
            for at in range(512 // CHUNK):
                if i < 3:
                    highest = scores_of(i + 1, unit_y, at, highest)
                total = exps_of(i, at, top, total)
            inverse = 1.0 / jnp.sum(total, axis=0, keepdims=True)
            out = dot(vt[i], wb[i % 2]) * inverse
            outs.append(
                jnp.concatenate(
                    [
                        out[32 * h : 32 * h + 32, 128 * (h // 2) : 128 * (h // 2) + 128]
                        for h in range(4)
                    ],
                    axis=0,
                )
            )
            if i % 2 == 1:
                finish(i // 2, unit_y, outs[i - 1], outs[i])

        for off in range(4):
            cl = 4 * unit_y + off
            send_gated(cl)

    def send_gated(cl):
        to = 16 * p + cl

        @pl.when(to == c)
        def _():
            pltpu.make_async_copy(gs.at[:, cl], h_buf.at[pl.ds(4 * q, 4)], recv4).start()

        @pl.when(to != c)
        def _():
            pltpu.make_async_remote_copy(
                src_ref=gs.at[:, cl],
                dst_ref=h_buf.at[pl.ds(4 * q, 4)],
                send_sem=send4,
                recv_sem=recv4,
                device_id=(r, to),
                device_id_type=MESH,
            ).start()

    loop(0, 4, block)

    def gated_sent():
        wait_bytes(gs.at[:, pl.ds(0, 15)], send4)

        @pl.when((c >> 4) != p)
        def _():
            wait_bytes(gs.at[:, 0], send4)

    sent.append(gated_sent)

    for wait in sent:
        wait()

    wait_bytes(h_buf, recv4)
    product = dot(h_buf[...].reshape(1024, 128), aout_ref[...])
    out_ref[...] = (up[...] + product).astype(BF16).reshape(64, 16, 128)


def local(pair_map, res_mask, tri_proj, tri_gate, tri_out, att_qkvg, att_bias, att_out):
    dma = pltpu.SemaphoreType.DMA
    return pl.pallas_call(
        kernel,
        out_shape=jax.ShapeDtypeStruct((64, 16, 128), BF16),
        in_specs=[pl.BlockSpec(memory_space=pltpu.HBM)] * 9,
        out_specs=pl.BlockSpec(memory_space=pltpu.VMEM),
        scratch_shapes=[
            pltpu.VMEM((64, 16, 128), BF16),
            pltpu.SMEM((512,), jnp.int32),
            pltpu.VMEM((4, 128), jnp.int32),
            pltpu.VMEM((128, 512), BF16),
            pltpu.VMEM((128, 128), BF16),
            pltpu.VMEM((128, 128), BF16),
            pltpu.VMEM((128, 512), BF16),
            pltpu.VMEM((4, 128), BF16),
            pltpu.VMEM((128, 128), BF16),
            dma((9,)),
            pltpu.VMEM((1024, 128), F32),
            pltpu.VMEM((1024, 128), F32),
            pltpu.VMEM((16, 128, 128), BF16),
            pltpu.VMEM((512, 128), BF16),
            pltpu.VMEM((512, 128), F32),
            pltpu.VMEM((2, 4, 16, 16, 128), BF16),
            pltpu.VMEM((8, 128, 128), F32),
            pltpu.VMEM((8, 128, 128), F32),
            pltpu.VMEM((128, 128), BF16),
            pltpu.VMEM((128, 128), BF16),
            pltpu.VMEM((512, 128), BF16),
            pltpu.VMEM((2, 8, 16, 16, 128), BF16),
            pltpu.VMEM((2, 512, 256), BF16),
            pltpu.VMEM((4, 16, 16, 128), BF16),
            pltpu.VMEM((128, 16, 128), BF16),
            pltpu.VMEM((2048, 128), F32),
            pltpu.VMEM((8, 128, 128), F32),
            pltpu.VMEM((8, 128, 128), F32),
            pltpu.VMEM((1024, 128), F32),
            pltpu.VMEM((64, 16, 128), BF16),
            pltpu.VMEM((32, 128), F32),
            pltpu.VMEM((16, 256), BF16),
            pltpu.VMEM((1024, 128), F32),
            pltpu.VMEM((4, 2, 16, 16, 128), BF16),
            pltpu.VMEM((2, 4, 4, 4, 16, 256), BF16),
            pltpu.VMEM((4, 2, 256, 128), BF16),
            pltpu.VMEM((4, 128, 512), BF16),
            pltpu.VMEM((4, 4, 128, 256), BF16),
            pltpu.VMEM((2, 4, 128, 128), F32),
            pltpu.VMEM((512, 256), F32),
            pltpu.VMEM((2, 512, 256), F32),
            pltpu.VMEM((2, 512, 256), BF16),
            pltpu.VMEM((4, 16, 16, 128), BF16),
            pltpu.VMEM((64, 16, 128), BF16),
            dma, dma((8,)),
            dma((8,)), dma((8,)),
            dma, dma((8,)),
            dma((8,)), dma((8,)),
            dma, dma,
            dma, dma,
            dma((2,)),
            dma, dma((2, 4, 4)),
            dma, dma,
        ],
        compiler_params=pltpu.CompilerParams(
            collective_id=0, has_side_effects=True, vmem_limit_bytes=48 * 1024 * 1024
        ),
    )(
        *(
            pltpu.with_memory_space_constraint(operand, pltpu.HBM)
            for operand in (
                pair_map, res_mask, res_mask.reshape(4, 128), tri_proj, tri_gate, tri_out, att_qkvg,
                att_bias.T, att_out,
            )
        )
    )


def solution(mesh):
    in_specs = (P("row", "col", None), P(), P(), P(), P(), P(), P(), P())
    out_specs = P("row", "col", None)
    return jax.shard_map(local, mesh=mesh, in_specs=in_specs, out_specs=out_specs, check_vma=False)
```

```python
import math

import jax
import jax.numpy as jnp
from jax import lax
from jax.experimental import pallas as pl
from jax.experimental.pallas import tpu as pltpu
from jax.sharding import PartitionSpec as P

EPS = 1e-05
MESH = pl.DeviceIdType.MESH
F32 = jnp.float32
BF16 = jnp.bfloat16
NT = (((1,), (1,)), ((), ()))
FAR4 = (2, 3, 1, 0)
FAR8 = (4, 5, 7, 3, 6, 2, 1, 0)


def loop(low, high, body, unroll=None):
    def step(index, carry):
        body(index)
        return carry

    lax.fori_loop(low, high, step, 0, unroll=unroll)


def norm_over(values, axis):
    centre = values - jnp.mean(values, axis=axis, keepdims=True)
    spread = jnp.mean(centre * centre, axis=axis, keepdims=True)
    return centre * lax.rsqrt(spread + EPS)


def dot(a, b):
    return jnp.dot(a, b, preferred_element_type=F32)


def dot_nt(a, b):
    return lax.dot_general(a, b, NT, preferred_element_type=F32)


def flip(values):
    return values.astype(F32).T.astype(BF16)


def wait_bytes(ref, sem):
    pltpu.make_async_copy(ref, ref, sem).wait()


def kernel(
    pair_hbm, mask_hbm, mask_rows_hbm, proj_hbm, gate_hbm, tout_hbm, qkvg_hbm, abias_hbm, aout_hbm,
    out_ref,
    pair_ref, mask_smem, mask_ref, proj_ref, gate_ref, tout_ref, qkvg_ref, abias_ref, aout_ref, loads,
    pr_buf, xn, nk, wpt, ms, sb, pt, gt, gate_t, tout_t, qkvg_t,
    a_buf, lt, tr, s_buf, t_buf, tf, updt, n2t, bscr, bm, up,
    x_buf, bias, kt, ve, qe, gq, bf, gs, h_buf,
    send1, recv1, fsend, frecv, send2, recv2, gsend, grecv, psend, precv, xsend, xrecv,
    bsend, bz, bu, send4, recv4,
):
    r = lax.axis_index("row")
    c = lax.axis_index("col")
    q = c >> 1
    p = c & 1
    chip = r * 16 + q
    half = r >> 2
    y = r & 3
    x = c >> 3
    zh = q & 3
    sibling = (r, c ^ 1)

    fetches = [
        pltpu.make_async_copy(source, target, loads.at[at])
        for at, (source, target) in enumerate(
            [
                (pair_hbm, pair_ref), (mask_hbm, mask_smem), (mask_rows_hbm, mask_ref),
                (proj_hbm, proj_ref), (gate_hbm, gate_ref), (tout_hbm, tout_ref),
                (qkvg_hbm, qkvg_ref), (abias_hbm, abias_ref), (aout_hbm, aout_ref),
            ]
        )
    ]
    for fetch in fetches:
        fetch.start()

    barrier = pltpu.get_barrier_semaphore()

    def greet(row, col):
        pl.semaphore_signal(barrier, inc=1, device_id=(row, col), device_id_type=MESH)

    for dz in FAR8:
        for dy in FAR4:
            for dx in FAR4:
                if dz or dy or dx:
                    greet(r ^ ((dz & 1) << 2 | dy), c ^ (dx << 3 | (dz >> 1) << 1))
    for dq in range(16):
        greet(r, c ^ (2 * dq + 1))
    for dz in range(4):
        greet(r ^ 4, c ^ (2 * dz + 1))

    lane = lax.broadcasted_iota(jnp.int32, (1, 128), 1)
    low = lane < 64

    def half_lanes(a, b):
        return jnp.where(low, a, b)

    def swap(values):
        return pltpu.roll(values, 64, 1)

    for fetch in fetches:
        fetch.wait()

    flat = pair_ref[...].astype(F32).reshape(1024, 128)
    xn[...] = norm_over(flat, 1).astype(BF16).astype(F32)
    wpt[...] = flip(proj_ref[...])
    for k in range(16):
        part = xn[pl.ds(k, 64, stride=16), :].astype(BF16)
        nk[k] = jnp.concatenate([part, part], axis=0)

    two = mask_ref[pl.ds(r >> 1, 1), :].astype(F32)
    odd = (r & 1) == 1
    turned = swap(jnp.broadcast_to(two, (8, 128)))[0:1]
    is_left = (lane >> 6) == jnp.where(odd, 0, 1)
    row_live = half_lanes(jnp.where(odd, turned, two), jnp.where(odd, two, turned))
    col_live = [mask_smem[c * 16 + k].astype(F32) for k in range(16)]

    pl.semaphore_wait(barrier, 147)

    def project(step):
        to_y = y ^ 2 ^ step ^ (step >> 1)
        first = pl.multiple_of(to_y * 16, 16)
        weights = jnp.concatenate(
            [wpt[pl.ds(64 * b + first, 16), :] for b in range(8)], axis=0
        )
        for k in range(16):
            z = dot_nt(weights, nk[k])
            g = jnp.where(is_left, z[0:32], z[64:96])
            v = jnp.where(is_left, z[32:64], z[96:128])
            ms[pl.ds(k, 32, stride=16), :] = jax.nn.sigmoid(g) * v * (row_live * col_live[k])
        for zl in range(2):
            sb[zl, to_y] = ms[256 * zl : 256 * zl + 256, :].astype(BF16).reshape(16, 16, 128)

        def send(dx, dz):
            to_zl = half ^ (dz & 1)
            flips = dx << 2 | dz >> 1
            return pltpu.make_async_remote_copy(
                src_ref=sb.at[to_zl, to_y, q ^ flips],
                dst_ref=a_buf.at[p, r, q],
                send_sem=send1,
                recv_sem=recv1.at[r],
                device_id=(to_zl * 4 + to_y, c ^ (flips << 1)),
                device_id_type=MESH,
            )

        for dx in FAR4:
            for dz in FAR8:
                if dx or dz:
                    send(dx, dz).start()

        @pl.when(step < 3)
        def _():
            send(0, 0).start()

        @pl.when(step == 3)
        def _():
            pltpu.make_async_copy(sb.at[half, y, q], a_buf.at[p, r, q], recv1.at[r]).start()

    loop(0, 4, project)
    sent = [lambda: wait_bytes(sb.at[0], send1), lambda: wait_bytes(sb.at[0, pl.ds(0, 3)], send1)]
    sent.append(lambda: wait_bytes(sb.at[0, 0, pl.ds(0, 15)], send1))

    def pair_send(flips):
        to = c ^ flips
        pltpu.make_async_remote_copy(
            src_ref=pair_ref.at[pl.ds(2 * to, 2)],
            dst_ref=pr_buf.at[:, c],
            send_sem=psend,
            recv_sem=precv,
            device_id=(r, to),
            device_id_type=MESH,
        ).start()

    for dx in FAR4:
        for dz in FAR4:
            for core in range(2):
                if dx or dz or core:
                    pair_send(dx << 3 | dz << 1 | core)
    pltpu.make_async_copy(pair_ref.at[pl.ds(2 * c, 2)], pr_buf.at[:, c], precv).start()
    sent.append(lambda: wait_bytes(pr_buf.at[:, pl.ds(0, 31)], psend))

    gate_t[...] = flip(gate_ref[...])
    tout_t[...] = flip(tout_ref[...])
    qkvg_t[...] = flip(qkvg_ref[...])

    def forward_copy(row):
        return pltpu.make_async_remote_copy(
            src_ref=a_buf.at[p, row],
            dst_ref=a_buf.at[p, row],
            send_sem=fsend.at[row],
            recv_sem=frecv.at[row],
            device_id=sibling,
            device_id_type=MESH,
        )

    def turn(core, row):
        @pl.when((row >> 2) == p)
        def _():
            part = flip(a_buf[core, row].reshape(256, 128))
            at = pl.multiple_of((row & 3) * 64, 64)
            lt[core, pl.ds(at, 64), :] = jnp.where((row & 1) == 1, part[0:64], part[64:128])

    def arriving(step):
        pair = step >> 1
        return r ^ (2 ^ pair ^ (pair >> 1)) ^ ((step & 1) << 2)

    def forward(step):
        row = arriving(step)
        wait_bytes(a_buf.at[p, row], recv1.at[row])
        forward_copy(row).start()
        turn(p, row)

    loop(0, 8, forward)
    sent.append(lambda: loop(0, 8, lambda row: forward_copy(row).wait_send()))

    def turn_other(step):
        row = arriving(step)
        wait_bytes(a_buf.at[1 - p, row], frecv.at[row])
        turn(1 - p, row)

    loop(0, 8, turn_other, unroll=4)

    def triangle(step):
        pair = (y >> 1) ^ 1 ^ step
        rows = pl.ds(pl.multiple_of(128 * pair, 128), 128)
        for jc in range(4):
            sides = [
                jnp.concatenate(
                    [a_buf[core, 2 * jc + e].reshape(256, 128) for e in range(2)], axis=1
                )
                for core in range(2)
            ]
            prod = dot(lt[0, rows, :], sides[0]) + dot(lt[1, rows, :], sides[1])
            tr[pl.ds(jc, 128, stride=4), :] = half_lanes(prod[:, 0:128], prod[:, 128:256])
        for e in range(2):
            s_buf[2 * pair + e] = tr[256 * e : 256 * e + 256, :].astype(BF16).reshape(16, 16, 128)

        def send(to_y, flips):
            return pltpu.make_async_remote_copy(
                src_ref=s_buf.at[to_y, q ^ flips],
                dst_ref=t_buf.at[chip],
                send_sem=send2,
                recv_sem=recv2.at[r],
                device_id=(4 * p + to_y, c ^ (flips << 1)),
                device_id_type=MESH,
            )

        for own in range(2):
            to_y = y ^ (2 * (1 - step)) ^ (own ^ step)
            for dx in FAR4:
                for dz in FAR4:
                    if dx or dz:
                        send(to_y, dx << 2 | dz).start()
            here = jnp.logical_and(to_y == y, p == half)

            @pl.when(jnp.logical_not(here))
            def _():
                send(to_y, 0).start()

            @pl.when(here)
            def _():
                pltpu.make_async_copy(s_buf.at[to_y, q], t_buf.at[chip], recv2.at[r]).start()

    loop(0, 2, triangle, unroll=2)

    def triangle_sent():
        wait_bytes(s_buf.at[pl.ds(0, 3)], send2)
        wait_bytes(s_buf.at[0, pl.ds(0, 15)], send2)

        @pl.when(p != half)
        def _():
            wait_bytes(s_buf.at[0, 0], send2)

    sent.append(triangle_sent)

    wait_bytes(pr_buf, precv)

    def prepare(s):
        at = s & 3
        rows = pr_buf[s >> 2, pl.ds(8 * at, 8)].astype(F32).reshape(128, 128)
        pt[s] = rows.T
        gt[s] = jax.nn.sigmoid(dot_nt(gate_t[...], norm_over(rows, 1).astype(BF16)))

    loop(0, 8, prepare, unroll=2)

    def hand_copy(row):
        block = t_buf.at[pl.ds(pl.multiple_of(row * 16, 16), 16)]
        return pltpu.make_async_remote_copy(
            src_ref=block,
            dst_ref=block,
            send_sem=gsend.at[row],
            recv_sem=grecv.at[row],
            device_id=sibling,
            device_id_type=MESH,
        )

    def widen(row):
        block = t_buf[pl.ds(pl.multiple_of(row * 16, 16), 16)]
        tf[pl.ds(pl.multiple_of(row * 256, 256), 256), :] = block.astype(F32).reshape(256, 128)

    @pl.when(p == half)
    def _():
        def hand(step):
            row = arriving(step)
            wait_bytes(t_buf.at[pl.ds(pl.multiple_of(row * 16, 16), 16)], recv2.at[row])
            hand_copy(row).start()
            widen(row)

        loop(0, 8, hand, unroll=4)

    @pl.when(p != half)
    def _():
        def take(step):
            row = arriving(step)
            wait_bytes(t_buf.at[pl.ds(pl.multiple_of(row * 16, 16), 16)], grecv.at[row])
            widen(row)

        loop(0, 8, take, unroll=4)

    def handed():
        @pl.when(p == half)
        def _():
            loop(0, 8, lambda row: hand_copy(row).wait_send())

    sent.append(handed)

    def home(s):
        tri = tf[pl.ds(8 * p + s, 128, stride=16), :]
        tri_norm = norm_over(tri, 0).astype(BF16)
        updated = pt[s] + gt[s] * dot(tout_t[...], tri_norm)
        updt[s] = updated
        norm_two = norm_over(updated, 0)
        n2t[s] = norm_two
        heads = dot(abias_ref[...], norm_two.astype(BF16))[0:4]
        live = mask_ref[pl.ds(s & 3, 1), :] > 0
        bscr[s & 1, pl.ds(8 * ((s & 3) >> 1) + (s >> 2), 4, stride=2), :] = jnp.where(
            live, heads, -1000000000.0
        )

    loop(0, 8, home, unroll=4)

    bm[:, 0:128] = bscr[0].astype(BF16)
    bm[:, 128:256] = bscr[1].astype(BF16)

    def bias_copy(src, dst, sem, recv, row, col):
        return pltpu.make_async_remote_copy(
            src_ref=src, dst_ref=dst, send_sem=bsend.at[sem], recv_sem=recv,
            device_id=(row, col), device_id_type=MESH,
        )

    def along_z(dz):
        to = (c ^ ((dz >> 1) << 1)) & 30 | half
        return bias_copy(bm, bias.at[p, y, x, zh], 0, bz, r ^ ((dz & 1) << 2), to)

    for dz in FAR8:
        if dz:
            along_z(dz).start()

    @pl.when(p == half)
    def _():
        pltpu.make_async_copy(bm, bias.at[p, y, x, zh], bz).start()

    @pl.when(p != half)
    def _():
        along_z(0).start()

    def bias_z_sent():
        wait_bytes(bias.at[0, 0, 0], bsend.at[0])
        wait_bytes(bias.at[0, 0, 0, pl.ds(0, 3)], bsend.at[0])

        @pl.when(p != half)
        def _():
            wait_bytes(bias.at[0, 0, 0, 0], bsend.at[0])

    sent.append(bias_z_sent)

    def rows_of(s):
        at = pl.ds(pl.multiple_of(128 * (s & 3), 128), 128)
        x_buf[2 * p + (s >> 2), at, :] = n2t[s].T.astype(BF16)
        up[2 * p + (s >> 2), at, :] = updt[s].T

    loop(0, 8, rows_of, unroll=4)

    def to_sibling(ref, at):
        return pltpu.make_async_remote_copy(
            src_ref=ref, dst_ref=ref, send_sem=xsend.at[at], recv_sem=xrecv.at[at],
            device_id=sibling, device_id_type=MESH,
        )

    swaps = [
        to_sibling(x_buf.at[pl.ds(2 * p, 2)], 0),
        to_sibling(up.at[pl.ds(2 * p, 2), pl.ds(pl.multiple_of(256 * (1 - p), 256), 256)], 1),
    ]
    for swapping in swaps:
        swapping.start()
        sent.append(swapping.wait_send)

    def unit_copy(core, unit_y, unit_x, dy, dx):
        unit = bias.at[core, unit_y, unit_x]
        return bias_copy(unit, unit, 1, bu.at[core, unit_y, unit_x], r ^ dy, c ^ (dx << 3))

    def unit_wait(core, unit_y, unit_x):
        wait_bytes(bias.at[core, unit_y, unit_x], bu.at[core, unit_y, unit_x])

    wait_bytes(bias.at[:, 0, 0], bz)
    for d in (1, 3, 2):
        unit_copy(0, y, x, 0, d).start()
        unit_copy(1, y, x, 0, d).start()
    for d in (1, 3, 2):
        unit_copy(0, y, x, d, 0).start()
        unit_copy(1, y, x, d, 0).start()
    row_at = lax.broadcasted_iota(jnp.int32, (256, 64), 0)
    spread = ((row_at // 8) * 2 + row_at % 2 == lax.broadcasted_iota(jnp.int32, (256, 64), 1)).astype(
        F32
    ).astype(BF16)
    lane_at = lax.broadcasted_iota(jnp.int32, (64, 256), 1)
    gather = ((lane_at // 8) * 2 + lane_at % 2 == lax.broadcasted_iota(jnp.int32, (64, 256), 0)).astype(
        F32
    ).astype(BF16)
    own_head = (lax.broadcasted_iota(jnp.int32, (256, 128), 0) % 8) // 2 == (
        lax.broadcasted_iota(jnp.int32, (256, 128), 1) // 32
    )

    def project_row(i):
        rows = x_buf[i]
        kt[i] = dot_nt(qkvg_t[128:256, :], rows).astype(BF16)
        ve[i, :, 0:128] = dot(rows, qkvg_ref[:, 256:384]).astype(BF16)
        ve[i, :, 128:256] = jnp.ones((512, 128), BF16)
        mine = x_buf[i, pl.ds(pl.multiple_of(256 * p, 256), 256), :]
        queries = dot(mine, qkvg_ref[:, 0:128]).astype(BF16)
        gq[i] = jax.nn.sigmoid(dot(mine, qkvg_ref[:, 384:512]))
        for unit_y in range(4):
            wide = dot(spread, queries[64 * unit_y : 64 * unit_y + 64])
            qe[i, unit_y] = jnp.where(own_head, wide, 0.0).astype(BF16)

    for own in range(2):
        project_row(2 * p + own)

    for near in (1, 3, 2):
        unit_wait(0, y, x ^ near)
    for dy in (1, 3, 2):
        for near in (1, 3, 2):
            unit_copy(0, y, x ^ near, dy, 0).start()
        unit_wait(1, y ^ dy, x)
        for dx in (1, 3, 2):
            unit_copy(1, y ^ dy, x, 0, dx).start()

    def bias_sent():
        wait_bytes(bias.at[0], bsend.at[1])
        wait_bytes(bias.at[1, pl.ds(0, 3)], bsend.at[1])
        wait_bytes(bias.at[1, 0, pl.ds(0, 2)], bsend.at[1])

    sent.append(bias_sent)

    for swapping in swaps:
        swapping.wait_recv()
    for own in range(2):
        project_row(2 - 2 * p + own)

    log2e = 1.0 / math.log(2.0)
    scale = log2e / math.sqrt(32.0)

    def attend(i, unit_y):
        scores = dot(qe[i, unit_y], kt[i]) * scale + bf[...].reshape(256, 512)
        exps = jnp.exp2(scores - jnp.max(scores, axis=1, keepdims=True)).astype(BF16)
        out = dot(exps, ve[i])
        out = jnp.where(own_head, out[:, 0:128] * (1.0 / out[:, 128:256]), 0.0)
        high = out.astype(BF16)
        rest = (out - high.astype(F32)).astype(BF16)
        attended = dot(gather, high) + dot(gather, rest)
        at = pl.multiple_of(64 * unit_y, 64)
        gated = (gq[i, pl.ds(at, 64), :] * attended).astype(BF16)
        result = up[i, pl.ds(pl.multiple_of(256 * p + at, 64), 64), :] + dot(gated, aout_ref[...])
        gs[i, pl.ds(4 * unit_y, 4)] = result.astype(BF16).reshape(4, 16, 128)

    def block(step):
        unit_y = y ^ step ^ (step >> 1)

        @pl.when(step == 0)
        def _():
            for d in (1, 3, 2):
                unit_wait(1, y, x ^ d)

        @pl.when(step > 0)
        def _():
            unit_wait(0, unit_y, x)
            for d in (1, 3, 2):
                unit_wait(0, unit_y, x ^ d)
                unit_wait(1, unit_y, x ^ d)

        for core in range(2):
            tiles = bias[core, unit_y].reshape(16, 16, 256).astype(F32) * log2e
            bf[:, core, :, 0:256] = tiles[:, 0:8]
            bf[:, core, :, 256:512] = tiles[:, 8:16]
        for i in range(4):
            attend(i, unit_y)

        for off in range(4):
            cl = 4 * unit_y + off
            send_gated(cl)

    def send_gated(cl):
        to = 16 * p + cl

        @pl.when(to == c)
        def _():
            pltpu.make_async_copy(gs.at[:, cl], h_buf.at[pl.ds(4 * q, 4)], recv4).start()

        @pl.when(to != c)
        def _():
            pltpu.make_async_remote_copy(
                src_ref=gs.at[:, cl],
                dst_ref=h_buf.at[pl.ds(4 * q, 4)],
                send_sem=send4,
                recv_sem=recv4,
                device_id=(r, to),
                device_id_type=MESH,
            ).start()

    loop(0, 4, block)

    def gated_sent():
        wait_bytes(gs.at[:, pl.ds(0, 15)], send4)

        @pl.when((c >> 4) != p)
        def _():
            wait_bytes(gs.at[:, 0], send4)

    sent.append(gated_sent)

    for wait in sent:
        wait()

    wait_bytes(h_buf, recv4)
    out_ref[...] = h_buf[...]


def local(pair_map, res_mask, tri_proj, tri_gate, tri_out, att_qkvg, att_bias, att_out):
    dma = pltpu.SemaphoreType.DMA
    return pl.pallas_call(
        kernel,
        out_shape=jax.ShapeDtypeStruct((64, 16, 128), BF16),
        in_specs=[pl.BlockSpec(memory_space=pltpu.HBM)] * 9,
        out_specs=pl.BlockSpec(memory_space=pltpu.VMEM),
        scratch_shapes=[
            pltpu.VMEM((64, 16, 128), BF16),
            pltpu.SMEM((512,), jnp.int32),
            pltpu.VMEM((4, 128), jnp.int32),
            pltpu.VMEM((128, 512), BF16),
            pltpu.VMEM((128, 128), BF16),
            pltpu.VMEM((128, 128), BF16),
            pltpu.VMEM((128, 512), BF16),
            pltpu.VMEM((4, 128), BF16),
            pltpu.VMEM((128, 128), BF16),
            dma((9,)),
            pltpu.VMEM((2, 32, 16, 128), BF16),
            pltpu.VMEM((1024, 128), F32),
            pltpu.VMEM((16, 128, 128), BF16),
            pltpu.VMEM((512, 128), BF16),
            pltpu.VMEM((512, 128), F32),
            pltpu.VMEM((2, 4, 16, 16, 128), BF16),
            pltpu.VMEM((8, 128, 128), F32),
            pltpu.VMEM((8, 128, 128), F32),
            pltpu.VMEM((128, 128), BF16),
            pltpu.VMEM((128, 128), BF16),
            pltpu.VMEM((512, 128), BF16),
            pltpu.VMEM((2, 8, 16, 16, 128), BF16),
            pltpu.VMEM((2, 256, 256), BF16),
            pltpu.VMEM((512, 128), F32),
            pltpu.VMEM((4, 16, 16, 128), BF16),
            pltpu.VMEM((128, 16, 128), BF16),
            pltpu.VMEM((2048, 128), F32),
            pltpu.VMEM((8, 128, 128), F32),
            pltpu.VMEM((8, 128, 128), F32),
            pltpu.VMEM((2, 16, 128), F32),
            pltpu.VMEM((16, 256), BF16),
            pltpu.VMEM((4, 512, 128), F32),
            pltpu.VMEM((4, 512, 128), BF16),
            pltpu.VMEM((2, 4, 4, 4, 16, 256), BF16),
            pltpu.VMEM((4, 128, 512), BF16),
            pltpu.VMEM((4, 512, 256), BF16),
            pltpu.VMEM((4, 4, 256, 128), BF16),
            pltpu.VMEM((4, 256, 128), F32),
            pltpu.VMEM((16, 2, 8, 512), F32),
            pltpu.VMEM((4, 16, 16, 128), BF16),
            pltpu.VMEM((64, 16, 128), BF16),
            dma, dma((8,)),
            dma((8,)), dma((8,)),
            dma, dma((8,)),
            dma((8,)), dma((8,)),
            dma, dma,
            dma((2,)), dma((2,)),
            dma((2,)),
            dma, dma((2, 4, 4)),
            dma, dma,
        ],
        compiler_params=pltpu.CompilerParams(
            collective_id=0, has_side_effects=True, vmem_limit_bytes=48 * 1024 * 1024
        ),
    )(
        *(
            pltpu.with_memory_space_constraint(operand, pltpu.HBM)
            for operand in (
                pair_map, res_mask, res_mask.reshape(4, 128), tri_proj, tri_gate, tri_out, att_qkvg,
                att_bias.T, att_out,
            )
        )
    )


def solution(mesh):
    in_specs = (P("row", "col", None), P(), P(), P(), P(), P(), P(), P())
    out_specs = P("row", "col", None)
    return jax.shard_map(local, mesh=mesh, in_specs=in_specs, out_specs=out_specs, check_vma=False)
```

```python
import math

import jax
import jax.numpy as jnp
from jax import lax
from jax.experimental import pallas as pl
from jax.experimental.pallas import tpu as pltpu
from jax.sharding import PartitionSpec as P

EPS = 1e-05
MESH = pl.DeviceIdType.MESH
F32 = jnp.float32
BF16 = jnp.bfloat16
NT = (((1,), (1,)), ((), ()))
ROWS = 4
FAR4 = (2, 3, 1, 0)
FAR8 = (4, 5, 7, 3, 6, 2, 1, 0)


def loop(low, high, body, unroll=None):
    def step(index, carry):
        body(index)
        return carry

    lax.fori_loop(low, high, step, 0, unroll=unroll)


def norm_over(values, axis):
    centre = values - jnp.mean(values, axis=axis, keepdims=True)
    spread = jnp.mean(centre * centre, axis=axis, keepdims=True)
    return centre * lax.rsqrt(spread + EPS)


def dot(a, b):
    return jnp.dot(a, b, preferred_element_type=F32)


def dot_nt(a, b):
    return lax.dot_general(a, b, NT, preferred_element_type=F32)


def flip(values):
    return values.astype(F32).T.astype(BF16)


def wait_bytes(ref, sem):
    pltpu.make_async_copy(ref, ref, sem).wait()


def kernel(
    pair_hbm, mask_hbm, mask_rows_hbm, proj_hbm, gate_hbm, tout_hbm, qkvg_hbm, abias_hbm, aout_hbm,
    out_ref,
    pair_ref, mask_smem, mask_ref, proj_ref, gate_ref, tout_ref, qkvg_ref, abias_ref, aout_ref, loads,
    pr_buf, xn, nk, wpt, ms, sb, pt, gt, gate_t, tout_t, qkvg_t,
    a_buf, lt, tr, s_buf, t_buf, tf, updt, n2t, bscr, bm, up,
    x_buf, bias, kt, ve, qe, gq, bf, sc, wb, mixed, gs, h_buf,
    send1, recv1, fsend, frecv, send2, recv2, gsend, grecv, psend, precv, xsend, xrecv,
    bsend, bz, bu, send4, recv4,
):
    r = lax.axis_index("row")
    c = lax.axis_index("col")
    q = c >> 1
    p = c & 1
    chip = r * 16 + q
    half = r >> 2
    y = r & 3
    x = c >> 3
    zh = q & 3
    sibling = (r, c ^ 1)

    fetches = [
        pltpu.make_async_copy(source, target, loads.at[at])
        for at, (source, target) in enumerate(
            [
                (pair_hbm, pair_ref), (mask_hbm, mask_smem), (mask_rows_hbm, mask_ref),
                (proj_hbm, proj_ref), (gate_hbm, gate_ref), (tout_hbm, tout_ref),
                (qkvg_hbm, qkvg_ref), (abias_hbm, abias_ref), (aout_hbm, aout_ref),
            ]
        )
    ]
    for fetch in fetches:
        fetch.start()

    barrier = pltpu.get_barrier_semaphore()

    def greet(row, col):
        pl.semaphore_signal(barrier, inc=1, device_id=(row, col), device_id_type=MESH)

    for dz in FAR8:
        for dy in FAR4:
            for dx in FAR4:
                if dz or dy or dx:
                    greet(r ^ ((dz & 1) << 2 | dy), c ^ (dx << 3 | (dz >> 1) << 1))
    for dq in range(16):
        greet(r, c ^ (2 * dq + 1))
    for dz in range(4):
        greet(r ^ 4, c ^ (2 * dz + 1))

    lane = lax.broadcasted_iota(jnp.int32, (1, 128), 1)
    low = lane < 64

    def half_lanes(a, b):
        return jnp.where(low, a, b)

    def swap(values):
        return pltpu.roll(values, 64, 1)

    for fetch in fetches:
        fetch.wait()

    flat = pair_ref[...].astype(F32).reshape(1024, 128)
    xn[...] = norm_over(flat, 1).astype(BF16).astype(F32)
    wpt[...] = flip(proj_ref[...])
    for k in range(16):
        part = xn[pl.ds(k, 64, stride=16), :].astype(BF16)
        nk[k] = jnp.concatenate([part, part], axis=0)

    two = mask_ref[pl.ds(r >> 1, 1), :].astype(F32)
    odd = (r & 1) == 1
    turned = swap(jnp.broadcast_to(two, (8, 128)))[0:1]
    is_left = (lane >> 6) == jnp.where(odd, 0, 1)
    row_live = half_lanes(jnp.where(odd, turned, two), jnp.where(odd, two, turned))
    col_live = [mask_smem[c * 16 + k].astype(F32) for k in range(16)]


    def tiles(step):
        to_y = y ^ 2 ^ step ^ (step >> 1)
        first = pl.multiple_of(to_y * 16, 16)
        weights = jnp.concatenate(
            [wpt[pl.ds(64 * b + first, 16), :] for b in range(8)], axis=0
        )
        for k in range(16):
            z = dot_nt(weights, nk[k])
            g = jnp.where(is_left, z[0:32], z[64:96])
            v = jnp.where(is_left, z[32:64], z[96:128])
            ms[pl.ds(k, 32, stride=16), :] = jax.nn.sigmoid(g) * v * (row_live * col_live[k])
        for zl in range(2):
            sb[zl, to_y] = ms[256 * zl : 256 * zl + 256, :].astype(BF16).reshape(16, 16, 128)

    def project(step):
        to_y = y ^ 2 ^ step ^ (step >> 1)

        def send(dx, dz):
            to_zl = half ^ (dz & 1)
            flips = dx << 2 | dz >> 1
            return pltpu.make_async_remote_copy(
                src_ref=sb.at[to_zl, to_y, q ^ flips],
                dst_ref=a_buf.at[p, r, q],
                send_sem=send1,
                recv_sem=recv1.at[r],
                device_id=(to_zl * 4 + to_y, c ^ (flips << 1)),
                device_id_type=MESH,
            )

        for dx in FAR4:
            for dz in FAR8:
                if dx or dz:
                    send(dx, dz).start()

        @pl.when(step < 3)
        def _():
            send(0, 0).start()

        @pl.when(step == 3)
        def _():
            pltpu.make_async_copy(sb.at[half, y, q], a_buf.at[p, r, q], recv1.at[r]).start()

    tiles(0)
    pl.semaphore_wait(barrier, 147)
    project(0)

    def rest(step):
        tiles(step)
        project(step)

    loop(1, 4, rest)
    sent = [lambda: wait_bytes(sb.at[0], send1), lambda: wait_bytes(sb.at[0, pl.ds(0, 3)], send1)]
    sent.append(lambda: wait_bytes(sb.at[0, 0, pl.ds(0, 15)], send1))

    def pair_send(flips):
        to = c ^ flips
        pltpu.make_async_remote_copy(
            src_ref=pair_ref.at[pl.ds(2 * to, 2)],
            dst_ref=pr_buf.at[:, c],
            send_sem=psend,
            recv_sem=precv,
            device_id=(r, to),
            device_id_type=MESH,
        ).start()

    for dx in FAR4:
        for dz in FAR4:
            for core in range(2):
                if dx or dz or core:
                    pair_send(dx << 3 | dz << 1 | core)
    pltpu.make_async_copy(pair_ref.at[pl.ds(2 * c, 2)], pr_buf.at[:, c], precv).start()
    sent.append(lambda: wait_bytes(pr_buf.at[:, pl.ds(0, 31)], psend))

    gate_t[...] = flip(gate_ref[...])
    tout_t[...] = flip(tout_ref[...])
    qkvg_t[...] = flip(qkvg_ref[...])

    def forward_copy(row):
        return pltpu.make_async_remote_copy(
            src_ref=a_buf.at[p, row],
            dst_ref=a_buf.at[p, row],
            send_sem=fsend.at[row],
            recv_sem=frecv.at[row],
            device_id=sibling,
            device_id_type=MESH,
        )

    def turn(core, row):
        @pl.when((row >> 2) == p)
        def _():
            part = flip(a_buf[core, row].reshape(256, 128))
            at = pl.multiple_of((row & 3) * 64, 64)
            lt[core, pl.ds(at, 64), :] = jnp.where((row & 1) == 1, part[0:64], part[64:128])

    def arriving(step):
        pair = step >> 1
        return r ^ (2 ^ pair ^ (pair >> 1)) ^ ((step & 1) << 2)

    def forward(step):
        row = arriving(step)
        wait_bytes(a_buf.at[p, row], recv1.at[row])
        forward_copy(row).start()
        turn(p, row)

    loop(0, 8, forward)
    sent.append(lambda: loop(0, 8, lambda row: forward_copy(row).wait_send()))

    def turn_other(step):
        row = arriving(step)
        wait_bytes(a_buf.at[1 - p, row], frecv.at[row])
        turn(1 - p, row)

    loop(0, 8, turn_other, unroll=4)

    def triangle(step):
        pair = (y >> 1) ^ 1 ^ step
        rows = pl.ds(pl.multiple_of(128 * pair, 128), 128)
        for jc in range(4):
            sides = [
                jnp.concatenate(
                    [a_buf[core, 2 * jc + e].reshape(256, 128) for e in range(2)], axis=1
                )
                for core in range(2)
            ]
            prod = dot(lt[0, rows, :], sides[0]) + dot(lt[1, rows, :], sides[1])
            tr[pl.ds(jc, 128, stride=4), :] = half_lanes(prod[:, 0:128], prod[:, 128:256])
        for e in range(2):
            s_buf[2 * pair + e] = tr[256 * e : 256 * e + 256, :].astype(BF16).reshape(16, 16, 128)

        def send(to_y, flips):
            return pltpu.make_async_remote_copy(
                src_ref=s_buf.at[to_y, q ^ flips],
                dst_ref=t_buf.at[chip],
                send_sem=send2,
                recv_sem=recv2.at[r],
                device_id=(4 * p + to_y, c ^ (flips << 1)),
                device_id_type=MESH,
            )

        for own in range(2):
            to_y = y ^ (2 * (1 - step)) ^ (own ^ step)
            for dx in FAR4:
                for dz in FAR4:
                    if dx or dz:
                        send(to_y, dx << 2 | dz).start()
            here = jnp.logical_and(to_y == y, p == half)

            @pl.when(jnp.logical_not(here))
            def _():
                send(to_y, 0).start()

            @pl.when(here)
            def _():
                pltpu.make_async_copy(s_buf.at[to_y, q], t_buf.at[chip], recv2.at[r]).start()

    loop(0, 2, triangle, unroll=2)

    def triangle_sent():
        wait_bytes(s_buf.at[pl.ds(0, 3)], send2)
        wait_bytes(s_buf.at[0, pl.ds(0, 15)], send2)

        @pl.when(p != half)
        def _():
            wait_bytes(s_buf.at[0, 0], send2)

    sent.append(triangle_sent)

    wait_bytes(pr_buf, precv)

    def prepare(s):
        at = s & 3
        rows = pr_buf[s >> 2, pl.ds(8 * at, 8)].astype(F32).reshape(128, 128)
        pt[s] = rows.T
        gt[s] = jax.nn.sigmoid(dot_nt(gate_t[...], norm_over(rows, 1).astype(BF16)))

    loop(0, 8, prepare, unroll=2)

    def hand_copy(row):
        block = t_buf.at[pl.ds(pl.multiple_of(row * 16, 16), 16)]
        return pltpu.make_async_remote_copy(
            src_ref=block,
            dst_ref=block,
            send_sem=gsend.at[row],
            recv_sem=grecv.at[row],
            device_id=sibling,
            device_id_type=MESH,
        )

    def widen(row):
        block = t_buf[pl.ds(pl.multiple_of(row * 16, 16), 16)]
        tf[pl.ds(pl.multiple_of(row * 256, 256), 256), :] = block.astype(F32).reshape(256, 128)

    @pl.when(p == half)
    def _():
        def hand(step):
            row = arriving(step)
            wait_bytes(t_buf.at[pl.ds(pl.multiple_of(row * 16, 16), 16)], recv2.at[row])
            hand_copy(row).start()
            widen(row)

        loop(0, 8, hand, unroll=4)

    @pl.when(p != half)
    def _():
        def take(step):
            row = arriving(step)
            wait_bytes(t_buf.at[pl.ds(pl.multiple_of(row * 16, 16), 16)], grecv.at[row])
            widen(row)

        loop(0, 8, take, unroll=4)

    def handed():
        @pl.when(p == half)
        def _():
            loop(0, 8, lambda row: hand_copy(row).wait_send())

    sent.append(handed)

    def home(s):
        tri = tf[pl.ds(8 * p + s, 128, stride=16), :]
        tri_norm = norm_over(tri, 0).astype(BF16)
        updated = pt[s] + gt[s] * dot(tout_t[...], tri_norm)
        updt[s] = updated
        norm_two = norm_over(updated, 0)
        n2t[s] = norm_two
        heads = dot(abias_ref[...], norm_two.astype(BF16))[0:4]
        live = mask_ref[pl.ds(s & 3, 1), :] > 0
        bscr[s & 1, pl.ds(8 * ((s & 3) >> 1) + (s >> 2), 4, stride=2), :] = jnp.where(
            live, heads, -1000000000.0
        )

    loop(0, 8, home, unroll=4)

    bm[:, 0:128] = bscr[0].astype(BF16)
    bm[:, 128:256] = bscr[1].astype(BF16)

    def bias_copy(src, dst, sem, recv, row, col):
        return pltpu.make_async_remote_copy(
            src_ref=src, dst_ref=dst, send_sem=bsend.at[sem], recv_sem=recv,
            device_id=(row, col), device_id_type=MESH,
        )

    def along_z(dz):
        to = (c ^ ((dz >> 1) << 1)) & 30 | half
        return bias_copy(bm, bias.at[p, y, x, zh], 0, bz.at[zh], r ^ ((dz & 1) << 2), to)

    for dz in FAR8:
        if dz:
            along_z(dz).start()

    @pl.when(p == half)
    def _():
        pltpu.make_async_copy(bm, bias.at[p, y, x, zh], bz.at[zh]).start()

    @pl.when(p != half)
    def _():
        along_z(0).start()

    def bias_z_sent():
        wait_bytes(bias.at[0, 0, 0], bsend.at[0])
        wait_bytes(bias.at[0, 0, 0, pl.ds(0, 3)], bsend.at[0])

        @pl.when(p != half)
        def _():
            wait_bytes(bias.at[0, 0, 0, 0], bsend.at[0])

    sent.append(bias_z_sent)

    def rows_of(s):
        at = pl.ds(pl.multiple_of(128 * (s & 3), 128), 128)
        x_buf[2 * p + (s >> 2), at, :] = n2t[s].T.astype(BF16)
        up[2 * p + (s >> 2), at, :] = updt[s].T

    loop(0, 8, rows_of, unroll=4)

    def to_sibling(ref, at):
        return pltpu.make_async_remote_copy(
            src_ref=ref, dst_ref=ref, send_sem=xsend.at[at], recv_sem=xrecv.at[at],
            device_id=sibling, device_id_type=MESH,
        )

    swaps = [
        to_sibling(x_buf.at[pl.ds(2 * p, 2)], 0),
        to_sibling(up.at[pl.ds(2 * p, 2), pl.ds(pl.multiple_of(256 * (1 - p), 256), 256)], 1),
    ]
    for swapping in swaps:
        swapping.start()
        sent.append(swapping.wait_send)

    def unit_copy(core, unit_y, unit_x, dy, dx):
        unit = bias.at[core, unit_y, unit_x]
        return bias_copy(unit, unit, 1, bu.at[core, unit_y, unit_x], r ^ dy, c ^ (dx << 3))

    def unit_wait(core, unit_y, unit_x):
        wait_bytes(bias.at[core, unit_y, unit_x], bu.at[core, unit_y, unit_x])

    def part_copy(core, part, dy, dx):
        block = bias.at[core, y, x, part]
        return bias_copy(block, block, 1, bu.at[core, y, x], r ^ dy, c ^ (dx << 3))

    for flips in (0, 1, 3, 2):
        part = zh ^ flips
        wait_bytes(bias.at[:, 0, 0, 0], bz.at[part])
        for d in (1, 3, 2):
            for core in range(2):
                part_copy(core, part, 0, d).start()
                part_copy(core, part, d, 0).start()

    row_at = lax.broadcasted_iota(jnp.int32, (256, 64), 0)
    spread = ((row_at // 8) * 2 + row_at % 2 == lax.broadcasted_iota(jnp.int32, (256, 64), 1)).astype(
        F32
    ).astype(BF16)
    lane_at = lax.broadcasted_iota(jnp.int32, (64, 256), 1)
    gather = ((lane_at // 8) * 2 + lane_at % 2 == lax.broadcasted_iota(jnp.int32, (64, 256), 0)).astype(
        F32
    ).astype(BF16)
    own_head = (lax.broadcasted_iota(jnp.int32, (256, 128), 0) % 8) // 2 == (
        lax.broadcasted_iota(jnp.int32, (256, 128), 1) // 32
    )

    def project_row(i):
        rows = x_buf[i]
        kt[i] = dot_nt(qkvg_t[128:256, :], rows).astype(BF16)
        ve[i, :, 0:128] = dot(rows, qkvg_ref[:, 256:384]).astype(BF16)
        ve[i, :, 128:256] = jnp.ones((512, 128), BF16)
        mine = x_buf[i, pl.ds(pl.multiple_of(256 * p, 256), 256), :]
        queries = dot(mine, qkvg_ref[:, 0:128]).astype(BF16)
        gq[i] = jax.nn.sigmoid(dot(mine, qkvg_ref[:, 384:512]))
        for unit_y in range(4):
            wide = dot(spread, queries[64 * unit_y : 64 * unit_y + 64])
            qe[i, unit_y] = jnp.where(own_head, wide, 0.0).astype(BF16)

    log2e = 1.0 / math.log(2.0)
    scale = log2e / math.sqrt(32.0)

    def scores_of(i):
        for unit_y in range(4):
            sc[unit_y, i] = dot(qe[i, unit_y], kt[i]) * scale

    for own in range(2):
        project_row(2 * p + own)

    for near in (1, 3, 2):
        unit_wait(0, y, x ^ near)
    for dy in (1, 3, 2):
        for near in (1, 3, 2):
            unit_copy(0, y, x ^ near, dy, 0).start()
        unit_wait(1, y ^ dy, x)
        for dx in (1, 3, 2):
            unit_copy(1, y ^ dy, x, 0, dx).start()

    def bias_sent():
        wait_bytes(bias.at[0], bsend.at[1])
        wait_bytes(bias.at[1, pl.ds(0, 3)], bsend.at[1])
        wait_bytes(bias.at[1, 0, pl.ds(0, 2)], bsend.at[1])

    sent.append(bias_sent)

    for swapping in swaps:
        swapping.wait_recv()
    for own in range(2):
        scores_of(2 * p + own)
    for own in range(2):
        project_row(2 - 2 * p + own)
    for own in range(2):
        scores_of(2 - 2 * p + own)

    def soften(i, unit_y):
        for at in range(0, 16, ROWS):
            part = sc[unit_y, i, 16 * at : 16 * (at + ROWS), :]
            part = part + bf[at : at + ROWS].reshape(16 * ROWS, 512)
            exps = jnp.exp2(part - jnp.max(part, axis=1, keepdims=True))
            wb[i, 16 * at : 16 * (at + ROWS), :] = exps.astype(BF16)

    def mix(i):
        out = dot(wb[i], ve[i])
        out = jnp.where(own_head, out[:, 0:128] * (1.0 / out[:, 128:256]), 0.0)
        high = out.astype(BF16)
        mixed[0, :, 128 * i : 128 * i + 128] = high
        mixed[1, :, 128 * i : 128 * i + 128] = (out - high.astype(F32)).astype(BF16)

    def block(step):
        unit_y = y ^ step ^ (step >> 1)

        @pl.when(step == 0)
        def _():
            for d in (1, 3, 2):
                unit_wait(1, y, x ^ d)

        @pl.when(step > 0)
        def _():
            unit_wait(0, unit_y, x)
            for d in (1, 3, 2):
                unit_wait(0, unit_y, x ^ d)
                unit_wait(1, unit_y, x ^ d)

        for core in range(2):
            tiles = bias[core, unit_y].reshape(16, 16, 256).astype(F32) * log2e
            bf[:, core, :, 0:256] = tiles[:, 0:8]
            bf[:, core, :, 256:512] = tiles[:, 8:16]
        for i in range(4):
            soften(i, unit_y)
            if i > 0:
                mix(i - 1)
        mix(3)
        attended = dot(gather, mixed[0]) + dot(gather, mixed[1])
        at = pl.multiple_of(64 * unit_y, 64)
        gated = jnp.concatenate(
            [gq[i, pl.ds(at, 64), :] * attended[:, 128 * i : 128 * i + 128] for i in range(4)], axis=0
        )
        update = dot(gated.astype(BF16), aout_ref[...])
        for i in range(4):
            result = up[i, pl.ds(pl.multiple_of(256 * p + at, 64), 64), :]
            result = result + update[64 * i : 64 * i + 64]
            gs[i, pl.ds(4 * unit_y, 4)] = result.astype(BF16).reshape(4, 16, 128)

        for off in range(4):
            cl = 4 * unit_y + off
            send_gated(cl)

    def send_gated(cl):
        to = 16 * p + cl

        @pl.when(to == c)
        def _():
            pltpu.make_async_copy(gs.at[:, cl], h_buf.at[pl.ds(4 * q, 4)], recv4).start()

        @pl.when(to != c)
        def _():
            pltpu.make_async_remote_copy(
                src_ref=gs.at[:, cl],
                dst_ref=h_buf.at[pl.ds(4 * q, 4)],
                send_sem=send4,
                recv_sem=recv4,
                device_id=(r, to),
                device_id_type=MESH,
            ).start()

    loop(0, 4, block)

    def gated_sent():
        wait_bytes(gs.at[:, pl.ds(0, 15)], send4)

        @pl.when((c >> 4) != p)
        def _():
            wait_bytes(gs.at[:, 0], send4)

    sent.append(gated_sent)

    for wait in sent:
        wait()

    wait_bytes(h_buf, recv4)
    out_ref[...] = h_buf[...]


def local(pair_map, res_mask, tri_proj, tri_gate, tri_out, att_qkvg, att_bias, att_out):
    dma = pltpu.SemaphoreType.DMA
    return pl.pallas_call(
        kernel,
        out_shape=jax.ShapeDtypeStruct((64, 16, 128), BF16),
        in_specs=[pl.BlockSpec(memory_space=pltpu.HBM)] * 9,
        out_specs=pl.BlockSpec(memory_space=pltpu.VMEM),
        scratch_shapes=[
            pltpu.VMEM((64, 16, 128), BF16),
            pltpu.SMEM((512,), jnp.int32),
            pltpu.VMEM((4, 128), jnp.int32),
            pltpu.VMEM((128, 512), BF16),
            pltpu.VMEM((128, 128), BF16),
            pltpu.VMEM((128, 128), BF16),
            pltpu.VMEM((128, 512), BF16),
            pltpu.VMEM((4, 128), BF16),
            pltpu.VMEM((128, 128), BF16),
            dma((9,)),
            pltpu.VMEM((2, 32, 16, 128), BF16),
            pltpu.VMEM((1024, 128), F32),
            pltpu.VMEM((16, 128, 128), BF16),
            pltpu.VMEM((512, 128), BF16),
            pltpu.VMEM((512, 128), F32),
            pltpu.VMEM((2, 4, 16, 16, 128), BF16),
            pltpu.VMEM((8, 128, 128), F32),
            pltpu.VMEM((8, 128, 128), F32),
            pltpu.VMEM((128, 128), BF16),
            pltpu.VMEM((128, 128), BF16),
            pltpu.VMEM((512, 128), BF16),
            pltpu.VMEM((2, 8, 16, 16, 128), BF16),
            pltpu.VMEM((2, 256, 256), BF16),
            pltpu.VMEM((512, 128), F32),
            pltpu.VMEM((4, 16, 16, 128), BF16),
            pltpu.VMEM((128, 16, 128), BF16),
            pltpu.VMEM((2048, 128), F32),
            pltpu.VMEM((8, 128, 128), F32),
            pltpu.VMEM((8, 128, 128), F32),
            pltpu.VMEM((2, 16, 128), F32),
            pltpu.VMEM((16, 256), BF16),
            pltpu.VMEM((4, 512, 128), F32),
            pltpu.VMEM((4, 512, 128), BF16),
            pltpu.VMEM((2, 4, 4, 4, 16, 256), BF16),
            pltpu.VMEM((4, 128, 512), BF16),
            pltpu.VMEM((4, 512, 256), BF16),
            pltpu.VMEM((4, 4, 256, 128), BF16),
            pltpu.VMEM((4, 256, 128), F32),
            pltpu.VMEM((16, 2, 8, 512), F32),
            pltpu.VMEM((4, 4, 256, 512), F32),
            pltpu.VMEM((4, 256, 512), BF16),
            pltpu.VMEM((2, 256, 512), BF16),
            pltpu.VMEM((4, 16, 16, 128), BF16),
            pltpu.VMEM((64, 16, 128), BF16),
            dma, dma((8,)),
            dma((8,)), dma((8,)),
            dma, dma((8,)),
            dma((8,)), dma((8,)),
            dma, dma,
            dma((2,)), dma((2,)),
            dma((2,)),
            dma((4,)), dma((2, 4, 4)),
            dma, dma,
        ],
        compiler_params=pltpu.CompilerParams(
            collective_id=0, has_side_effects=True, vmem_limit_bytes=48 * 1024 * 1024
        ),
    )(
        *(
            pltpu.with_memory_space_constraint(operand, pltpu.HBM)
            for operand in (
                pair_map, res_mask, res_mask.reshape(4, 128), tri_proj, tri_gate, tri_out, att_qkvg,
                att_bias.T, att_out,
            )
        )
    )


def solution(mesh):
    in_specs = (P("row", "col", None), P(), P(), P(), P(), P(), P(), P())
    out_specs = P("row", "col", None)
    return jax.shard_map(local, mesh=mesh, in_specs=in_specs, out_specs=out_specs, check_vma=False)
```

```python
import math

import jax
import jax.numpy as jnp
from jax import lax
from jax.experimental import pallas as pl
from jax.experimental.pallas import tpu as pltpu
from jax.sharding import PartitionSpec as P

EPS = 1e-05
MESH = pl.DeviceIdType.MESH
F32 = jnp.float32
BF16 = jnp.bfloat16
NT = (((1,), (1,)), ((), ()))
FAR4 = (2, 3, 1, 0)
FAR8 = (4, 5, 7, 3, 6, 2, 1, 0)


def loop(low, high, body, unroll=None):
    def step(index, carry):
        body(index)
        return carry

    lax.fori_loop(low, high, step, 0, unroll=unroll)


def norm_over(values, axis):
    centre = values - jnp.mean(values, axis=axis, keepdims=True)
    spread = jnp.mean(centre * centre, axis=axis, keepdims=True)
    return centre * lax.rsqrt(spread + EPS)


def dot(a, b):
    return jnp.dot(a, b, preferred_element_type=F32)


def dot_nt(a, b):
    return lax.dot_general(a, b, NT, preferred_element_type=F32)


def flip(values):
    return values.astype(F32).T.astype(BF16)


def wait_bytes(ref, sem):
    pltpu.make_async_copy(ref, ref, sem).wait()


def kernel(
    pair_hbm, mask_hbm, mask_rows_hbm, proj_hbm, gate_hbm, tout_hbm, qkvg_hbm, abias_hbm, aout_hbm,
    out_ref,
    pair_ref, mask_smem, mask_ref, proj_ref, gate_ref, tout_ref, qkvg_ref, abias_ref, aout_ref, loads,
    pr_buf, xn, nk, wpt, ms, sb, pt, gt, gate_t, tout_t, qkvg_t,
    a_buf, lt, tr, s_buf, t_buf, tf, updt, n2t, bscr, bm, up,
    x_buf, bias, kt, ve, qe, gq, bf, sc, wb, mixed, gs, h_buf,
    send1, recv1, fsend, frecv, send2, recv2, gsend, grecv, psend, precv, xsend, xrecv,
    bsend, bz, bu, send4, recv4,
):
    r = lax.axis_index("row")
    c = lax.axis_index("col")
    q = c >> 1
    p = c & 1
    chip = r * 16 + q
    half = r >> 2
    y = r & 3
    x = c >> 3
    zh = q & 3
    sibling = (r, c ^ 1)

    fetches = [
        pltpu.make_async_copy(source, target, loads.at[at])
        for at, (source, target) in enumerate(
            [
                (pair_hbm, pair_ref), (mask_hbm, mask_smem), (mask_rows_hbm, mask_ref),
                (proj_hbm, proj_ref), (gate_hbm, gate_ref), (tout_hbm, tout_ref),
                (qkvg_hbm, qkvg_ref), (abias_hbm, abias_ref), (aout_hbm, aout_ref),
            ]
        )
    ]
    for fetch in fetches:
        fetch.start()

    barrier = pltpu.get_barrier_semaphore()

    def greet(row, col):
        pl.semaphore_signal(barrier, inc=1, device_id=(row, col), device_id_type=MESH)

    for dz in FAR8:
        for dy in FAR4:
            for dx in FAR4:
                if dz or dy or dx:
                    greet(r ^ ((dz & 1) << 2 | dy), c ^ (dx << 3 | (dz >> 1) << 1))
    for dq in range(16):
        greet(r, c ^ (2 * dq + 1))
    for dz in range(4):
        greet(r ^ 4, c ^ (2 * dz + 1))

    lane = lax.broadcasted_iota(jnp.int32, (1, 128), 1)
    low = lane < 64

    def half_lanes(a, b):
        return jnp.where(low, a, b)

    def swap(values):
        return pltpu.roll(values, 64, 1)

    for fetch in fetches:
        fetch.wait()

    flat = pair_ref[...].astype(F32).reshape(1024, 128)
    xn[...] = norm_over(flat, 1).astype(BF16).astype(F32)
    wpt[...] = flip(proj_ref[...])
    for k in range(16):
        part = xn[pl.ds(k, 64, stride=16), :].astype(BF16)
        nk[k] = jnp.concatenate([part, part], axis=0)

    two = mask_ref[pl.ds(r >> 1, 1), :].astype(F32)
    odd = (r & 1) == 1
    turned = swap(jnp.broadcast_to(two, (8, 128)))[0:1]
    is_left = (lane >> 6) == jnp.where(odd, 0, 1)
    row_live = half_lanes(jnp.where(odd, turned, two), jnp.where(odd, two, turned))
    col_live = [mask_smem[c * 16 + k].astype(F32) for k in range(16)]


    def tiles(step):
        to_y = y ^ 2 ^ step ^ (step >> 1)
        first = pl.multiple_of(to_y * 16, 16)
        weights = jnp.concatenate(
            [wpt[pl.ds(64 * b + first, 16), :] for b in range(8)], axis=0
        )
        for k in range(16):
            z = dot_nt(weights, nk[k])
            g = jnp.where(is_left, z[0:32], z[64:96])
            v = jnp.where(is_left, z[32:64], z[96:128])
            ms[pl.ds(k, 32, stride=16), :] = jax.nn.sigmoid(g) * v * (row_live * col_live[k])
        for zl in range(2):
            sb[zl, to_y] = ms[256 * zl : 256 * zl + 256, :].astype(BF16).reshape(16, 16, 128)

    def project(step):
        to_y = y ^ 2 ^ step ^ (step >> 1)

        def send(dx, dz):
            to_zl = half ^ (dz & 1)
            flips = dx << 2 | dz >> 1
            return pltpu.make_async_remote_copy(
                src_ref=sb.at[to_zl, to_y, q ^ flips],
                dst_ref=a_buf.at[p, r, q],
                send_sem=send1,
                recv_sem=recv1.at[r],
                device_id=(to_zl * 4 + to_y, c ^ (flips << 1)),
                device_id_type=MESH,
            )

        for dx in FAR4:
            for dz in FAR8:
                if dx or dz:
                    send(dx, dz).start()

        @pl.when(step < 3)
        def _():
            send(0, 0).start()

        @pl.when(step == 3)
        def _():
            pltpu.make_async_copy(sb.at[half, y, q], a_buf.at[p, r, q], recv1.at[r]).start()

    tiles(0)
    pl.semaphore_wait(barrier, 147)
    project(0)

    def rest(step):
        tiles(step)
        project(step)

    loop(1, 4, rest)
    sent = [lambda: wait_bytes(sb.at[0], send1), lambda: wait_bytes(sb.at[0, pl.ds(0, 3)], send1)]
    sent.append(lambda: wait_bytes(sb.at[0, 0, pl.ds(0, 15)], send1))

    def pair_send(flips):
        to = c ^ flips
        pltpu.make_async_remote_copy(
            src_ref=pair_ref.at[pl.ds(2 * to, 2)],
            dst_ref=pr_buf.at[:, c],
            send_sem=psend,
            recv_sem=precv,
            device_id=(r, to),
            device_id_type=MESH,
        ).start()

    for dx in FAR4:
        for dz in FAR4:
            for core in range(2):
                if dx or dz or core:
                    pair_send(dx << 3 | dz << 1 | core)
    pltpu.make_async_copy(pair_ref.at[pl.ds(2 * c, 2)], pr_buf.at[:, c], precv).start()
    sent.append(lambda: wait_bytes(pr_buf.at[:, pl.ds(0, 31)], psend))

    gate_t[...] = flip(gate_ref[...])
    tout_t[...] = flip(tout_ref[...])
    qkvg_t[...] = flip(qkvg_ref[...])

    def forward_copy(row):
        return pltpu.make_async_remote_copy(
            src_ref=a_buf.at[p, row],
            dst_ref=a_buf.at[p, row],
            send_sem=fsend.at[row],
            recv_sem=frecv.at[row],
            device_id=sibling,
            device_id_type=MESH,
        )

    def turn(core, row):
        @pl.when((row >> 2) == p)
        def _():
            part = flip(a_buf[core, row].reshape(256, 128))
            at = pl.multiple_of((row & 3) * 64, 64)
            lt[core, pl.ds(at, 64), :] = jnp.where((row & 1) == 1, part[0:64], part[64:128])

    def arriving(step):
        pair = step >> 1
        return r ^ (2 ^ pair ^ (pair >> 1)) ^ ((step & 1) << 2)

    def forward(step):
        row = arriving(step)
        wait_bytes(a_buf.at[p, row], recv1.at[row])
        forward_copy(row).start()
        turn(p, row)

    loop(0, 8, forward)
    sent.append(lambda: loop(0, 8, lambda row: forward_copy(row).wait_send()))

    def turn_other(step):
        row = arriving(step)
        wait_bytes(a_buf.at[1 - p, row], frecv.at[row])
        turn(1 - p, row)

    loop(0, 8, turn_other, unroll=4)

    def triangle(step):
        pair = (y >> 1) ^ 1 ^ step
        rows = pl.ds(pl.multiple_of(128 * pair, 128), 128)
        for jc in range(4):
            sides = [
                jnp.concatenate(
                    [a_buf[core, 2 * jc + e].reshape(256, 128) for e in range(2)], axis=1
                )
                for core in range(2)
            ]
            prod = dot(lt[0, rows, :], sides[0]) + dot(lt[1, rows, :], sides[1])
            tr[pl.ds(jc, 128, stride=4), :] = half_lanes(prod[:, 0:128], prod[:, 128:256])
        for e in range(2):
            s_buf[2 * pair + e] = tr[256 * e : 256 * e + 256, :].astype(BF16).reshape(16, 16, 128)

        def send(to_y, flips):
            return pltpu.make_async_remote_copy(
                src_ref=s_buf.at[to_y, q ^ flips],
                dst_ref=t_buf.at[chip],
                send_sem=send2,
                recv_sem=recv2.at[r],
                device_id=(4 * p + to_y, c ^ (flips << 1)),
                device_id_type=MESH,
            )

        for own in range(2):
            to_y = y ^ (2 * (1 - step)) ^ (own ^ step)
            for dx in FAR4:
                for dz in FAR4:
                    if dx or dz:
                        send(to_y, dx << 2 | dz).start()
            here = jnp.logical_and(to_y == y, p == half)

            @pl.when(jnp.logical_not(here))
            def _():
                send(to_y, 0).start()

            @pl.when(here)
            def _():
                pltpu.make_async_copy(s_buf.at[to_y, q], t_buf.at[chip], recv2.at[r]).start()

    loop(0, 2, triangle, unroll=2)

    def triangle_sent():
        wait_bytes(s_buf.at[pl.ds(0, 3)], send2)
        wait_bytes(s_buf.at[0, pl.ds(0, 15)], send2)

        @pl.when(p != half)
        def _():
            wait_bytes(s_buf.at[0, 0], send2)

    sent.append(triangle_sent)

    wait_bytes(pr_buf, precv)

    def prepare(s):
        at = s & 3
        rows = pr_buf[s >> 2, pl.ds(8 * at, 8)].astype(F32).reshape(128, 128)
        pt[s] = rows.T
        gt[s] = jax.nn.sigmoid(dot_nt(gate_t[...], norm_over(rows, 1).astype(BF16)))

    loop(0, 8, prepare, unroll=2)

    def hand_copy(row):
        block = t_buf.at[pl.ds(pl.multiple_of(row * 16, 16), 16)]
        return pltpu.make_async_remote_copy(
            src_ref=block,
            dst_ref=block,
            send_sem=gsend.at[row],
            recv_sem=grecv.at[row],
            device_id=sibling,
            device_id_type=MESH,
        )

    def widen(row):
        block = t_buf[pl.ds(pl.multiple_of(row * 16, 16), 16)]
        tf[pl.ds(pl.multiple_of(row * 256, 256), 256), :] = block.astype(F32).reshape(256, 128)

    @pl.when(p == half)
    def _():
        def hand(step):
            row = arriving(step)
            wait_bytes(t_buf.at[pl.ds(pl.multiple_of(row * 16, 16), 16)], recv2.at[row])
            hand_copy(row).start()
            widen(row)

        loop(0, 8, hand, unroll=4)

    @pl.when(p != half)
    def _():
        def take(step):
            row = arriving(step)
            wait_bytes(t_buf.at[pl.ds(pl.multiple_of(row * 16, 16), 16)], grecv.at[row])
            widen(row)

        loop(0, 8, take, unroll=4)

    def handed():
        @pl.when(p == half)
        def _():
            loop(0, 8, lambda row: hand_copy(row).wait_send())

    sent.append(handed)

    def home(s):
        tri = tf[pl.ds(8 * p + s, 128, stride=16), :]
        tri_norm = norm_over(tri, 0).astype(BF16)
        updated = pt[s] + gt[s] * dot(tout_t[...], tri_norm)
        updt[s] = updated
        norm_two = norm_over(updated, 0)
        n2t[s] = norm_two
        heads = dot(abias_ref[...], norm_two.astype(BF16))[0:4]
        live = mask_ref[pl.ds(s & 3, 1), :] > 0
        bscr[s & 1, pl.ds(8 * ((s & 3) >> 1) + (s >> 2), 4, stride=2), :] = jnp.where(
            live, heads, -1000000000.0
        )

    loop(0, 8, home, unroll=8)

    bm[:, 0:128] = bscr[0].astype(BF16)
    bm[:, 128:256] = bscr[1].astype(BF16)

    def bias_copy(src, dst, sem, recv, row, col):
        return pltpu.make_async_remote_copy(
            src_ref=src, dst_ref=dst, send_sem=bsend.at[sem], recv_sem=recv,
            device_id=(row, col), device_id_type=MESH,
        )

    def along_z(dz):
        to = (c ^ ((dz >> 1) << 1)) & 30 | half
        return bias_copy(bm, bias.at[p, y, x, zh], 0, bz.at[zh >> 1], r ^ ((dz & 1) << 2), to)

    for dz in FAR8:
        if dz:
            along_z(dz).start()

    @pl.when(p == half)
    def _():
        pltpu.make_async_copy(bm, bias.at[p, y, x, zh], bz.at[zh >> 1]).start()

    @pl.when(p != half)
    def _():
        along_z(0).start()

    def bias_z_sent():
        wait_bytes(bias.at[0, 0, 0], bsend.at[0])
        wait_bytes(bias.at[0, 0, 0, pl.ds(0, 3)], bsend.at[0])

        @pl.when(p != half)
        def _():
            wait_bytes(bias.at[0, 0, 0, 0], bsend.at[0])

    sent.append(bias_z_sent)

    def rows_of(s):
        at = pl.ds(pl.multiple_of(128 * (s & 3), 128), 128)
        x_buf[2 * p + (s >> 2), at, :] = n2t[s].T.astype(BF16)
        up[2 * p + (s >> 2), at, :] = updt[s].T

    loop(0, 8, rows_of, unroll=4)

    def to_sibling(ref, at):
        return pltpu.make_async_remote_copy(
            src_ref=ref, dst_ref=ref, send_sem=xsend.at[at], recv_sem=xrecv.at[at],
            device_id=sibling, device_id_type=MESH,
        )

    swaps = [
        to_sibling(x_buf.at[pl.ds(2 * p, 2)], 0),
        to_sibling(up.at[pl.ds(2 * p, 2), pl.ds(pl.multiple_of(256 * (1 - p), 256), 256)], 1),
    ]
    for swapping in swaps:
        swapping.start()
        sent.append(swapping.wait_send)

    def unit_of(core, unit_y, unit_x, part):
        return bias.at[core, unit_y, unit_x, pl.ds(2 * part, 2)]

    def unit_copy(core, unit_y, unit_x, part, dy, dx):
        unit = unit_of(core, unit_y, unit_x, part)
        return bias_copy(
            unit, unit, 1, bu.at[core, unit_y, unit_x, part], r ^ dy, c ^ (dx << 3)
        )

    def unit_wait(core, unit_y, unit_x, part):
        wait_bytes(unit_of(core, unit_y, unit_x, part), bu.at[core, unit_y, unit_x, part])

    def straight(own):
        part = (zh >> 1) ^ own
        wait_bytes(bias.at[:, 0, 0, pl.ds(0, 2)], bz.at[part])
        for d in (1, 3, 2):
            for core in range(2):
                unit_copy(core, y, x, part, 0, d).start()
                unit_copy(core, y, x, part, d, 0).start()

    def onward(own):
        part = (zh >> 1) ^ own
        for near in (1, 3, 2):
            unit_wait(0, y, x ^ near, part)
        for dy in (1, 3, 2):
            for near in (1, 3, 2):
                unit_copy(0, y, x ^ near, part, dy, 0).start()
            unit_wait(1, y ^ dy, x, part)
            for dx in (1, 3, 2):
                unit_copy(1, y ^ dy, x, part, 0, dx).start()

    row_at = lax.broadcasted_iota(jnp.int32, (256, 64), 0)
    spread = ((row_at // 8) * 2 + row_at % 2 == lax.broadcasted_iota(jnp.int32, (256, 64), 1)).astype(
        F32
    ).astype(BF16)
    lane_at = lax.broadcasted_iota(jnp.int32, (64, 256), 1)
    gather = ((lane_at // 8) * 2 + lane_at % 2 == lax.broadcasted_iota(jnp.int32, (64, 256), 0)).astype(
        F32
    ).astype(BF16)
    own_head = (lax.broadcasted_iota(jnp.int32, (256, 128), 0) % 8) // 2 == (
        lax.broadcasted_iota(jnp.int32, (256, 128), 1) // 32
    )

    def project_row(i):
        rows = x_buf[i]
        kt[i] = dot_nt(qkvg_t[128:256, :], rows).astype(BF16)
        ve[i, :, 0:128] = dot(rows, qkvg_ref[:, 256:384]).astype(BF16)
        ve[i, :, 128:256] = jnp.ones((512, 128), BF16)
        mine = x_buf[i, pl.ds(pl.multiple_of(256 * p, 256), 256), :]
        queries = dot(mine, qkvg_ref[:, 0:128]).astype(BF16)
        gq[i] = jax.nn.sigmoid(dot(mine, qkvg_ref[:, 384:512]))
        for unit_y in range(4):
            wide = dot(spread, queries[64 * unit_y : 64 * unit_y + 64])
            qe[i, unit_y] = jnp.where(own_head, wide, 0.0).astype(BF16)

    log2e = 1.0 / math.log(2.0)
    scale = log2e / math.sqrt(32.0)

    def scores_of(i):
        for unit_y in range(4):
            sc[unit_y, i] = dot(qe[i, unit_y], kt[i]) * scale

    straight(0)
    project_row(2 * p)
    straight(1)
    project_row(2 * p + 1)
    onward(0)
    scores_of(2 * p)
    onward(1)
    scores_of(2 * p + 1)

    def bias_sent():
        wait_bytes(bias.at[0], bsend.at[1])
        wait_bytes(bias.at[1, pl.ds(0, 3)], bsend.at[1])
        wait_bytes(bias.at[1, 0, pl.ds(0, 2)], bsend.at[1])

    sent.append(bias_sent)

    for swapping in swaps:
        swapping.wait_recv()
    for own in range(2):
        project_row(2 - 2 * p + own)
        scores_of(2 - 2 * p + own)

    def soften(unit_y, i):
        for unit_x in range(4):
            rows = slice(64 * unit_x, 64 * unit_x + 64)
            if i == 0:
                for core in range(2):
                    tiles = bias[core, unit_y, unit_x].astype(F32) * log2e
                    bf[4 * unit_x : 4 * unit_x + 4, core, :, 0:256] = tiles[:, 0:8]
                    bf[4 * unit_x : 4 * unit_x + 4, core, :, 256:512] = tiles[:, 8:16]
            part = sc[unit_y, i, rows, :] + bf[4 * unit_x : 4 * unit_x + 4].reshape(64, 512)
            exps = jnp.exp2(part - jnp.max(part, axis=1, keepdims=True))
            wb[i, rows, :] = exps.astype(BF16)

    def mix(i):
        out = dot(wb[i], ve[i])
        out = jnp.where(own_head, out[:, 0:128] * (1.0 / out[:, 128:256]), 0.0)
        high = out.astype(BF16)
        mixed[0, :, 128 * i : 128 * i + 128] = high
        mixed[1, :, 128 * i : 128 * i + 128] = (out - high.astype(F32)).astype(BF16)

    def block(step):
        unit_y = y ^ step ^ (step >> 1)
        own_y = isinstance(step, int)
        for near in (0, 1, 3, 2):
            for part in range(2):
                if not own_y:
                    unit_wait(0, unit_y, x ^ near, part)
                if near:
                    unit_wait(1, unit_y, x ^ near, part)
        for i in range(4):
            soften(unit_y, i)
            if i > 0:
                mix(i - 1)
        mix(3)
        attended = dot(gather, mixed[0]) + dot(gather, mixed[1])
        at = pl.multiple_of(64 * unit_y, 64)
        gated = jnp.concatenate(
            [gq[i, pl.ds(at, 64), :] * attended[:, 128 * i : 128 * i + 128] for i in range(4)], axis=0
        )
        update = dot(gated.astype(BF16), aout_ref[...])
        for i in range(4):
            result = up[i, pl.ds(pl.multiple_of(256 * p + at, 64), 64), :]
            result = result + update[64 * i : 64 * i + 64]
            gs[i, pl.ds(4 * unit_y, 4)] = result.astype(BF16).reshape(4, 16, 128)

        for off in range(4):
            cl = 4 * unit_y + off
            send_gated(cl)

    def send_gated(cl):
        to = 16 * p + cl

        @pl.when(to == c)
        def _():
            pltpu.make_async_copy(gs.at[:, cl], h_buf.at[pl.ds(4 * q, 4)], recv4).start()

        @pl.when(to != c)
        def _():
            pltpu.make_async_remote_copy(
                src_ref=gs.at[:, cl],
                dst_ref=h_buf.at[pl.ds(4 * q, 4)],
                send_sem=send4,
                recv_sem=recv4,
                device_id=(r, to),
                device_id_type=MESH,
            ).start()

    block(0)
    loop(1, 4, block)

    def gated_sent():
        wait_bytes(gs.at[:, pl.ds(0, 15)], send4)

        @pl.when((c >> 4) != p)
        def _():
            wait_bytes(gs.at[:, 0], send4)

    sent.append(gated_sent)

    for wait in sent:
        wait()

    wait_bytes(h_buf, recv4)
    out_ref[...] = h_buf[...]


def local(pair_map, res_mask, tri_proj, tri_gate, tri_out, att_qkvg, att_bias, att_out):
    dma = pltpu.SemaphoreType.DMA
    return pl.pallas_call(
        kernel,
        out_shape=jax.ShapeDtypeStruct((64, 16, 128), BF16),
        in_specs=[pl.BlockSpec(memory_space=pltpu.HBM)] * 9,
        out_specs=pl.BlockSpec(memory_space=pltpu.VMEM),
        scratch_shapes=[
            pltpu.VMEM((64, 16, 128), BF16),
            pltpu.SMEM((512,), jnp.int32),
            pltpu.VMEM((4, 128), jnp.int32),
            pltpu.VMEM((128, 512), BF16),
            pltpu.VMEM((128, 128), BF16),
            pltpu.VMEM((128, 128), BF16),
            pltpu.VMEM((128, 512), BF16),
            pltpu.VMEM((4, 128), BF16),
            pltpu.VMEM((128, 128), BF16),
            dma((9,)),
            pltpu.VMEM((2, 32, 16, 128), BF16),
            pltpu.VMEM((1024, 128), F32),
            pltpu.VMEM((16, 128, 128), BF16),
            pltpu.VMEM((512, 128), BF16),
            pltpu.VMEM((512, 128), F32),
            pltpu.VMEM((2, 4, 16, 16, 128), BF16),
            pltpu.VMEM((8, 128, 128), F32),
            pltpu.VMEM((8, 128, 128), F32),
            pltpu.VMEM((128, 128), BF16),
            pltpu.VMEM((128, 128), BF16),
            pltpu.VMEM((512, 128), BF16),
            pltpu.VMEM((2, 8, 16, 16, 128), BF16),
            pltpu.VMEM((2, 256, 256), BF16),
            pltpu.VMEM((512, 128), F32),
            pltpu.VMEM((4, 16, 16, 128), BF16),
            pltpu.VMEM((128, 16, 128), BF16),
            pltpu.VMEM((2048, 128), F32),
            pltpu.VMEM((8, 128, 128), F32),
            pltpu.VMEM((8, 128, 128), F32),
            pltpu.VMEM((2, 16, 128), F32),
            pltpu.VMEM((16, 256), BF16),
            pltpu.VMEM((4, 512, 128), F32),
            pltpu.VMEM((4, 512, 128), BF16),
            pltpu.VMEM((2, 4, 4, 4, 16, 256), BF16),
            pltpu.VMEM((4, 128, 512), BF16),
            pltpu.VMEM((4, 512, 256), BF16),
            pltpu.VMEM((4, 4, 256, 128), BF16),
            pltpu.VMEM((4, 256, 128), F32),
            pltpu.VMEM((16, 2, 8, 512), F32),
            pltpu.VMEM((4, 4, 256, 512), F32),
            pltpu.VMEM((4, 256, 512), BF16),
            pltpu.VMEM((2, 256, 512), BF16),
            pltpu.VMEM((4, 16, 16, 128), BF16),
            pltpu.VMEM((64, 16, 128), BF16),
            dma, dma((8,)),
            dma((8,)), dma((8,)),
            dma, dma((8,)),
            dma((8,)), dma((8,)),
            dma, dma,
            dma((2,)), dma((2,)),
            dma((2,)),
            dma((2,)), dma((2, 4, 4, 2)),
            dma, dma,
        ],
        compiler_params=pltpu.CompilerParams(
            collective_id=0, has_side_effects=True, vmem_limit_bytes=48 * 1024 * 1024
        ),
    )(
        *(
            pltpu.with_memory_space_constraint(operand, pltpu.HBM)
            for operand in (
                pair_map, res_mask, res_mask.reshape(4, 128), tri_proj, tri_gate, tri_out, att_qkvg,
                att_bias.T, att_out,
            )
        )
    )


def solution(mesh):
    in_specs = (P("row", "col", None), P(), P(), P(), P(), P(), P(), P())
    out_specs = P("row", "col", None)
    return jax.shard_map(local, mesh=mesh, in_specs=in_specs, out_specs=out_specs, check_vma=False)
```

```python
import math

import jax
import jax.numpy as jnp
from jax import lax
from jax.experimental import pallas as pl
from jax.experimental.pallas import tpu as pltpu
from jax.sharding import PartitionSpec as P

EPS = 1e-05
MESH = pl.DeviceIdType.MESH
F32 = jnp.float32
BF16 = jnp.bfloat16
NT = (((1,), (1,)), ((), ()))
FAR4 = (2, 3, 1, 0)
FAR8 = (4, 5, 7, 3, 6, 2, 1, 0)


def loop(low, high, body, unroll=None):
    def step(index, carry):
        body(index)
        return carry

    lax.fori_loop(low, high, step, 0, unroll=unroll)


def norm_over(values, axis):
    centre = values - jnp.mean(values, axis=axis, keepdims=True)
    spread = jnp.mean(centre * centre, axis=axis, keepdims=True)
    return centre * lax.rsqrt(spread + EPS)


def dot(a, b):
    return jnp.dot(a, b, preferred_element_type=F32)


def dot_nt(a, b):
    return lax.dot_general(a, b, NT, preferred_element_type=F32)


def flip(values):
    return values.astype(F32).T.astype(BF16)


def wait_bytes(ref, sem):
    pltpu.make_async_copy(ref, ref, sem).wait()


def kernel(
    pair_hbm, mask_hbm, mask_rows_hbm, proj_hbm, gate_hbm, tout_hbm, qkvg_hbm, abias_hbm, aout_hbm,
    out_ref,
    pair_ref, mask_smem, mask_ref, proj_ref, gate_ref, tout_ref, qkvg_ref, abias_ref, aout_ref, loads,
    pr_buf, xn, nk, wpt, ms, sb, pt, gt, gate_t, tout_t, qkvg_t,
    a_buf, lt, tr, s_buf, t_buf, tf, updt, n2t, bscr, mask_wide, bm, up,
    x_buf, bias, kt, ve, qe, gq, bf, sc, wb, mixed, gs, h_buf,
    send1, recv1, fsend, frecv, send2, recv2, gsend, grecv, psend, precv, xsend, xrecv,
    bsend, bz, bu, send4, recv4,
):
    r = lax.axis_index("row")
    c = lax.axis_index("col")
    q = c >> 1
    p = c & 1
    chip = r * 16 + q
    half = r >> 2
    y = r & 3
    x = c >> 3
    zh = q & 3
    sibling = (r, c ^ 1)

    fetches = [
        pltpu.make_async_copy(source, target, loads.at[at])
        for at, (source, target) in enumerate(
            [
                (pair_hbm, pair_ref), (mask_hbm, mask_smem), (mask_rows_hbm, mask_ref),
                (proj_hbm, proj_ref), (gate_hbm, gate_ref), (tout_hbm, tout_ref),
                (qkvg_hbm, qkvg_ref), (abias_hbm, abias_ref), (aout_hbm, aout_ref),
            ]
        )
    ]
    for fetch in fetches:
        fetch.start()

    barrier = pltpu.get_barrier_semaphore()

    def greet(row, col):
        pl.semaphore_signal(barrier, inc=1, device_id=(row, col), device_id_type=MESH)

    for dz in FAR8:
        for dy in FAR4:
            for dx in FAR4:
                if dz or dy or dx:
                    greet(r ^ ((dz & 1) << 2 | dy), c ^ (dx << 3 | (dz >> 1) << 1))
    for dq in range(16):
        greet(r, c ^ (2 * dq + 1))
    for dz in range(4):
        greet(r ^ 4, c ^ (2 * dz + 1))

    lane = lax.broadcasted_iota(jnp.int32, (1, 128), 1)
    low = lane < 64

    def half_lanes(a, b):
        return jnp.where(low, a, b)

    def swap(values):
        return pltpu.roll(values, 64, 1)

    for fetch in fetches:
        fetch.wait()

    flat = pair_ref[...].astype(F32).reshape(1024, 128)
    xn[...] = norm_over(flat, 1).astype(BF16).astype(F32)
    wpt[...] = flip(proj_ref[...])
    for k in range(16):
        part = xn[pl.ds(k, 64, stride=16), :].astype(BF16)
        nk[k] = jnp.concatenate([part, part], axis=0)

    mask_wide[0:4, :] = mask_ref[...]
    two = mask_wide[pl.ds(r >> 1, 1), :].astype(F32)
    odd = (r & 1) == 1
    turned = swap(jnp.broadcast_to(two, (8, 128)))[0:1]
    is_left = (lane >> 6) == jnp.where(odd, 0, 1)
    row_live = half_lanes(jnp.where(odd, turned, two), jnp.where(odd, two, turned))
    col_live = [mask_smem[c * 16 + k].astype(F32) for k in range(16)]


    def tiles(step):
        to_y = y ^ 2 ^ step ^ (step >> 1)
        first = pl.multiple_of(to_y * 16, 16)
        weights = jnp.concatenate(
            [wpt[pl.ds(64 * b + first, 16), :] for b in range(8)], axis=0
        )
        for k in range(16):
            z = dot_nt(weights, nk[k])
            g = jnp.where(is_left, z[0:32], z[64:96])
            v = jnp.where(is_left, z[32:64], z[96:128])
            ms[pl.ds(k, 32, stride=16), :] = jax.nn.sigmoid(g) * v * (row_live * col_live[k])
        for zl in range(2):
            sb[zl, to_y] = ms[256 * zl : 256 * zl + 256, :].astype(BF16).reshape(16, 16, 128)

    def project(step):
        to_y = y ^ 2 ^ step ^ (step >> 1)

        def send(dx, dz):
            to_zl = half ^ (dz & 1)
            flips = dx << 2 | dz >> 1
            return pltpu.make_async_remote_copy(
                src_ref=sb.at[to_zl, to_y, q ^ flips],
                dst_ref=a_buf.at[p, r, q],
                send_sem=send1,
                recv_sem=recv1.at[r],
                device_id=(to_zl * 4 + to_y, c ^ (flips << 1)),
                device_id_type=MESH,
            )

        for dx in FAR4:
            for dz in FAR8:
                if dx or dz:
                    send(dx, dz).start()

        @pl.when(step < 3)
        def _():
            send(0, 0).start()

        @pl.when(step == 3)
        def _():
            pltpu.make_async_copy(sb.at[half, y, q], a_buf.at[p, r, q], recv1.at[r]).start()

    tiles(0)
    pl.semaphore_wait(barrier, 147)
    project(0)

    def rest(step):
        tiles(step)
        project(step)

    loop(1, 4, rest)
    sent = [lambda: wait_bytes(sb.at[0], send1), lambda: wait_bytes(sb.at[0, pl.ds(0, 3)], send1)]
    sent.append(lambda: wait_bytes(sb.at[0, 0, pl.ds(0, 15)], send1))

    def pair_send(flips):
        to = c ^ flips
        pltpu.make_async_remote_copy(
            src_ref=pair_ref.at[pl.ds(2 * to, 2)],
            dst_ref=pr_buf.at[:, c],
            send_sem=psend,
            recv_sem=precv,
            device_id=(r, to),
            device_id_type=MESH,
        ).start()

    for dx in FAR4:
        for dz in FAR4:
            for core in range(2):
                if dx or dz or core:
                    pair_send(dx << 3 | dz << 1 | core)
    pltpu.make_async_copy(pair_ref.at[pl.ds(2 * c, 2)], pr_buf.at[:, c], precv).start()
    sent.append(lambda: wait_bytes(pr_buf.at[:, pl.ds(0, 31)], psend))

    gate_t[...] = flip(gate_ref[...])
    tout_t[...] = flip(tout_ref[...])
    qkvg_t[...] = flip(qkvg_ref[...])

    def forward_copy(row):
        return pltpu.make_async_remote_copy(
            src_ref=a_buf.at[p, row],
            dst_ref=a_buf.at[p, row],
            send_sem=fsend.at[row],
            recv_sem=frecv.at[row],
            device_id=sibling,
            device_id_type=MESH,
        )

    def turn(core, row):
        @pl.when((row >> 2) == p)
        def _():
            part = flip(a_buf[core, row].reshape(256, 128))
            at = pl.multiple_of((row & 3) * 64, 64)
            lt[core, pl.ds(at, 64), :] = jnp.where((row & 1) == 1, part[0:64], part[64:128])

    def arriving(step):
        pair = step >> 1
        return r ^ (2 ^ pair ^ (pair >> 1)) ^ ((step & 1) << 2)

    def forward(step):
        row = arriving(step)
        wait_bytes(a_buf.at[p, row], recv1.at[row])
        forward_copy(row).start()
        turn(p, row)

    loop(0, 8, forward)
    sent.append(lambda: loop(0, 8, lambda row: forward_copy(row).wait_send()))

    def turn_other(step):
        row = arriving(step)
        wait_bytes(a_buf.at[1 - p, row], frecv.at[row])
        turn(1 - p, row)

    loop(0, 8, turn_other, unroll=4)

    def triangle(step):
        pair = (y >> 1) ^ 1 ^ step
        rows = pl.ds(pl.multiple_of(128 * pair, 128), 128)
        for jc in range(4):
            sides = [
                jnp.concatenate(
                    [a_buf[core, 2 * jc + e].reshape(256, 128) for e in range(2)], axis=1
                )
                for core in range(2)
            ]
            prod = dot(lt[0, rows, :], sides[0]) + dot(lt[1, rows, :], sides[1])
            tr[pl.ds(jc, 128, stride=4), :] = half_lanes(prod[:, 0:128], prod[:, 128:256])
        for e in range(2):
            s_buf[2 * pair + e] = tr[256 * e : 256 * e + 256, :].astype(BF16).reshape(16, 16, 128)

        def send(to_y, flips):
            return pltpu.make_async_remote_copy(
                src_ref=s_buf.at[to_y, q ^ flips],
                dst_ref=t_buf.at[chip],
                send_sem=send2,
                recv_sem=recv2.at[r],
                device_id=(4 * p + to_y, c ^ (flips << 1)),
                device_id_type=MESH,
            )

        for own in range(2):
            to_y = y ^ (2 * (1 - step)) ^ (own ^ step)
            for dx in FAR4:
                for dz in FAR4:
                    if dx or dz:
                        send(to_y, dx << 2 | dz).start()
            here = jnp.logical_and(to_y == y, p == half)

            @pl.when(jnp.logical_not(here))
            def _():
                send(to_y, 0).start()

            @pl.when(here)
            def _():
                pltpu.make_async_copy(s_buf.at[to_y, q], t_buf.at[chip], recv2.at[r]).start()

    loop(0, 2, triangle, unroll=2)

    def triangle_sent():
        wait_bytes(s_buf.at[pl.ds(0, 3)], send2)
        wait_bytes(s_buf.at[0, pl.ds(0, 15)], send2)

        @pl.when(p != half)
        def _():
            wait_bytes(s_buf.at[0, 0], send2)

    sent.append(triangle_sent)

    wait_bytes(pr_buf, precv)

    def prepare(s):
        at = s & 3
        rows = pr_buf[s >> 2, pl.ds(8 * at, 8)].astype(F32).reshape(128, 128)
        pt[s] = rows.T
        gt[s] = jax.nn.sigmoid(dot_nt(gate_t[...], norm_over(rows, 1).astype(BF16)))

    loop(0, 8, prepare, unroll=2)

    def hand_copy(row):
        block = t_buf.at[pl.ds(pl.multiple_of(row * 16, 16), 16)]
        return pltpu.make_async_remote_copy(
            src_ref=block,
            dst_ref=block,
            send_sem=gsend.at[row],
            recv_sem=grecv.at[row],
            device_id=sibling,
            device_id_type=MESH,
        )

    def widen(row):
        block = t_buf[pl.ds(pl.multiple_of(row * 16, 16), 16)]
        tf[pl.ds(pl.multiple_of(row * 256, 256), 256), :] = block.astype(F32).reshape(256, 128)

    @pl.when(p == half)
    def _():
        def hand(step):
            row = arriving(step)
            wait_bytes(t_buf.at[pl.ds(pl.multiple_of(row * 16, 16), 16)], recv2.at[row])
            hand_copy(row).start()
            widen(row)

        loop(0, 8, hand, unroll=4)

    @pl.when(p != half)
    def _():
        def take(step):
            row = arriving(step)
            wait_bytes(t_buf.at[pl.ds(pl.multiple_of(row * 16, 16), 16)], grecv.at[row])
            widen(row)

        loop(0, 8, take, unroll=4)

    def handed():
        @pl.when(p == half)
        def _():
            loop(0, 8, lambda row: hand_copy(row).wait_send())

    sent.append(handed)

    def home(s):
        tri = tf[pl.ds(8 * p + s, 128, stride=16), :]
        tri_norm = norm_over(tri, 0).astype(BF16)
        updated = pt[s] + gt[s] * dot(tout_t[...], tri_norm)
        updt[s] = updated
        norm_two = norm_over(updated, 0)
        n2t[s] = norm_two
        heads = dot(abias_ref[...], norm_two.astype(BF16))[0:4]
        live = mask_wide[pl.ds(s & 3, 1), :] > 0
        bscr[s & 1, pl.ds(8 * ((s & 3) >> 1) + (s >> 2), 4, stride=2), :] = jnp.where(
            live, heads, -1000000000.0
        )

    loop(0, 8, home, unroll=8)

    bm[:, 0:128] = bscr[0, 0:16, :].astype(BF16)
    bm[:, 128:256] = bscr[1, 0:16, :].astype(BF16)

    def bias_copy(src, dst, sem, recv, row, col):
        return pltpu.make_async_remote_copy(
            src_ref=src, dst_ref=dst, send_sem=bsend.at[sem], recv_sem=recv,
            device_id=(row, col), device_id_type=MESH,
        )

    def along_z(dz):
        to = (c ^ ((dz >> 1) << 1)) & 30 | half
        return bias_copy(bm, bias.at[p, y, x, zh], 0, bz.at[zh >> 1], r ^ ((dz & 1) << 2), to)

    for dz in FAR8:
        if dz:
            along_z(dz).start()

    @pl.when(p == half)
    def _():
        pltpu.make_async_copy(bm, bias.at[p, y, x, zh], bz.at[zh >> 1]).start()

    @pl.when(p != half)
    def _():
        along_z(0).start()

    def bias_z_sent():
        wait_bytes(bias.at[0, 0, 0], bsend.at[0])
        wait_bytes(bias.at[0, 0, 0, pl.ds(0, 3)], bsend.at[0])

        @pl.when(p != half)
        def _():
            wait_bytes(bias.at[0, 0, 0, 0], bsend.at[0])

    sent.append(bias_z_sent)

    def rows_of(s):
        at = pl.ds(pl.multiple_of(128 * (s & 3), 128), 128)
        x_buf[2 * p + (s >> 2), at, :] = n2t[s].T.astype(BF16)
        up[2 * p + (s >> 2), at, :] = updt[s].T

    loop(0, 8, rows_of, unroll=4)

    def to_sibling(ref, at):
        return pltpu.make_async_remote_copy(
            src_ref=ref, dst_ref=ref, send_sem=xsend.at[at], recv_sem=xrecv.at[at],
            device_id=sibling, device_id_type=MESH,
        )

    swaps = [
        to_sibling(x_buf.at[pl.ds(2 * p, 2)], 0),
        to_sibling(up.at[pl.ds(2 * p, 2), pl.ds(pl.multiple_of(256 * (1 - p), 256), 256)], 1),
    ]
    for swapping in swaps:
        swapping.start()
        sent.append(swapping.wait_send)

    def unit_of(core, unit_y, unit_x, part):
        return bias.at[core, unit_y, unit_x, pl.ds(2 * part, 2)]

    def unit_copy(core, unit_y, unit_x, part, dy, dx):
        unit = unit_of(core, unit_y, unit_x, part)
        return bias_copy(
            unit, unit, 1, bu.at[core, unit_y, unit_x, part], r ^ dy, c ^ (dx << 3)
        )

    def unit_wait(core, unit_y, unit_x, part):
        wait_bytes(unit_of(core, unit_y, unit_x, part), bu.at[core, unit_y, unit_x, part])

    def straight(own):
        part = (zh >> 1) ^ own
        wait_bytes(bias.at[:, 0, 0, pl.ds(0, 2)], bz.at[part])
        for d in (1, 3, 2):
            for core in range(2):
                unit_copy(core, y, x, part, 0, d).start()
                unit_copy(core, y, x, part, d, 0).start()

    def onward(own):
        part = (zh >> 1) ^ own
        for near in (1, 3, 2):
            unit_wait(0, y, x ^ near, part)
        for dy in (1, 3, 2):
            for near in (1, 3, 2):
                unit_copy(0, y, x ^ near, part, dy, 0).start()
            unit_wait(1, y ^ dy, x, part)
            for dx in (1, 3, 2):
                unit_copy(1, y ^ dy, x, part, 0, dx).start()

    row_at = lax.broadcasted_iota(jnp.int32, (256, 64), 0)
    spread = ((row_at // 8) * 2 + row_at % 2 == lax.broadcasted_iota(jnp.int32, (256, 64), 1)).astype(
        F32
    ).astype(BF16)
    lane_at = lax.broadcasted_iota(jnp.int32, (64, 256), 1)
    gather = ((lane_at // 8) * 2 + lane_at % 2 == lax.broadcasted_iota(jnp.int32, (64, 256), 0)).astype(
        F32
    ).astype(BF16)
    own_head = (lax.broadcasted_iota(jnp.int32, (256, 128), 0) % 8) // 2 == (
        lax.broadcasted_iota(jnp.int32, (256, 128), 1) // 32
    )

    def project_row(i):
        rows = x_buf[i]
        kt[i] = dot_nt(qkvg_t[128:256, :], rows).astype(BF16)
        ve[i, :, 0:128] = dot(rows, qkvg_ref[:, 256:384]).astype(BF16)
        ve[i, :, 128:256] = jnp.ones((512, 128), BF16)
        mine = x_buf[i, pl.ds(pl.multiple_of(256 * p, 256), 256), :]
        queries = dot(mine, qkvg_ref[:, 0:128]).astype(BF16)
        gq[i] = jax.nn.sigmoid(dot(mine, qkvg_ref[:, 384:512]))
        for unit_y in range(4):
            wide = dot(spread, queries[64 * unit_y : 64 * unit_y + 64])
            qe[i, unit_y] = jnp.where(own_head, wide, 0.0).astype(BF16)

    log2e = 1.0 / math.log(2.0)
    scale = log2e / math.sqrt(32.0)

    def scores_of(i):
        for unit_y in range(4):
            sc[unit_y, i] = dot(qe[i, unit_y], kt[i]) * scale

    straight(0)
    project_row(2 * p)
    straight(1)
    project_row(2 * p + 1)
    onward(0)
    scores_of(2 * p)
    onward(1)
    scores_of(2 * p + 1)

    def bias_sent():
        wait_bytes(bias.at[0], bsend.at[1])
        wait_bytes(bias.at[1, pl.ds(0, 3)], bsend.at[1])
        wait_bytes(bias.at[1, 0, pl.ds(0, 2)], bsend.at[1])

    sent.append(bias_sent)

    for swapping in swaps:
        swapping.wait_recv()
    for own in range(2):
        project_row(2 - 2 * p + own)
        scores_of(2 - 2 * p + own)

    def soften(unit_y, i):
        for unit_x in range(4):
            rows = slice(64 * unit_x, 64 * unit_x + 64)
            if i == 0:
                for core in range(2):
                    tiles = bias[core, unit_y, unit_x].astype(F32) * log2e
                    bf[4 * unit_x : 4 * unit_x + 4, core, :, 0:256] = tiles[:, 0:8]
                    bf[4 * unit_x : 4 * unit_x + 4, core, :, 256:512] = tiles[:, 8:16]
            part = sc[unit_y, i, rows, :] + bf[4 * unit_x : 4 * unit_x + 4].reshape(64, 512)
            exps = jnp.exp2(part - jnp.max(part, axis=1, keepdims=True))
            wb[i, rows, :] = exps.astype(BF16)

    def mix(i):
        out = dot(wb[i], ve[i])
        out = jnp.where(own_head, out[:, 0:128] * (1.0 / out[:, 128:256]), 0.0)
        high = out.astype(BF16)
        mixed[0, :, 128 * i : 128 * i + 128] = high
        mixed[1, :, 128 * i : 128 * i + 128] = (out - high.astype(F32)).astype(BF16)

    def block(step):
        unit_y = y ^ step ^ (step >> 1)
        own_y = isinstance(step, int)
        for near in (0, 1, 3, 2):
            for part in range(2):
                if not own_y:
                    unit_wait(0, unit_y, x ^ near, part)
                if near:
                    unit_wait(1, unit_y, x ^ near, part)
        for i in range(4):
            soften(unit_y, i)
            if i > 0:
                mix(i - 1)
        mix(3)
        attended = dot(gather, mixed[0]) + dot(gather, mixed[1])
        at = pl.multiple_of(64 * unit_y, 64)
        gated = jnp.concatenate(
            [gq[i, pl.ds(at, 64), :] * attended[:, 128 * i : 128 * i + 128] for i in range(4)], axis=0
        )
        update = dot(gated.astype(BF16), aout_ref[...])
        for i in range(4):
            result = up[i, pl.ds(pl.multiple_of(256 * p + at, 64), 64), :]
            result = result + update[64 * i : 64 * i + 64]
            gs[i, pl.ds(4 * unit_y, 4)] = result.astype(BF16).reshape(4, 16, 128)

        for off in range(4):
            cl = 4 * unit_y + off
            send_gated(cl)

    def send_gated(cl):
        to = 16 * p + cl

        @pl.when(to == c)
        def _():
            pltpu.make_async_copy(gs.at[:, cl], h_buf.at[pl.ds(4 * q, 4)], recv4).start()

        @pl.when(to != c)
        def _():
            pltpu.make_async_remote_copy(
                src_ref=gs.at[:, cl],
                dst_ref=h_buf.at[pl.ds(4 * q, 4)],
                send_sem=send4,
                recv_sem=recv4,
                device_id=(r, to),
                device_id_type=MESH,
            ).start()

    block(0)
    loop(1, 4, block)

    def gated_sent():
        wait_bytes(gs.at[:, pl.ds(0, 15)], send4)

        @pl.when((c >> 4) != p)
        def _():
            wait_bytes(gs.at[:, 0], send4)

    sent.append(gated_sent)

    for wait in sent:
        wait()

    wait_bytes(h_buf, recv4)
    out_ref[...] = h_buf[...]


def local(pair_map, res_mask, tri_proj, tri_gate, tri_out, att_qkvg, att_bias, att_out):
    dma = pltpu.SemaphoreType.DMA
    return pl.pallas_call(
        kernel,
        out_shape=jax.ShapeDtypeStruct((64, 16, 128), BF16),
        in_specs=[pl.BlockSpec(memory_space=pltpu.HBM)] * 9,
        out_specs=pl.BlockSpec(memory_space=pltpu.VMEM),
        scratch_shapes=[
            pltpu.VMEM((64, 16, 128), BF16),
            pltpu.SMEM((512,), jnp.int32),
            pltpu.VMEM((4, 128), jnp.int32),
            pltpu.VMEM((128, 512), BF16),
            pltpu.VMEM((128, 128), BF16),
            pltpu.VMEM((128, 128), BF16),
            pltpu.VMEM((128, 512), BF16),
            pltpu.VMEM((4, 128), BF16),
            pltpu.VMEM((128, 128), BF16),
            dma((9,)),
            pltpu.VMEM((2, 32, 16, 128), BF16),
            pltpu.VMEM((1024, 128), F32),
            pltpu.VMEM((16, 128, 128), BF16),
            pltpu.VMEM((512, 128), BF16),
            pltpu.VMEM((512, 128), F32),
            pltpu.VMEM((2, 4, 16, 16, 128), BF16),
            pltpu.VMEM((8, 128, 128), F32),
            pltpu.VMEM((8, 128, 128), F32),
            pltpu.VMEM((128, 128), BF16),
            pltpu.VMEM((128, 128), BF16),
            pltpu.VMEM((512, 128), BF16),
            pltpu.VMEM((2, 8, 16, 16, 128), BF16),
            pltpu.VMEM((2, 256, 256), BF16),
            pltpu.VMEM((512, 128), F32),
            pltpu.VMEM((4, 16, 16, 128), BF16),
            pltpu.VMEM((128, 16, 128), BF16),
            pltpu.VMEM((2048, 128), F32),
            pltpu.VMEM((8, 128, 128), F32),
            pltpu.VMEM((8, 128, 128), F32),
            pltpu.VMEM((2, 24, 128), F32),
            pltpu.VMEM((16, 128), jnp.int32),
            pltpu.VMEM((16, 256), BF16),
            pltpu.VMEM((4, 512, 128), F32),
            pltpu.VMEM((4, 512, 128), BF16),
            pltpu.VMEM((2, 4, 4, 4, 16, 256), BF16),
            pltpu.VMEM((4, 128, 512), BF16),
            pltpu.VMEM((4, 512, 256), BF16),
            pltpu.VMEM((4, 4, 256, 128), BF16),
            pltpu.VMEM((4, 256, 128), F32),
            pltpu.VMEM((16, 2, 8, 512), F32),
            pltpu.VMEM((4, 4, 256, 512), F32),
            pltpu.VMEM((4, 256, 512), BF16),
            pltpu.VMEM((2, 256, 512), BF16),
            pltpu.VMEM((4, 16, 16, 128), BF16),
            pltpu.VMEM((64, 16, 128), BF16),
            dma, dma((8,)),
            dma((8,)), dma((8,)),
            dma, dma((8,)),
            dma((8,)), dma((8,)),
            dma, dma,
            dma((2,)), dma((2,)),
            dma((2,)),
            dma((2,)), dma((2, 4, 4, 2)),
            dma, dma,
        ],
        compiler_params=pltpu.CompilerParams(
            collective_id=0, has_side_effects=True, vmem_limit_bytes=48 * 1024 * 1024
        ),
    )(
        *(
            pltpu.with_memory_space_constraint(operand, pltpu.HBM)
            for operand in (
                pair_map, res_mask, res_mask.reshape(4, 128), tri_proj, tri_gate, tri_out, att_qkvg,
                att_bias.T, att_out,
            )
        )
    )


def solution(mesh):
    in_specs = (P("row", "col", None), P(), P(), P(), P(), P(), P(), P())
    out_specs = P("row", "col", None)
    return jax.shard_map(local, mesh=mesh, in_specs=in_specs, out_specs=out_specs, check_vma=False)
```

```python
import math

import jax
import jax.numpy as jnp
from jax import lax
from jax.experimental import pallas as pl
from jax.experimental.pallas import tpu as pltpu
from jax.sharding import PartitionSpec as P

EPS = 1e-05
MESH = pl.DeviceIdType.MESH
F32 = jnp.float32
BF16 = jnp.bfloat16
NT = (((1,), (1,)), ((), ()))
FAR4 = (2, 3, 1, 0)
FAR8 = (4, 5, 7, 3, 6, 2, 1, 0)


def loop(low, high, body, unroll=None):
    def step(index, carry):
        body(index)
        return carry

    lax.fori_loop(low, high, step, 0, unroll=unroll)


def norm_over(values, axis):
    centre = values - jnp.mean(values, axis=axis, keepdims=True)
    spread = jnp.mean(centre * centre, axis=axis, keepdims=True)
    return centre * lax.rsqrt(spread + EPS)


def dot(a, b):
    return jnp.dot(a, b, preferred_element_type=F32)


def dot_nt(a, b):
    return lax.dot_general(a, b, NT, preferred_element_type=F32)


def flip(values):
    return values.astype(F32).T.astype(BF16)


def wait_bytes(ref, sem):
    pltpu.make_async_copy(ref, ref, sem).wait()


def kernel(
    pair_hbm, mask_hbm, mask_rows_hbm, proj_hbm, gate_hbm, tout_hbm, qkvg_hbm, abias_hbm, aout_hbm,
    out_ref,
    pair_ref, mask_smem, mask_ref, proj_ref, gate_ref, tout_ref, qkvg_ref, abias_ref, aout_ref, loads,
    pr_buf, xn, nk, wpt, ms, sb, pt, gt, gate_t, tout_t, qkvg_t,
    a_buf, lt, tr, s_buf, t_buf, tf, updt, n2t, bscr, mask_wide, bm, up,
    x_buf, bias, kt, ve, qe, gq, bf, sc, wb, mixed, gs, h_buf,
    send1, recv1, fsend, frecv, send2, recv2, gsend, grecv, psend, precv, xsend, xrecv,
    bsend, bz, bu, send4, recv4,
):
    r = lax.axis_index("row")
    c = lax.axis_index("col")
    q = c >> 1
    p = c & 1
    chip = r * 16 + q
    half = r >> 2
    y = r & 3
    x = c >> 3
    zh = q & 3
    sibling = (r, c ^ 1)

    fetches = [
        pltpu.make_async_copy(source, target, loads.at[at])
        for at, (source, target) in enumerate(
            [
                (pair_hbm, pair_ref), (mask_hbm, mask_smem), (mask_rows_hbm, mask_ref),
                (proj_hbm, proj_ref), (gate_hbm, gate_ref), (tout_hbm, tout_ref),
                (qkvg_hbm, qkvg_ref), (abias_hbm, abias_ref), (aout_hbm, aout_ref),
            ]
        )
    ]
    for fetch in fetches:
        fetch.start()

    barrier = pltpu.get_barrier_semaphore()

    def greet(row, col):
        pl.semaphore_signal(barrier, inc=1, device_id=(row, col), device_id_type=MESH)

    for dz in FAR8:
        for dy in FAR4:
            for dx in FAR4:
                if dz or dy or dx:
                    greet(r ^ ((dz & 1) << 2 | dy), c ^ (dx << 3 | (dz >> 1) << 1))
    for dq in range(16):
        greet(r, c ^ (2 * dq + 1))
    for dz in range(4):
        greet(r ^ 4, c ^ (2 * dz + 1))

    lane = lax.broadcasted_iota(jnp.int32, (1, 128), 1)
    low = lane < 64

    def half_lanes(a, b):
        return jnp.where(low, a, b)

    def swap(values):
        return pltpu.roll(values, 64, 1)

    for fetch in fetches:
        fetch.wait()

    flat = pair_ref[...].astype(F32).reshape(1024, 128)
    xn[...] = norm_over(flat, 1).astype(BF16).astype(F32)
    wpt[...] = flip(proj_ref[...])
    for k in range(16):
        part = xn[pl.ds(k, 64, stride=16), :].astype(BF16)
        nk[k] = jnp.concatenate([part, part], axis=0)

    mask_wide[0:4, :] = mask_ref[...]
    two = mask_wide[pl.ds(r >> 1, 1), :].astype(F32)
    odd = (r & 1) == 1
    turned = swap(jnp.broadcast_to(two, (8, 128)))[0:1]
    is_left = (lane >> 6) == jnp.where(odd, 0, 1)
    row_live = half_lanes(jnp.where(odd, turned, two), jnp.where(odd, two, turned))
    col_live = [mask_smem[c * 16 + k].astype(F32) for k in range(16)]


    def tiles(step):
        to_y = y ^ 2 ^ step ^ (step >> 1)
        first = pl.multiple_of(to_y * 16, 16)
        weights = jnp.concatenate(
            [wpt[pl.ds(64 * b + first, 16), :] for b in range(8)], axis=0
        )
        for k in range(16):
            z = dot_nt(weights, nk[k])
            g = jnp.where(is_left, z[0:32], z[64:96])
            v = jnp.where(is_left, z[32:64], z[96:128])
            ms[pl.ds(k, 32, stride=16), :] = jax.nn.sigmoid(g) * v * (row_live * col_live[k])
        for zl in range(2):
            sb[zl, to_y] = ms[256 * zl : 256 * zl + 256, :].astype(BF16).reshape(16, 16, 128)

    def project(step):
        to_y = y ^ 2 ^ step ^ (step >> 1)

        def send(dx, dz):
            to_zl = half ^ (dz & 1)
            flips = dx << 2 | dz >> 1
            return pltpu.make_async_remote_copy(
                src_ref=sb.at[to_zl, to_y, q ^ flips],
                dst_ref=a_buf.at[p, r, q],
                send_sem=send1,
                recv_sem=recv1.at[r],
                device_id=(to_zl * 4 + to_y, c ^ (flips << 1)),
                device_id_type=MESH,
            )

        for dx in FAR4:
            for dz in FAR8:
                if dx or dz:
                    send(dx, dz).start()

        @pl.when(step < 3)
        def _():
            send(0, 0).start()

        @pl.when(step == 3)
        def _():
            pltpu.make_async_copy(sb.at[half, y, q], a_buf.at[p, r, q], recv1.at[r]).start()

    tiles(0)
    pl.semaphore_wait(barrier, 147)
    project(0)

    def rest(step):
        tiles(step)
        project(step)

    loop(1, 4, rest)
    sent = [lambda: wait_bytes(sb.at[0], send1), lambda: wait_bytes(sb.at[0, pl.ds(0, 3)], send1)]
    sent.append(lambda: wait_bytes(sb.at[0, 0, pl.ds(0, 15)], send1))

    def pair_send(flips):
        to = c ^ flips
        pltpu.make_async_remote_copy(
            src_ref=pair_ref.at[pl.ds(2 * to, 2)],
            dst_ref=pr_buf.at[:, c],
            send_sem=psend,
            recv_sem=precv,
            device_id=(r, to),
            device_id_type=MESH,
        ).start()

    for dx in FAR4:
        for dz in FAR4:
            for core in range(2):
                if dx or dz or core:
                    pair_send(dx << 3 | dz << 1 | core)
    pltpu.make_async_copy(pair_ref.at[pl.ds(2 * c, 2)], pr_buf.at[:, c], precv).start()
    sent.append(lambda: wait_bytes(pr_buf.at[:, pl.ds(0, 31)], psend))

    gate_t[...] = flip(gate_ref[...])
    tout_t[...] = flip(tout_ref[...])
    qkvg_t[...] = flip(qkvg_ref[...])

    def forward_copy(row):
        return pltpu.make_async_remote_copy(
            src_ref=a_buf.at[p, row],
            dst_ref=a_buf.at[p, row],
            send_sem=fsend.at[row],
            recv_sem=frecv.at[row],
            device_id=sibling,
            device_id_type=MESH,
        )

    def turn(core, row):
        @pl.when((row >> 2) == p)
        def _():
            part = flip(a_buf[core, row].reshape(256, 128))
            at = pl.multiple_of((row & 3) * 64, 64)
            lt[core, pl.ds(at, 64), :] = jnp.where((row & 1) == 1, part[0:64], part[64:128])

    def arriving(step):
        pair = step >> 1
        return r ^ (2 ^ pair ^ (pair >> 1)) ^ ((step & 1) << 2)

    def forward(step):
        row = arriving(step)
        wait_bytes(a_buf.at[p, row], recv1.at[row])
        forward_copy(row).start()
        turn(p, row)

    loop(0, 8, forward)
    sent.append(lambda: loop(0, 8, lambda row: forward_copy(row).wait_send()))

    def turn_other(step):
        row = arriving(step)
        wait_bytes(a_buf.at[1 - p, row], frecv.at[row])
        turn(1 - p, row)

    loop(0, 8, turn_other, unroll=4)

    def triangle(step):
        pair = (y >> 1) ^ 1 ^ step
        rows = pl.ds(pl.multiple_of(128 * pair, 128), 128)
        for jc in range(4):
            sides = [
                jnp.concatenate(
                    [a_buf[core, 2 * jc + e].reshape(256, 128) for e in range(2)], axis=1
                )
                for core in range(2)
            ]
            prod = dot(lt[0, rows, :], sides[0]) + dot(lt[1, rows, :], sides[1])
            tr[pl.ds(jc, 128, stride=4), :] = half_lanes(prod[:, 0:128], prod[:, 128:256])
        for e in range(2):
            s_buf[2 * pair + e] = tr[256 * e : 256 * e + 256, :].astype(BF16).reshape(16, 16, 128)

        def send(to_y, flips):
            return pltpu.make_async_remote_copy(
                src_ref=s_buf.at[to_y, q ^ flips],
                dst_ref=t_buf.at[chip],
                send_sem=send2,
                recv_sem=recv2.at[r],
                device_id=(4 * p + to_y, c ^ (flips << 1)),
                device_id_type=MESH,
            )

        for own in range(2):
            to_y = y ^ (2 * (1 - step)) ^ (own ^ step)
            for dx in FAR4:
                for dz in FAR4:
                    if dx or dz:
                        send(to_y, dx << 2 | dz).start()
            here = jnp.logical_and(to_y == y, p == half)

            @pl.when(jnp.logical_not(here))
            def _():
                send(to_y, 0).start()

            @pl.when(here)
            def _():
                pltpu.make_async_copy(s_buf.at[to_y, q], t_buf.at[chip], recv2.at[r]).start()

    loop(0, 2, triangle, unroll=2)

    def triangle_sent():
        wait_bytes(s_buf.at[pl.ds(0, 3)], send2)
        wait_bytes(s_buf.at[0, pl.ds(0, 15)], send2)

        @pl.when(p != half)
        def _():
            wait_bytes(s_buf.at[0, 0], send2)

    sent.append(triangle_sent)

    wait_bytes(pr_buf, precv)

    def prepare(s):
        at = s & 3
        rows = pr_buf[s >> 2, pl.ds(8 * at, 8)].astype(F32).reshape(128, 128)
        pt[s] = rows.T
        gt[s] = jax.nn.sigmoid(dot_nt(gate_t[...], norm_over(rows, 1).astype(BF16)))

    loop(0, 8, prepare, unroll=2)

    def hand_copy(row):
        block = t_buf.at[pl.ds(pl.multiple_of(row * 16, 16), 16)]
        return pltpu.make_async_remote_copy(
            src_ref=block,
            dst_ref=block,
            send_sem=gsend.at[row],
            recv_sem=grecv.at[row],
            device_id=sibling,
            device_id_type=MESH,
        )

    def widen(row):
        block = t_buf[pl.ds(pl.multiple_of(row * 16, 16), 16)]
        tf[pl.ds(pl.multiple_of(row * 256, 256), 256), :] = block.astype(F32).reshape(256, 128)

    @pl.when(p == half)
    def _():
        def hand(step):
            row = arriving(step)
            wait_bytes(t_buf.at[pl.ds(pl.multiple_of(row * 16, 16), 16)], recv2.at[row])
            hand_copy(row).start()
            widen(row)

        loop(0, 8, hand, unroll=4)

    @pl.when(p != half)
    def _():
        def take(step):
            row = arriving(step)
            wait_bytes(t_buf.at[pl.ds(pl.multiple_of(row * 16, 16), 16)], grecv.at[row])
            widen(row)

        loop(0, 8, take, unroll=4)

    def handed():
        @pl.when(p == half)
        def _():
            loop(0, 8, lambda row: hand_copy(row).wait_send())

    sent.append(handed)

    def home(s):
        tri = tf[pl.ds(8 * p + s, 128, stride=16), :]
        tri_norm = norm_over(tri, 0).astype(BF16)
        updated = pt[s] + gt[s] * dot(tout_t[...], tri_norm)
        updt[s] = updated
        norm_two = norm_over(updated, 0)
        n2t[s] = norm_two
        heads = dot(abias_ref[...], norm_two.astype(BF16))[0:4]
        live = mask_wide[pl.ds(s & 3, 1), :] > 0
        bscr[s & 1, pl.ds(8 * ((s & 3) >> 1) + (s >> 2), 4, stride=2), :] = jnp.where(
            live, heads, -1000000000.0
        )

    loop(0, 8, home, unroll=8)

    bm[:, 0:128] = bscr[0, 0:16, :].astype(BF16)
    bm[:, 128:256] = bscr[1, 0:16, :].astype(BF16)

    def bias_copy(src, dst, sem, recv, row, col):
        return pltpu.make_async_remote_copy(
            src_ref=src, dst_ref=dst, send_sem=bsend.at[sem], recv_sem=recv,
            device_id=(row, col), device_id_type=MESH,
        )

    def along_z(dz):
        to = (c ^ ((dz >> 1) << 1)) & 30 | half
        return bias_copy(bm, bias.at[p, y, x, zh], 0, bz.at[zh >> 1], r ^ ((dz & 1) << 2), to)

    for dz in FAR8:
        if dz:
            along_z(dz).start()

    @pl.when(p == half)
    def _():
        pltpu.make_async_copy(bm, bias.at[p, y, x, zh], bz.at[zh >> 1]).start()

    @pl.when(p != half)
    def _():
        along_z(0).start()

    def bias_z_sent():
        wait_bytes(bias.at[0, 0, 0], bsend.at[0])
        wait_bytes(bias.at[0, 0, 0, pl.ds(0, 3)], bsend.at[0])

        @pl.when(p != half)
        def _():
            wait_bytes(bias.at[0, 0, 0, 0], bsend.at[0])

    sent.append(bias_z_sent)

    def rows_of(s):
        at = pl.ds(pl.multiple_of(128 * (s & 3), 128), 128)
        x_buf[2 * p + (s >> 2), at, :] = n2t[s].T.astype(BF16)
        up[2 * p + (s >> 2), at, :] = updt[s].T

    loop(0, 8, rows_of, unroll=4)

    def to_sibling(ref, at):
        return pltpu.make_async_remote_copy(
            src_ref=ref, dst_ref=ref, send_sem=xsend.at[at], recv_sem=xrecv.at[at],
            device_id=sibling, device_id_type=MESH,
        )

    swaps = [
        to_sibling(x_buf.at[pl.ds(2 * p, 2)], 0),
        to_sibling(up.at[pl.ds(2 * p, 2), pl.ds(pl.multiple_of(256 * (1 - p), 256), 256)], 1),
    ]
    for swapping in swaps:
        swapping.start()
        sent.append(swapping.wait_send)

    def unit_of(core, unit_y, unit_x, part):
        return bias.at[core, unit_y, unit_x, pl.ds(2 * part, 2)]

    def unit_copy(core, unit_y, unit_x, part, dy, dx):
        unit = unit_of(core, unit_y, unit_x, part)
        return bias_copy(
            unit, unit, 1, bu.at[core, unit_y, unit_x, part], r ^ dy, c ^ (dx << 3)
        )

    def unit_wait(core, unit_y, unit_x, part):
        wait_bytes(unit_of(core, unit_y, unit_x, part), bu.at[core, unit_y, unit_x, part])

    def straight(own):
        part = (zh >> 1) ^ own
        wait_bytes(bias.at[:, 0, 0, pl.ds(0, 2)], bz.at[part])
        for d in (2, 1, 3):
            for core in range(2):
                unit_copy(core, y, x, part, 0, d).start()
                unit_copy(core, y, x, part, d, 0).start()

    def onward(own):
        part = (zh >> 1) ^ own
        for near in (1, 3, 2):
            unit_wait(0, y, x ^ near, part)
            for dy in (2, 1, 3):
                unit_copy(0, y, x ^ near, part, dy, 0).start()
            unit_wait(1, y ^ near, x, part)
            for dx in (2, 1, 3):
                unit_copy(1, y ^ near, x, part, 0, dx).start()

    row_at = lax.broadcasted_iota(jnp.int32, (256, 64), 0)
    spread = ((row_at // 8) * 2 + row_at % 2 == lax.broadcasted_iota(jnp.int32, (256, 64), 1)).astype(
        F32
    ).astype(BF16)
    lane_at = lax.broadcasted_iota(jnp.int32, (64, 256), 1)
    gather = ((lane_at // 8) * 2 + lane_at % 2 == lax.broadcasted_iota(jnp.int32, (64, 256), 0)).astype(
        F32
    ).astype(BF16)
    own_head = (lax.broadcasted_iota(jnp.int32, (256, 128), 0) % 8) // 2 == (
        lax.broadcasted_iota(jnp.int32, (256, 128), 1) // 32
    )

    def project_row(i):
        rows = x_buf[i]
        kt[i] = dot_nt(qkvg_t[128:256, :], rows).astype(BF16)
        ve[i, :, 0:128] = dot(rows, qkvg_ref[:, 256:384]).astype(BF16)
        ve[i, :, 128:256] = jnp.ones((512, 128), BF16)
        mine = x_buf[i, pl.ds(pl.multiple_of(256 * p, 256), 256), :]
        queries = dot(mine, qkvg_ref[:, 0:128]).astype(BF16)
        gq[i] = jax.nn.sigmoid(dot(mine, qkvg_ref[:, 384:512]))
        for unit_y in range(4):
            wide = dot(spread, queries[64 * unit_y : 64 * unit_y + 64])
            qe[i, unit_y] = jnp.where(own_head, wide, 0.0).astype(BF16)

    log2e = 1.0 / math.log(2.0)
    scale = log2e / math.sqrt(32.0)

    def scores_of(i):
        for unit_y in range(4):
            sc[unit_y, i] = dot(qe[i, unit_y], kt[i]) * scale

    straight(0)
    project_row(2 * p)
    straight(1)
    project_row(2 * p + 1)
    onward(0)
    scores_of(2 * p)
    onward(1)
    scores_of(2 * p + 1)

    def bias_sent():
        wait_bytes(bias.at[0], bsend.at[1])
        wait_bytes(bias.at[1, pl.ds(0, 3)], bsend.at[1])
        wait_bytes(bias.at[1, 0, pl.ds(0, 2)], bsend.at[1])

    sent.append(bias_sent)

    for swapping in swaps:
        swapping.wait_recv()
    for own in range(2):
        project_row(2 - 2 * p + own)
        scores_of(2 - 2 * p + own)

    def soften(unit_y, i):
        for unit_x in range(4):
            rows = slice(64 * unit_x, 64 * unit_x + 64)
            if i == 0:
                for core in range(2):
                    tiles = bias[core, unit_y, unit_x].astype(F32) * log2e
                    bf[4 * unit_x : 4 * unit_x + 4, core, :, 0:256] = tiles[:, 0:8]
                    bf[4 * unit_x : 4 * unit_x + 4, core, :, 256:512] = tiles[:, 8:16]
            part = sc[unit_y, i, rows, :] + bf[4 * unit_x : 4 * unit_x + 4].reshape(64, 512)
            exps = jnp.exp2(part - jnp.max(part, axis=1, keepdims=True))
            wb[i, rows, :] = exps.astype(BF16)

    def mix(i):
        out = dot(wb[i], ve[i])
        out = jnp.where(own_head, out[:, 0:128] * (1.0 / out[:, 128:256]), 0.0)
        high = out.astype(BF16)
        mixed[0, :, 128 * i : 128 * i + 128] = high
        mixed[1, :, 128 * i : 128 * i + 128] = (out - high.astype(F32)).astype(BF16)

    def block(step):
        unit_y = y ^ step ^ (step >> 1)
        own_y = isinstance(step, int)
        for near in (0, 1, 3, 2):
            for part in range(2):
                if not own_y:
                    unit_wait(0, unit_y, x ^ near, part)
                if near:
                    unit_wait(1, unit_y, x ^ near, part)
        for i in range(4):
            soften(unit_y, i)
            if i > 0:
                mix(i - 1)
        mix(3)
        attended = dot(gather, mixed[0]) + dot(gather, mixed[1])
        at = pl.multiple_of(64 * unit_y, 64)
        gated = jnp.concatenate(
            [gq[i, pl.ds(at, 64), :] * attended[:, 128 * i : 128 * i + 128] for i in range(4)], axis=0
        )
        update = dot(gated.astype(BF16), aout_ref[...])
        for i in range(4):
            result = up[i, pl.ds(pl.multiple_of(256 * p + at, 64), 64), :]
            result = result + update[64 * i : 64 * i + 64]
            gs[i, pl.ds(4 * unit_y, 4)] = result.astype(BF16).reshape(4, 16, 128)

        for off in range(4):
            cl = 4 * unit_y + off
            send_gated(cl)

    def send_gated(cl):
        to = 16 * p + cl

        @pl.when(to == c)
        def _():
            pltpu.make_async_copy(gs.at[:, cl], h_buf.at[pl.ds(4 * q, 4)], recv4).start()

        @pl.when(to != c)
        def _():
            pltpu.make_async_remote_copy(
                src_ref=gs.at[:, cl],
                dst_ref=h_buf.at[pl.ds(4 * q, 4)],
                send_sem=send4,
                recv_sem=recv4,
                device_id=(r, to),
                device_id_type=MESH,
            ).start()

    block(0)
    loop(1, 4, block)

    def gated_sent():
        wait_bytes(gs.at[:, pl.ds(0, 15)], send4)

        @pl.when((c >> 4) != p)
        def _():
            wait_bytes(gs.at[:, 0], send4)

    sent.append(gated_sent)

    for wait in sent:
        wait()

    wait_bytes(h_buf, recv4)
    out_ref[...] = h_buf[...]


def local(pair_map, res_mask, tri_proj, tri_gate, tri_out, att_qkvg, att_bias, att_out):
    dma = pltpu.SemaphoreType.DMA
    return pl.pallas_call(
        kernel,
        out_shape=jax.ShapeDtypeStruct((64, 16, 128), BF16),
        in_specs=[pl.BlockSpec(memory_space=pltpu.HBM)] * 9,
        out_specs=pl.BlockSpec(memory_space=pltpu.VMEM),
        scratch_shapes=[
            pltpu.VMEM((64, 16, 128), BF16),
            pltpu.SMEM((512,), jnp.int32),
            pltpu.VMEM((4, 128), jnp.int32),
            pltpu.VMEM((128, 512), BF16),
            pltpu.VMEM((128, 128), BF16),
            pltpu.VMEM((128, 128), BF16),
            pltpu.VMEM((128, 512), BF16),
            pltpu.VMEM((4, 128), BF16),
            pltpu.VMEM((128, 128), BF16),
            dma((9,)),
            pltpu.VMEM((2, 32, 16, 128), BF16),
            pltpu.VMEM((1024, 128), F32),
            pltpu.VMEM((16, 128, 128), BF16),
            pltpu.VMEM((512, 128), BF16),
            pltpu.VMEM((512, 128), F32),
            pltpu.VMEM((2, 4, 16, 16, 128), BF16),
            pltpu.VMEM((8, 128, 128), F32),
            pltpu.VMEM((8, 128, 128), F32),
            pltpu.VMEM((128, 128), BF16),
            pltpu.VMEM((128, 128), BF16),
            pltpu.VMEM((512, 128), BF16),
            pltpu.VMEM((2, 8, 16, 16, 128), BF16),
            pltpu.VMEM((2, 256, 256), BF16),
            pltpu.VMEM((512, 128), F32),
            pltpu.VMEM((4, 16, 16, 128), BF16),
            pltpu.VMEM((128, 16, 128), BF16),
            pltpu.VMEM((2048, 128), F32),
            pltpu.VMEM((8, 128, 128), F32),
            pltpu.VMEM((8, 128, 128), F32),
            pltpu.VMEM((2, 24, 128), F32),
            pltpu.VMEM((16, 128), jnp.int32),
            pltpu.VMEM((16, 256), BF16),
            pltpu.VMEM((4, 512, 128), F32),
            pltpu.VMEM((4, 512, 128), BF16),
            pltpu.VMEM((2, 4, 4, 4, 16, 256), BF16),
            pltpu.VMEM((4, 128, 512), BF16),
            pltpu.VMEM((4, 512, 256), BF16),
            pltpu.VMEM((4, 4, 256, 128), BF16),
            pltpu.VMEM((4, 256, 128), F32),
            pltpu.VMEM((16, 2, 8, 512), F32),
            pltpu.VMEM((4, 4, 256, 512), F32),
            pltpu.VMEM((4, 256, 512), BF16),
            pltpu.VMEM((2, 256, 512), BF16),
            pltpu.VMEM((4, 16, 16, 128), BF16),
            pltpu.VMEM((64, 16, 128), BF16),
            dma, dma((8,)),
            dma((8,)), dma((8,)),
            dma, dma((8,)),
            dma((8,)), dma((8,)),
            dma, dma,
            dma((2,)), dma((2,)),
            dma((2,)),
            dma((2,)), dma((2, 4, 4, 2)),
            dma, dma,
        ],
        compiler_params=pltpu.CompilerParams(
            collective_id=0, has_side_effects=True, vmem_limit_bytes=48 * 1024 * 1024
        ),
    )(
        *(
            pltpu.with_memory_space_constraint(operand, pltpu.HBM)
            for operand in (
                pair_map, res_mask, res_mask.reshape(4, 128), tri_proj, tri_gate, tri_out, att_qkvg,
                att_bias.T, att_out,
            )
        )
    )


def solution(mesh):
    in_specs = (P("row", "col", None), P(), P(), P(), P(), P(), P(), P())
    out_specs = P("row", "col", None)
    return jax.shard_map(local, mesh=mesh, in_specs=in_specs, out_specs=out_specs, check_vma=False)
```

```python
import math

import jax
import jax.numpy as jnp
from jax import lax
from jax.experimental import pallas as pl
from jax.experimental.pallas import tpu as pltpu
from jax.sharding import PartitionSpec as P

EPS = 1e-05
MESH = pl.DeviceIdType.MESH
F32 = jnp.float32
BF16 = jnp.bfloat16
NT = (((1,), (1,)), ((), ()))
FAR4 = (2, 3, 1, 0)
FAR8 = (4, 5, 7, 3, 6, 2, 1, 0)


def loop(low, high, body, unroll=None):
    def step(index, carry):
        body(index)
        return carry

    lax.fori_loop(low, high, step, 0, unroll=unroll)


def norm_over(values, axis):
    centre = values - jnp.mean(values, axis=axis, keepdims=True)
    spread = jnp.mean(centre * centre, axis=axis, keepdims=True)
    return centre * lax.rsqrt(spread + EPS)


def dot(a, b):
    return jnp.dot(a, b, preferred_element_type=F32)


def dot_nt(a, b):
    return lax.dot_general(a, b, NT, preferred_element_type=F32)


def flip(values):
    return values.astype(F32).T.astype(BF16)


def wait_bytes(ref, sem):
    pltpu.make_async_copy(ref, ref, sem).wait()


def kernel(
    pair_hbm, mask_hbm, mask_rows_hbm, proj_hbm, gate_hbm, tout_hbm, qkvg_hbm, abias_hbm, aout_hbm,
    out_ref,
    pair_ref, mask_smem, mask_ref, proj_ref, gate_ref, tout_ref, qkvg_ref, abias_ref, aout_ref, loads,
    pr_buf, xn, nk, wpt, ms, sb, pt, gt, gate_t, tout_t, qkvg_t,
    a_buf, lt, tr, s_buf, t_buf, tf, updt, n2t, bscr, mask_wide, bm, up,
    x_buf, bias, kt, ve, qe, gq, bf, sc, wb, mixed, gs, h_buf,
    send1, recv1, fsend, frecv, send2, recv2, gsend, grecv, psend, precv, xsend, xrecv,
    bsend, bz, bu, send4, recv4,
):
    r = lax.axis_index("row")
    c = lax.axis_index("col")
    q = c >> 1
    p = c & 1
    chip = r * 16 + q
    half = r >> 2
    y = r & 3
    x = c >> 3
    zh = q & 3
    sibling = (r, c ^ 1)

    fetches = [
        pltpu.make_async_copy(source, target, loads.at[at])
        for at, (source, target) in enumerate(
            [
                (pair_hbm, pair_ref), (mask_hbm, mask_smem), (mask_rows_hbm, mask_ref),
                (proj_hbm, proj_ref), (gate_hbm, gate_ref), (tout_hbm, tout_ref),
                (qkvg_hbm, qkvg_ref), (abias_hbm, abias_ref), (aout_hbm, aout_ref),
            ]
        )
    ]
    for fetch in fetches[:4]:
        fetch.start()

    barrier = pltpu.get_barrier_semaphore()

    def greet(row, col):
        pl.semaphore_signal(barrier, inc=1, device_id=(row, col), device_id_type=MESH)

    for dz in FAR8:
        for dy in FAR4:
            for dx in FAR4:
                if dz or dy or dx:
                    greet(r ^ ((dz & 1) << 2 | dy), c ^ (dx << 3 | (dz >> 1) << 1))
    for dq in range(16):
        greet(r, c ^ (2 * dq + 1))
    for dz in range(4):
        greet(r ^ 4, c ^ (2 * dz + 1))

    for fetch in fetches[4:]:
        fetch.start()

    lane = lax.broadcasted_iota(jnp.int32, (1, 128), 1)
    low = lane < 64

    def half_lanes(a, b):
        return jnp.where(low, a, b)

    def swap(values):
        return pltpu.roll(values, 64, 1)

    for fetch in fetches[:4]:
        fetch.wait()

    flat = pair_ref[...].astype(F32).reshape(1024, 128)
    xn[...] = norm_over(flat, 1).astype(BF16).astype(F32)
    wpt[...] = flip(proj_ref[...])
    for k in range(16):
        part = xn[pl.ds(k, 64, stride=16), :].astype(BF16)
        nk[k] = jnp.concatenate([part, part], axis=0)

    mask_wide[0:4, :] = mask_ref[...]
    two = mask_wide[pl.ds(r >> 1, 1), :].astype(F32)
    odd = (r & 1) == 1
    turned = swap(jnp.broadcast_to(two, (8, 128)))[0:1]
    is_left = (lane >> 6) == jnp.where(odd, 0, 1)
    row_live = half_lanes(jnp.where(odd, turned, two), jnp.where(odd, two, turned))
    col_live = [mask_smem[c * 16 + k].astype(F32) for k in range(16)]


    def tiles(step):
        to_y = y ^ 2 ^ step ^ (step >> 1)
        first = pl.multiple_of(to_y * 16, 16)
        weights = jnp.concatenate(
            [wpt[pl.ds(64 * b + first, 16), :] for b in range(8)], axis=0
        )
        for k in range(16):
            z = dot_nt(weights, nk[k])
            g = jnp.where(is_left, z[0:32], z[64:96])
            v = jnp.where(is_left, z[32:64], z[96:128])
            ms[pl.ds(k, 32, stride=16), :] = jax.nn.sigmoid(g) * v * (row_live * col_live[k])
        for zl in range(2):
            sb[zl, to_y] = ms[256 * zl : 256 * zl + 256, :].astype(BF16).reshape(16, 16, 128)

    def project(step):
        to_y = y ^ 2 ^ step ^ (step >> 1)

        def send(dx, dz):
            to_zl = half ^ (dz & 1)
            flips = dx << 2 | dz >> 1
            return pltpu.make_async_remote_copy(
                src_ref=sb.at[to_zl, to_y, q ^ flips],
                dst_ref=a_buf.at[p, r, q],
                send_sem=send1,
                recv_sem=recv1.at[r],
                device_id=(to_zl * 4 + to_y, c ^ (flips << 1)),
                device_id_type=MESH,
            )

        for dx in FAR4:
            for dz in FAR8:
                if dx or dz:
                    send(dx, dz).start()

        @pl.when(step < 3)
        def _():
            send(0, 0).start()

        @pl.when(step == 3)
        def _():
            pltpu.make_async_copy(sb.at[half, y, q], a_buf.at[p, r, q], recv1.at[r]).start()

    tiles(0)
    pl.semaphore_wait(barrier, 147)
    project(0)

    def rest(step):
        tiles(step)
        project(step)

    loop(1, 4, rest)
    sent = [lambda: wait_bytes(sb.at[0], send1), lambda: wait_bytes(sb.at[0, pl.ds(0, 3)], send1)]
    sent.append(lambda: wait_bytes(sb.at[0, 0, pl.ds(0, 15)], send1))

    def pair_send(flips):
        to = c ^ flips
        pltpu.make_async_remote_copy(
            src_ref=pair_ref.at[pl.ds(2 * to, 2)],
            dst_ref=pr_buf.at[:, c],
            send_sem=psend,
            recv_sem=precv,
            device_id=(r, to),
            device_id_type=MESH,
        ).start()

    for dx in FAR4:
        for dz in FAR4:
            for core in range(2):
                if dx or dz or core:
                    pair_send(dx << 3 | dz << 1 | core)
    pltpu.make_async_copy(pair_ref.at[pl.ds(2 * c, 2)], pr_buf.at[:, c], precv).start()
    sent.append(lambda: wait_bytes(pr_buf.at[:, pl.ds(0, 31)], psend))

    for fetch in fetches[4:]:
        fetch.wait()
    gate_t[...] = flip(gate_ref[...])
    tout_t[...] = flip(tout_ref[...])
    qkvg_t[...] = flip(qkvg_ref[...])

    def forward_copy(row):
        return pltpu.make_async_remote_copy(
            src_ref=a_buf.at[p, row],
            dst_ref=a_buf.at[p, row],
            send_sem=fsend.at[row],
            recv_sem=frecv.at[row],
            device_id=sibling,
            device_id_type=MESH,
        )

    def turn(core, row):
        @pl.when((row >> 2) == p)
        def _():
            part = flip(a_buf[core, row].reshape(256, 128))
            at = pl.multiple_of((row & 3) * 64, 64)
            lt[core, pl.ds(at, 64), :] = jnp.where((row & 1) == 1, part[0:64], part[64:128])

    def arriving(step):
        pair = step >> 1
        return r ^ (2 ^ pair ^ (pair >> 1)) ^ ((step & 1) << 2)

    def forward(step):
        row = arriving(step)
        wait_bytes(a_buf.at[p, row], recv1.at[row])
        forward_copy(row).start()
        turn(p, row)

    loop(0, 8, forward)
    sent.append(lambda: loop(0, 8, lambda row: forward_copy(row).wait_send()))

    def turn_other(step):
        row = arriving(step)
        wait_bytes(a_buf.at[1 - p, row], frecv.at[row])
        turn(1 - p, row)

    loop(0, 8, turn_other, unroll=4)

    def triangle(step):
        pair = (y >> 1) ^ 1 ^ step
        rows = pl.ds(pl.multiple_of(128 * pair, 128), 128)
        for jc in range(4):
            sides = [
                jnp.concatenate(
                    [a_buf[core, 2 * jc + e].reshape(256, 128) for e in range(2)], axis=1
                )
                for core in range(2)
            ]
            prod = dot(lt[0, rows, :], sides[0]) + dot(lt[1, rows, :], sides[1])
            tr[pl.ds(jc, 128, stride=4), :] = half_lanes(prod[:, 0:128], prod[:, 128:256])
        for e in range(2):
            s_buf[2 * pair + e] = tr[256 * e : 256 * e + 256, :].astype(BF16).reshape(16, 16, 128)

        def send(to_y, flips):
            return pltpu.make_async_remote_copy(
                src_ref=s_buf.at[to_y, q ^ flips],
                dst_ref=t_buf.at[chip],
                send_sem=send2,
                recv_sem=recv2.at[r],
                device_id=(4 * p + to_y, c ^ (flips << 1)),
                device_id_type=MESH,
            )

        for own in range(2):
            to_y = y ^ (2 * (1 - step)) ^ (own ^ step)
            for dx in FAR4:
                for dz in FAR4:
                    if dx or dz:
                        send(to_y, dx << 2 | dz).start()
            here = jnp.logical_and(to_y == y, p == half)

            @pl.when(jnp.logical_not(here))
            def _():
                send(to_y, 0).start()

            @pl.when(here)
            def _():
                pltpu.make_async_copy(s_buf.at[to_y, q], t_buf.at[chip], recv2.at[r]).start()

    loop(0, 2, triangle, unroll=2)

    def triangle_sent():
        wait_bytes(s_buf.at[pl.ds(0, 3)], send2)
        wait_bytes(s_buf.at[0, pl.ds(0, 15)], send2)

        @pl.when(p != half)
        def _():
            wait_bytes(s_buf.at[0, 0], send2)

    sent.append(triangle_sent)

    wait_bytes(pr_buf, precv)

    def prepare(s):
        at = s & 3
        rows = pr_buf[s >> 2, pl.ds(8 * at, 8)].astype(F32).reshape(128, 128)
        pt[s] = rows.T
        gt[s] = jax.nn.sigmoid(dot_nt(gate_t[...], norm_over(rows, 1).astype(BF16)))

    loop(0, 8, prepare, unroll=2)

    def hand_copy(row):
        block = t_buf.at[pl.ds(pl.multiple_of(row * 16, 16), 16)]
        return pltpu.make_async_remote_copy(
            src_ref=block,
            dst_ref=block,
            send_sem=gsend.at[row],
            recv_sem=grecv.at[row],
            device_id=sibling,
            device_id_type=MESH,
        )

    def widen(row):
        block = t_buf[pl.ds(pl.multiple_of(row * 16, 16), 16)]
        tf[pl.ds(pl.multiple_of(row * 256, 256), 256), :] = block.astype(F32).reshape(256, 128)

    @pl.when(p == half)
    def _():
        def hand(step):
            row = arriving(step)
            wait_bytes(t_buf.at[pl.ds(pl.multiple_of(row * 16, 16), 16)], recv2.at[row])
            hand_copy(row).start()
            widen(row)

        loop(0, 8, hand, unroll=4)

    @pl.when(p != half)
    def _():
        def take(step):
            row = arriving(step)
            wait_bytes(t_buf.at[pl.ds(pl.multiple_of(row * 16, 16), 16)], grecv.at[row])
            widen(row)

        loop(0, 8, take, unroll=4)

    def handed():
        @pl.when(p == half)
        def _():
            loop(0, 8, lambda row: hand_copy(row).wait_send())

    sent.append(handed)

    def home(s):
        tri = tf[pl.ds(8 * p + s, 128, stride=16), :]
        tri_norm = norm_over(tri, 0).astype(BF16)
        updated = pt[s] + gt[s] * dot(tout_t[...], tri_norm)
        updt[s] = updated
        norm_two = norm_over(updated, 0)
        n2t[s] = norm_two
        heads = dot(abias_ref[...], norm_two.astype(BF16))[0:4]
        live = mask_wide[pl.ds(s & 3, 1), :] > 0
        bscr[s & 1, pl.ds(8 * ((s & 3) >> 1) + (s >> 2), 4, stride=2), :] = jnp.where(
            live, heads, -1000000000.0
        )

    loop(0, 8, home, unroll=8)

    bm[:, 0:128] = bscr[0, 0:16, :].astype(BF16)
    bm[:, 128:256] = bscr[1, 0:16, :].astype(BF16)

    def bias_copy(src, dst, sem, recv, row, col):
        return pltpu.make_async_remote_copy(
            src_ref=src, dst_ref=dst, send_sem=bsend.at[sem], recv_sem=recv,
            device_id=(row, col), device_id_type=MESH,
        )

    def along_z(dz):
        to = (c ^ ((dz >> 1) << 1)) & 30 | half
        return bias_copy(bm, bias.at[p, y, x, zh], 0, bz.at[zh >> 1], r ^ ((dz & 1) << 2), to)

    for dz in FAR8:
        if dz:
            along_z(dz).start()

    @pl.when(p == half)
    def _():
        pltpu.make_async_copy(bm, bias.at[p, y, x, zh], bz.at[zh >> 1]).start()

    @pl.when(p != half)
    def _():
        along_z(0).start()

    def bias_z_sent():
        wait_bytes(bias.at[0, 0, 0], bsend.at[0])
        wait_bytes(bias.at[0, 0, 0, pl.ds(0, 3)], bsend.at[0])

        @pl.when(p != half)
        def _():
            wait_bytes(bias.at[0, 0, 0, 0], bsend.at[0])

    sent.append(bias_z_sent)

    def rows_of(s):
        at = pl.ds(pl.multiple_of(128 * (s & 3), 128), 128)
        x_buf[2 * p + (s >> 2), at, :] = n2t[s].T.astype(BF16)
        up[2 * p + (s >> 2), at, :] = updt[s].T

    loop(0, 8, rows_of, unroll=4)

    def to_sibling(ref, at):
        return pltpu.make_async_remote_copy(
            src_ref=ref, dst_ref=ref, send_sem=xsend.at[at], recv_sem=xrecv.at[at],
            device_id=sibling, device_id_type=MESH,
        )

    swaps = [
        to_sibling(x_buf.at[pl.ds(2 * p, 2)], 0),
        to_sibling(up.at[pl.ds(2 * p, 2), pl.ds(pl.multiple_of(256 * (1 - p), 256), 256)], 1),
    ]
    for swapping in swaps:
        swapping.start()
        sent.append(swapping.wait_send)

    def unit_of(core, unit_y, unit_x, part):
        return bias.at[core, unit_y, unit_x, pl.ds(2 * part, 2)]

    def unit_copy(core, unit_y, unit_x, part, dy, dx):
        unit = unit_of(core, unit_y, unit_x, part)
        return bias_copy(
            unit, unit, 1, bu.at[core, unit_y, unit_x, part], r ^ dy, c ^ (dx << 3)
        )

    def unit_wait(core, unit_y, unit_x, part):
        wait_bytes(unit_of(core, unit_y, unit_x, part), bu.at[core, unit_y, unit_x, part])

    def straight(own):
        part = (zh >> 1) ^ own
        wait_bytes(bias.at[:, 0, 0, pl.ds(0, 2)], bz.at[part])
        for d in (2, 1, 3):
            for core in range(2):
                unit_copy(core, y, x, part, 0, d).start()
                unit_copy(core, y, x, part, d, 0).start()

    def onward(own):
        part = (zh >> 1) ^ own
        for near in (1, 3, 2):
            unit_wait(0, y, x ^ near, part)
            for dy in (2, 1, 3):
                unit_copy(0, y, x ^ near, part, dy, 0).start()
            unit_wait(1, y ^ near, x, part)
            for dx in (2, 1, 3):
                unit_copy(1, y ^ near, x, part, 0, dx).start()

    row_at = lax.broadcasted_iota(jnp.int32, (256, 64), 0)
    spread = ((row_at // 8) * 2 + row_at % 2 == lax.broadcasted_iota(jnp.int32, (256, 64), 1)).astype(
        F32
    ).astype(BF16)
    lane_at = lax.broadcasted_iota(jnp.int32, (64, 256), 1)
    gather = ((lane_at // 8) * 2 + lane_at % 2 == lax.broadcasted_iota(jnp.int32, (64, 256), 0)).astype(
        F32
    ).astype(BF16)
    own_head = (lax.broadcasted_iota(jnp.int32, (256, 128), 0) % 8) // 2 == (
        lax.broadcasted_iota(jnp.int32, (256, 128), 1) // 32
    )

    def project_row(i):
        rows = x_buf[i]
        kt[i] = dot_nt(qkvg_t[128:256, :], rows).astype(BF16)
        ve[i, :, 0:128] = dot(rows, qkvg_ref[:, 256:384]).astype(BF16)
        ve[i, :, 128:256] = jnp.ones((512, 128), BF16)
        mine = x_buf[i, pl.ds(pl.multiple_of(256 * p, 256), 256), :]
        queries = dot(mine, qkvg_ref[:, 0:128]).astype(BF16)
        gq[i] = jax.nn.sigmoid(dot(mine, qkvg_ref[:, 384:512]))
        for unit_y in range(4):
            wide = dot(spread, queries[64 * unit_y : 64 * unit_y + 64])
            qe[i, unit_y] = jnp.where(own_head, wide, 0.0).astype(BF16)

    log2e = 1.0 / math.log(2.0)
    scale = log2e / math.sqrt(32.0)

    def scores_of(i):
        for unit_y in range(4):
            sc[unit_y, i] = dot(qe[i, unit_y], kt[i]) * scale

    straight(0)
    project_row(2 * p)
    straight(1)
    project_row(2 * p + 1)
    onward(0)
    scores_of(2 * p)
    onward(1)
    scores_of(2 * p + 1)

    def bias_sent():
        wait_bytes(bias.at[0], bsend.at[1])
        wait_bytes(bias.at[1, pl.ds(0, 3)], bsend.at[1])
        wait_bytes(bias.at[1, 0, pl.ds(0, 2)], bsend.at[1])

    sent.append(bias_sent)

    for swapping in swaps:
        swapping.wait_recv()
    for own in range(2):
        project_row(2 - 2 * p + own)
        scores_of(2 - 2 * p + own)

    def soften(unit_y, i):
        for unit_x in range(4):
            rows = slice(64 * unit_x, 64 * unit_x + 64)
            if i == 0:
                for core in range(2):
                    tiles = bias[core, unit_y, unit_x].astype(F32) * log2e
                    bf[4 * unit_x : 4 * unit_x + 4, core, :, 0:256] = tiles[:, 0:8]
                    bf[4 * unit_x : 4 * unit_x + 4, core, :, 256:512] = tiles[:, 8:16]
            part = sc[unit_y, i, rows, :] + bf[4 * unit_x : 4 * unit_x + 4].reshape(64, 512)
            exps = jnp.exp2(part - jnp.max(part, axis=1, keepdims=True))
            wb[i, rows, :] = exps.astype(BF16)

    def mix(i):
        out = dot(wb[i], ve[i])
        out = jnp.where(own_head, out[:, 0:128] * (1.0 / out[:, 128:256]), 0.0)
        high = out.astype(BF16)
        mixed[0, :, 128 * i : 128 * i + 128] = high
        mixed[1, :, 128 * i : 128 * i + 128] = (out - high.astype(F32)).astype(BF16)

    def block(step):
        unit_y = y ^ step ^ (step >> 1)
        own_y = isinstance(step, int)
        for near in (0, 1, 3, 2):
            for part in range(2):
                if not own_y:
                    unit_wait(0, unit_y, x ^ near, part)
                if near:
                    unit_wait(1, unit_y, x ^ near, part)
        for i in range(4):
            soften(unit_y, i)
            if i > 0:
                mix(i - 1)
        mix(3)
        attended = dot(gather, mixed[0]) + dot(gather, mixed[1])
        at = pl.multiple_of(64 * unit_y, 64)
        gated = jnp.concatenate(
            [gq[i, pl.ds(at, 64), :] * attended[:, 128 * i : 128 * i + 128] for i in range(4)], axis=0
        )
        update = dot(gated.astype(BF16), aout_ref[...])
        for i in range(4):
            result = up[i, pl.ds(pl.multiple_of(256 * p + at, 64), 64), :]
            result = result + update[64 * i : 64 * i + 64]
            gs[i, pl.ds(4 * unit_y, 4)] = result.astype(BF16).reshape(4, 16, 128)

        for off in range(4):
            cl = 4 * unit_y + off
            send_gated(cl)

    def send_gated(cl):
        to = 16 * p + cl

        @pl.when(to == c)
        def _():
            pltpu.make_async_copy(gs.at[:, cl], h_buf.at[pl.ds(4 * q, 4)], recv4).start()

        @pl.when(to != c)
        def _():
            pltpu.make_async_remote_copy(
                src_ref=gs.at[:, cl],
                dst_ref=h_buf.at[pl.ds(4 * q, 4)],
                send_sem=send4,
                recv_sem=recv4,
                device_id=(r, to),
                device_id_type=MESH,
            ).start()

    block(0)
    loop(1, 4, block)

    def gated_sent():
        wait_bytes(gs.at[:, pl.ds(0, 15)], send4)

        @pl.when((c >> 4) != p)
        def _():
            wait_bytes(gs.at[:, 0], send4)

    sent.append(gated_sent)

    for wait in sent:
        wait()

    wait_bytes(h_buf, recv4)
    out_ref[...] = h_buf[...]


def local(pair_map, res_mask, tri_proj, tri_gate, tri_out, att_qkvg, att_bias, att_out):
    dma = pltpu.SemaphoreType.DMA
    return pl.pallas_call(
        kernel,
        out_shape=jax.ShapeDtypeStruct((64, 16, 128), BF16),
        in_specs=[pl.BlockSpec(memory_space=pltpu.HBM)] * 9,
        out_specs=pl.BlockSpec(memory_space=pltpu.VMEM),
        scratch_shapes=[
            pltpu.VMEM((64, 16, 128), BF16),
            pltpu.SMEM((512,), jnp.int32),
            pltpu.VMEM((4, 128), jnp.int32),
            pltpu.VMEM((128, 512), BF16),
            pltpu.VMEM((128, 128), BF16),
            pltpu.VMEM((128, 128), BF16),
            pltpu.VMEM((128, 512), BF16),
            pltpu.VMEM((4, 128), BF16),
            pltpu.VMEM((128, 128), BF16),
            dma((9,)),
            pltpu.VMEM((2, 32, 16, 128), BF16),
            pltpu.VMEM((1024, 128), F32),
            pltpu.VMEM((16, 128, 128), BF16),
            pltpu.VMEM((512, 128), BF16),
            pltpu.VMEM((512, 128), F32),
            pltpu.VMEM((2, 4, 16, 16, 128), BF16),
            pltpu.VMEM((8, 128, 128), F32),
            pltpu.VMEM((8, 128, 128), F32),
            pltpu.VMEM((128, 128), BF16),
            pltpu.VMEM((128, 128), BF16),
            pltpu.VMEM((512, 128), BF16),
            pltpu.VMEM((2, 8, 16, 16, 128), BF16),
            pltpu.VMEM((2, 256, 256), BF16),
            pltpu.VMEM((512, 128), F32),
            pltpu.VMEM((4, 16, 16, 128), BF16),
            pltpu.VMEM((128, 16, 128), BF16),
            pltpu.VMEM((2048, 128), F32),
            pltpu.VMEM((8, 128, 128), F32),
            pltpu.VMEM((8, 128, 128), F32),
            pltpu.VMEM((2, 24, 128), F32),
            pltpu.VMEM((16, 128), jnp.int32),
            pltpu.VMEM((16, 256), BF16),
            pltpu.VMEM((4, 512, 128), F32),
            pltpu.VMEM((4, 512, 128), BF16),
            pltpu.VMEM((2, 4, 4, 4, 16, 256), BF16),
            pltpu.VMEM((4, 128, 512), BF16),
            pltpu.VMEM((4, 512, 256), BF16),
            pltpu.VMEM((4, 4, 256, 128), BF16),
            pltpu.VMEM((4, 256, 128), F32),
            pltpu.VMEM((16, 2, 8, 512), F32),
            pltpu.VMEM((4, 4, 256, 512), F32),
            pltpu.VMEM((4, 256, 512), BF16),
            pltpu.VMEM((2, 256, 512), BF16),
            pltpu.VMEM((4, 16, 16, 128), BF16),
            pltpu.VMEM((64, 16, 128), BF16),
            dma, dma((8,)),
            dma((8,)), dma((8,)),
            dma, dma((8,)),
            dma((8,)), dma((8,)),
            dma, dma,
            dma((2,)), dma((2,)),
            dma((2,)),
            dma((2,)), dma((2, 4, 4, 2)),
            dma, dma,
        ],
        compiler_params=pltpu.CompilerParams(
            collective_id=0, has_side_effects=True, vmem_limit_bytes=48 * 1024 * 1024
        ),
    )(
        *(
            pltpu.with_memory_space_constraint(operand, pltpu.HBM)
            for operand in (
                pair_map, res_mask, res_mask.reshape(4, 128), tri_proj, tri_gate, tri_out, att_qkvg,
                att_bias.T, att_out,
            )
        )
    )


def solution(mesh):
    in_specs = (P("row", "col", None), P(), P(), P(), P(), P(), P(), P())
    out_specs = P("row", "col", None)
    return jax.shard_map(local, mesh=mesh, in_specs=in_specs, out_specs=out_specs, check_vma=False)
```
